128 devices in a mesh: node: 8 (over y, core), local: 4 (over z), cuts: 4 (over x).
Axes of the slice: x: 4, y: 4, z: 4, core: 2. Of those that a mesh axis runs over, the one named last changes fastest.
Arguments:
- tokens: bfloat16 [4096, 2048], P(('node', 'local'), 'cuts'), may hold values from -6 to 6
- routes: int32 [4096, 8], P(('node', 'local')), may hold values from 0 to 127, all different within a row; in each aligned block of 128 rows (0 to 127, 128 to 255, ...) at most 12 rows name the same one
- gates: bfloat16 [4096, 8], P(('node', 'local')), may hold values from 0.049804688 to 0.29882812
- cotangent: bfloat16 [4096, 2048], P(('node', 'local'), 'cuts'), may hold values from -6 to 6
- w_gate: bfloat16 [128, 768, 2048], P(('node', 'local'), 'cuts'), may hold values from -0.125 to 0.125
- w_up: bfloat16 [128, 768, 2048], P(('node', 'local'), 'cuts'), may hold values from -0.125 to 0.125
- w_down: bfloat16 [128, 768, 2048], P(('node', 'local'), 'cuts'), may hold values from -0.21875 to 0.21875
Outputs:
- mixed: bfloat16 [4096, 2048], P(('node', 'local'), 'cuts')
- grad_tokens: bfloat16 [4096, 2048], P(('node', 'local'), 'cuts')
- grad_gate: bfloat16 [128, 768, 2048], P(('node', 'local'), 'cuts')
- grad_up: bfloat16 [128, 768, 2048], P(('node', 'local'), 'cuts')
- grad_down: bfloat16 [128, 768, 2048], P(('node', 'local'), 'cuts')
The draws below stay inside these ranges and needn't reach their ends.
Inputs may be any that keep to these rules, and one draw needn't show every extreme that they name: `routes`: each row names 8 different experts. Within each aligned block of 128 rows (the tokens of one index of node and local) no expert is named more than 12 times, and in every draw some expert is named exactly 12 times in some block.
All inputs are finite; a program needn't handle non-finite values.
Results may differ from the reference program's by a relative error of at most 0.015.
Values may be sent and summed in bfloat16 or wider, within the bound.
No kernel may reach another device: no remote copies, remote signals or barrier semaphores. Data moves between devices by JAX's collectives and lax.ppermute only.
A program may use at most 128 MiB of HBM per device.

```python
import math
import jax
import jax.numpy as jnp
import numpy as np
from jax import lax

D = 2048
FF = 768
TOP = 8
TOK_GRP = 128
EXPERTS = 128
TOKENS = 4096
CAP = 12
N_NODE = 8
N_LOCAL = 4
N_CUTS = 4


def level_of(stream_key, dims, cuts, low, high):
    factor_of = 1.0
    for dim, parts in cuts:
        heights = jax.random.uniform(jax.random.fold_in(jax.random.fold_in(stream_key, 6), dim), (parts,), jnp.float32, low / len(cuts), high / len(cuts))
        factor_of = factor_of * jnp.repeat(jnp.exp(heights), dims[dim] // parts).reshape((-1,) + (1,) * (len(dims) - 1 - dim))
    return factor_of


def deal_out(rng, own, number, rows, amount, top, reach, skew):
    sequence = jax.random.permutation(rng, amount)
    heavy_load, usual = shares(amount, rows * top, reach, skew, True), shares(amount, rows * top, reach, skew, False)
    places = jnp.arange(amount)

    def named(tallies, turn):
        used = int((tallies > 0).sum())
        fixed = max(1, used // 4)
        moved = fixed + (places - fixed + turn * (used - fixed)) % max(1, amount - fixed)
        return jnp.zeros((amount,), jnp.int32).at[sequence[jnp.where(places < fixed, places, moved)]].set(jnp.asarray(tallies, jnp.int32))

    tallies = jnp.where(number % 4 == 0, named(heavy_load, number // 4), named(usual, number - number // 4 - 1))
    mixed = jax.random.permutation(jax.random.fold_in(own, 3), amount)
    source_of, taker = mixed[0:amount // 2 * 2:2], mixed[1:amount // 2 * 2:2]
    slack = jnp.minimum(tallies[source_of] - 1, reach - tallies[taker]) // 2
    slack = jnp.where((source_of == sequence[0]) | (taker == sequence[0]) | (tallies[taker] == 0), 0, jnp.maximum(slack, 0))
    moved = jax.random.randint(jax.random.fold_in(own, 4), (amount // 2,), 0, 1 << 20) % (slack + 1)
    tallies = tallies.at[source_of].add(-moved).at[taker].add(moved)
    items = jnp.searchsorted(jnp.cumsum(tallies), jnp.arange(rows * top), side="right").astype(jnp.int32)
    grid = items.reshape(top, rows).T
    grid = grid[jax.random.permutation(jax.random.fold_in(own, 1), rows)]
    turn = jax.random.randint(jax.random.fold_in(own, 2), (rows, 1), 0, top)
    return jnp.take_along_axis(grid, (jnp.arange(top)[None, :] + turn) % top, axis=1)


def shares(count, total, limit, lean, full):
    loads = [(1 << 20) // math.isqrt(standing ** lean) + 1 for standing in range(1, count + 1)]
    largest = limit if full else min(limit, max(-(-total // count), total * loads[0] // sum(loads)))
    least = 1 if total - largest >= count - 1 else 0
    holding, rest = [largest] + [least] * (count - 1), total - largest - least * (count - 1)
    while rest > 0:
        free = [i for i in range(1, count) if holding[i] < largest] or [i for i in range(1, count) if holding[i] < limit]
        whole, budget = sum([loads[i] for i in free]), rest
        for i in free:
            addition = min(limit - holding[i], max(1, budget * loads[i] // whole), rest)
            holding[i] = holding[i] + addition
            rest = rest - addition
    return np.array(holding)


def scatter_about(stream_key, dims, scale, limit, shards=(), kind=jnp.bfloat16):
    drawn = scale * jax.random.normal(stream_key, dims, jnp.float32)
    if shards:
        drawn = drawn * level_of(stream_key, dims, shards, -0.22, 0.18)
    return jnp.clip(drawn, -limit, limit).astype(kind)


def setup_inputs(seed: int = 0) -> dict:
    key_of = jax.random.split(jax.random.key(seed), 8)
    tokens = scatter_about(key_of[0], (TOKENS, D), 1.0, 6.0, ((0, 32), (1, 4)))
    routes_keys = jax.random.split(jax.random.fold_in(key_of[1], 1), TOKENS // TOK_GRP)
    routes_turns = jax.random.permutation(jax.random.fold_in(key_of[1], 3), TOKENS // TOK_GRP)
    routes = jax.vmap(lambda own, number: deal_out(jax.random.fold_in(key_of[1], 2), own, number, TOK_GRP, EXPERTS, TOP, CAP, 2))(routes_keys, routes_turns).reshape((TOKENS, TOP))
    gates = jnp.clip(0.049804688 + 0.24902344 * jax.random.uniform(key_of[2], (TOKENS, TOP), jnp.float32) ** level_of(key_of[2], (TOKENS, TOP), ((0, 32),), -0.2, 0.2), 0.049804688, 0.29882812).astype(jnp.bfloat16)
    cotangent = scatter_about(key_of[3], (TOKENS, D), 1.0, 6.0, ((0, 32), (1, 4)))
    w_gate = scatter_about(key_of[4], (EXPERTS, FF, D), D ** -0.5, 0.125, ((0, 32), (1, 4)))
    w_up = scatter_about(key_of[5], (EXPERTS, FF, D), D ** -0.5, 0.125, ((0, 32), (1, 4)))
    w_down = scatter_about(key_of[6], (EXPERTS, FF, D), FF ** -0.5, 0.21875, ((0, 32), (1, 4)))
    return dict(tokens=tokens, routes=routes, gates=gates, cotangent=cotangent, w_gate=w_gate, w_up=w_up, w_down=w_down)


def expert_pass(operands):
    expert_rows, expert_grads, gate_w, up_w, down_w = operands
    row_count = expert_rows.shape[0]
    gate_pre = jnp.dot(expert_rows, gate_w.T, preferred_element_type=jnp.float32)
    up_pre = jnp.dot(expert_rows, up_w.T, preferred_element_type=jnp.float32)
    activated = jax.nn.silu(gate_pre)
    hidden = (activated * up_pre).astype(jnp.bfloat16)
    grad_hidden = jnp.dot(expert_grads, down_w.T, preferred_element_type=jnp.float32)
    sigmoid_val = jax.nn.sigmoid(gate_pre)
    grad_a = (grad_hidden * up_pre * sigmoid_val * (1.0 + gate_pre * (1.0 - sigmoid_val))).astype(jnp.bfloat16)
    grad_b = (grad_hidden * activated).astype(jnp.bfloat16)
    block_width = FF // N_CUTS
    out_total = jnp.zeros((row_count, D), jnp.float32)
    back_total = jnp.zeros((row_count, D), jnp.float32)
    for cut_index in range(N_CUTS):
        start_col = cut_index * block_width
        end_col = start_col + block_width
        out_piece = jnp.dot(hidden[:, start_col:end_col], down_w[start_col:end_col], preferred_element_type=jnp.float32)
        back_piece = jnp.dot(grad_a[:, start_col:end_col], gate_w[start_col:end_col], preferred_element_type=jnp.float32)
        back_piece = back_piece + jnp.dot(grad_b[:, start_col:end_col], up_w[start_col:end_col], preferred_element_type=jnp.float32)
        out_piece, back_piece = lax.optimization_barrier((out_piece.astype(jnp.bfloat16), back_piece.astype(jnp.bfloat16)))
        out_total = out_total + out_piece.astype(jnp.float32)
        back_total = back_total + back_piece.astype(jnp.float32)
    weight_gate = jnp.dot(grad_a.T, expert_rows, preferred_element_type=jnp.float32).astype(jnp.bfloat16)
    weight_up = jnp.dot(grad_b.T, expert_rows, preferred_element_type=jnp.float32).astype(jnp.bfloat16)
    weight_down = jnp.dot(hidden.T, expert_grads, preferred_element_type=jnp.float32).astype(jnp.bfloat16)
    return (out_total.astype(jnp.bfloat16), back_total.astype(jnp.bfloat16), weight_gate, weight_up, weight_down)


def reference(tokens, routes, gates, cotangent, w_gate, w_up, w_down):
    expert_total = w_gate.shape[0]
    groups = N_NODE * N_LOCAL
    token_total, top_k = routes.shape
    tok_group = token_total // groups
    slot_total = groups * CAP
    grouped = routes.reshape(groups, tok_group * top_k)
    onehot = (grouped[:, :, None] == jnp.arange(expert_total, dtype=jnp.int32)[None, None, :]).astype(jnp.int32)
    slot_rank = jnp.sum((jnp.cumsum(onehot, axis=1) - 1) * onehot, axis=2).astype(jnp.int32)
    position = (jnp.arange(groups, dtype=jnp.int32)[:, None] * CAP + slot_rank).reshape(-1).astype(jnp.int32)
    expert_id = routes.reshape(-1).astype(jnp.int32)
    token_id = (jnp.arange(token_total * top_k, dtype=jnp.int32) // top_k).astype(jnp.int32)
    gate_flat = gates.reshape(-1).astype(jnp.float32)
    grad_rows = (gate_flat[:, None] * cotangent[token_id].astype(jnp.float32)).astype(jnp.bfloat16)
    x_buffer = jnp.zeros((expert_total, slot_total, D), jnp.bfloat16).at[expert_id, position].set(tokens[token_id])
    g_buffer = jnp.zeros((expert_total, slot_total, D), jnp.bfloat16).at[expert_id, position].set(grad_rows)
    out_buf, back_buf, grad_gate, grad_up, grad_down = lax.map(expert_pass, (x_buffer, g_buffer, w_gate, w_up, w_down))
    out_rows = out_buf[expert_id, position].astype(jnp.float32)
    back_rows = back_buf[expert_id, position].astype(jnp.float32)
    mixed = jnp.sum((gate_flat[:, None] * out_rows).reshape(token_total, top_k, D), axis=1).astype(jnp.bfloat16)
    grad_tokens = jnp.sum(back_rows.reshape(token_total, top_k, D), axis=1).astype(jnp.bfloat16)
    return (mixed, grad_tokens, grad_gate, grad_up, grad_down)
```

```python
import functools

import jax
import jax.numpy as jnp
from jax import lax
from jax.experimental import pallas as pl
from jax.experimental.pallas import tpu as pltpu
from jax.sharding import Mesh
from jax.sharding import PartitionSpec as P

BF = jnp.bfloat16
F32 = jnp.float32
CAP = 12
GROUP = ("y", "c", "z")
VMEM_LIMIT = 52 * 1024 * 1024


def fetch(a, axis, r):
    n = lax.axis_size(axis)
    return lax.ppermute(a, axis, [((i + r) % n, i) for i in range(n)])


def add(*terms):
    total = terms[0].astype(F32)
    for term in terms[1:]:
        total = total + term.astype(F32)
    return total.astype(BF)


def nt(a, b):
    return lax.dot_general(a, b, (((1,), (1,)), ((), ())), preferred_element_type=F32)


def tn(a, b):
    return lax.dot_general(a, b, (((0,), (0,)), ((), ())), preferred_element_type=F32)


def nn(a, b):
    return jnp.dot(a, b, preferred_element_type=F32)


def pick_rows(y, maps_ref, token_blocks, own_ref, sib_ref):
    n_exp = own_ref.shape[0]
    span = own_ref.shape[1] // 4
    for yr in range(4):
        y_abs = lax.rem(y + yr, 4)
        rows = pl.ds(pl.multiple_of(y_abs * span, 16), span)
        for f in range(2):
            picked = nn(maps_ref[y_abs], token_blocks[yr][f]()).astype(BF)
            width = picked.shape[1]
            for e in range(n_exp):
                own_ref[e, rows, f * width : (f + 1) * width] = picked[e * span : (e + 1) * span]
                lo = (n_exp + e) * span
                sib_ref[e, rows, f * width : (f + 1) * width] = picked[lo : lo + span]


def glue_rows(*pieces):
    return jnp.concatenate([p.reshape(-1, p.shape[-1]) for p in pieces], axis=0)


def pick_yfirst_kernel(ids_ref, maps_ref, y0, y1, lo2, hi2, y3, own_ref, sib_ref):
    blocks = []
    for refs in ((y0,), (y1,), (lo2, hi2), (y3,)):
        blocks.append([lambda refs=refs, f=f: glue_rows(*[r[:, f] for r in refs]) for f in range(2)])
    pick_rows(ids_ref[0], maps_ref, blocks, own_ref, sib_ref)


def pick_zfirst_kernel(ids_ref, maps_ref, z0, z1, lo2, hi2, z3, own_ref, sib_ref):
    blocks = []
    for yr in range(4):
        far = (lo2, yr) if yr < 2 else (hi2, yr - 2)
        refs = ((z0, yr), (z1, yr), far, (z3, yr))
        blocks.append([lambda refs=refs, f=f: glue_rows(*[r[i, f] for r, i in refs]) for f in range(2)])
    pick_rows(ids_ref[0], maps_ref, blocks, own_ref, sib_ref)


def pick(kernel, ids, maps, pieces, n_exp):
    width = 2 * pieces[0].shape[-1]
    rows = maps.shape[1] // (2 * n_exp) * 4
    shape = jax.ShapeDtypeStruct((n_exp, rows, width), BF)
    vmem = pl.BlockSpec(memory_space=pltpu.VMEM)
    flops = 2 * 4 * maps.shape[1] * maps.shape[2] * width
    return pl.pallas_call(
        kernel,
        out_shape=(shape, shape),
        in_specs=[pl.BlockSpec(memory_space=pltpu.SMEM)] + [vmem] * (1 + len(pieces)),
        out_specs=(vmem, vmem),
        compiler_params=pltpu.CompilerParams(vmem_limit_bytes=VMEM_LIMIT),
        cost_estimate=pl.CostEstimate(flops=flops, bytes_accessed=9 << 20, transcendentals=0),
    )(ids, maps, *pieces)


def token_sums(y, maps_ref, own_refs, sib_refs, yr):
    span = own_refs[0].shape[1] // 4
    y_abs = lax.rem(y + yr, 4)
    rows = pl.ds(pl.multiple_of(y_abs * span, 16), span)
    parts = [ref[e, rows, :] for ref in own_refs + sib_refs for e in range(ref.shape[0])]
    return tn(maps_ref[y_abs], jnp.concatenate(parts, axis=0)).astype(BF)


def put(total, refs):
    tok, half = 128, total.shape[1] // 2
    for i, (ref, place) in enumerate(refs):
        for f in range(2):
            ref[place, f] = total[i * tok : (i + 1) * tok, f * half : (f + 1) * half]


def sum_yfirst_kernel(ids_ref, maps_ref, o0, o1, s0, s1, y0, y1, lo2, hi2, y3):
    dest = {
        0: [(y0, i) for i in range(4)],
        1: [(y1, i) for i in range(4)],
        2: [(lo2, 0), (lo2, 1), (hi2, 0), (hi2, 1)],
        3: [(y3, i) for i in range(4)],
    }
    for yr in (2, 1, 3, 0):
        put(token_sums(ids_ref[0], maps_ref, (o0, o1), (s0, s1), yr), dest[yr])


def sum_zfirst_kernel(ids_ref, maps_ref, o0, o1, s0, s1, z0, z1, lo2, hi2, z3):
    for yr in range(4):
        far = (lo2, yr) if yr < 2 else (hi2, yr - 2)
        put(
            token_sums(ids_ref[0], maps_ref, (o0, o1), (s0, s1), yr),
            [(z0, yr), (z1, yr), far, (z3, yr)],
        )


def sum_tokens(kernel, ids, maps, rows):
    whole = jax.ShapeDtypeStruct((4, 2, 128, rows[0].shape[2] // 2), BF)
    half = jax.ShapeDtypeStruct((2,) + whole.shape[1:], BF)
    vmem = pl.BlockSpec(memory_space=pltpu.VMEM)
    flops = 2 * 4 * maps.shape[1] * maps.shape[2] * rows[0].shape[2]
    return pl.pallas_call(
        kernel,
        out_shape=(whole, whole, half, half, whole),
        in_specs=[pl.BlockSpec(memory_space=pltpu.SMEM)] + [vmem] * 5,
        out_specs=(vmem,) * 5,
        compiler_params=pltpu.CompilerParams(vmem_limit_bytes=VMEM_LIMIT),
        cost_estimate=pl.CostEstimate(flops=flops, bytes_accessed=9 << 20, transcendentals=0),
    )(ids, maps, *rows)


def expert_kernel(n_alias, ids_ref, *refs):
    x_refs, refs = refs[:4], refs[4:]
    (go1, go2, gs1, gs2, wg, wu, wd), refs = refs[:7], refs[7 + n_alias :]
    oo1, oo2, os1, os2 = refs[:4]
    back_refs = refs[4:8]
    dwg, dwu, dwd = refs[8:]
    c = ids_ref[2]
    me = ids_ref[3]
    width = x_refs[0].shape[-1]
    cols = [pl.ds(pl.multiple_of(lax.rem(me + r, 4) * width, width), width) for r in range(4)]
    half = x_refs[0].shape[2]
    x_rows = [jnp.concatenate([ref[0, c], ref[0, 1 - c]], axis=0) for ref in x_refs]
    g_rows = []
    for own, sib in ((go1, gs1), (go2, gs2)):
        for f in range(2):
            s = slice(f * width, (f + 1) * width)
            g_rows.append(jnp.concatenate([own[0, :, s], sib[0, :, s]], axis=0))
    a = sum(nt(x_rows[r], wg[0, :, cols[r]]) for r in range(4))
    b = sum(nt(x_rows[r], wu[0, :, cols[r]]) for r in range(4))
    gh = sum(nt(g_rows[r], wd[0, :, cols[r]]) for r in range(4))
    s = jax.nn.sigmoid(a)
    act = a * s
    hidden = (act * b).astype(BF)
    da = (gh * b * s * (1.0 + a * (1.0 - s))).astype(BF)
    db = (gh * act).astype(BF)
    out_refs = ((oo1, os1), (oo1, os1), (oo2, os2), (oo2, os2))
    for r in (2, 1, 3, 0):
        wdr, wgr, wur = wd[0, :, cols[r]], wg[0, :, cols[r]], wu[0, :, cols[r]]
        out = nn(hidden, wdr).astype(BF)
        s = slice((r % 2) * width, (r % 2 + 1) * width)
        out_refs[r][0][0, :, s] = out[:half]
        out_refs[r][1][0, :, s] = out[half:]
        back = (nn(da, wgr) + nn(db, wur)).astype(BF)
        back_refs[r][0, c] = back[:half]
        back_refs[r][0, 1 - c] = back[half:]
        dwg[0, :, cols[r]] = tn(da, x_rows[r]).astype(BF)
        dwu[0, :, cols[r]] = tn(db, x_rows[r]).astype(BF)
        dwd[0, :, cols[r]] = tn(hidden, g_rows[r]).astype(BF)


def experts(ids, part, x_blocks, g_blocks, weights, grads):
    n = x_blocks[0].shape[0]
    base = part * n
    here = lambda a: pl.BlockSpec((1,) + a.shape[1:], lambda i: (i,) + (0,) * (a.ndim - 1))
    there = lambda a: pl.BlockSpec((1,) + a.shape[1:], lambda i: (base + i,) + (0,) * (a.ndim - 1))
    rows = jax.ShapeDtypeStruct((n,) + g_blocks[0].shape[1:], BF)
    back = jax.ShapeDtypeStruct(x_blocks[0].shape, BF)
    dw = jax.ShapeDtypeStruct(weights[0].shape, BF)
    first = 1 + 4 + 4 + 3
    flops = 9 * 2 * n * 2 * g_blocks[0].shape[1] * weights[0].shape[1] * weights[0].shape[2]
    return pl.pallas_call(
        functools.partial(expert_kernel, len(grads)),
        grid=(n,),
        out_shape=(rows,) * 4 + (back,) * 4 + (dw,) * 3,
        in_specs=[pl.BlockSpec(memory_space=pltpu.SMEM)]
        + [here(a) for a in x_blocks]
        + [there(a) for a in g_blocks]
        + [there(a) for a in weights]
        + [pl.BlockSpec(memory_space=pl.ANY)] * len(grads),
        out_specs=tuple([here(rows)] * 4 + [here(back)] * 4 + [there(dw)] * 3),
        input_output_aliases={first + i: 8 + i for i in range(len(grads))},
        compiler_params=pltpu.CompilerParams(vmem_limit_bytes=VMEM_LIMIT),
        cost_estimate=pl.CostEstimate(flops=flops, bytes_accessed=22 << 20, transcendentals=0),
    )(ids, *x_blocks, *g_blocks, *weights, *grads)


def spread_small(a, axis):
    return jnp.stack([a] + [fetch(a, axis, r) for r in (1, 2, 3)])


def spread(a, axis):
    up, down = fetch(a, axis, 1), fetch(a, axis, -1)
    half = a.shape[0] // 2
    return (a, up, fetch(up[:half], axis, 1), fetch(down[half:], axis, -1), down)


def collect(parts, axis):
    own, up, far_lo, far_hi, down = parts
    half = far_lo.shape[0]
    got_lo, got_hi = fetch(far_lo, axis, -1), fetch(far_hi, axis, 1)
    up = jnp.concatenate([add(up[:half], got_lo), up[half:]])
    down = jnp.concatenate([down[:half], add(down[half:], got_hi)])
    return add(own, fetch(up, axis, -1), fetch(down, axis, 1))


def collect_small(parts, axis):
    return add(parts[0], *[fetch(parts[r], axis, -r) for r in (1, 2, 3)])


def ranks(named):
    tok = named.shape[-1]
    earlier = jnp.arange(tok)[:, None] < jnp.arange(tok)[None, :]
    count = jnp.dot(named.astype(BF), earlier.astype(BF), preferred_element_type=F32)
    return jnp.where(named > 0, count, -1.0)


def body(tokens, routes, gates, cotangent, w_gate, w_up, w_down):
    y, c, z, x = (lax.axis_index(a) for a in ("y", "c", "z", "x"))
    ids = jnp.stack([y, z, c, x]).astype(jnp.int32)
    n_exp = w_gate.shape[0]
    total_exp = n_exp * 32
    tok = tokens.shape[0]
    width = tokens.shape[1]

    cot = [cotangent] + [fetch(cotangent, "x", r) for r in (1, 2, 3)]

    routes_t = routes.T
    experts_all = jnp.arange(total_exp, dtype=jnp.int32)
    named = jnp.sum((routes_t[:, None, :] == experts_all[None, :, None]).astype(F32), axis=0)
    place = ranks(named).astype(BF)
    slots = total_exp * CAP
    slot = jnp.arange(slots, dtype=jnp.int32)
    repeat = (slot[:, None] // CAP == experts_all[None, :]).astype(BF)
    place_rep = jnp.dot(repeat, place, preferred_element_type=F32)
    own_map = (place_rep == (slot % CAP).astype(F32)[:, None]).astype(BF)

    sent = jnp.dot(own_map, tokens, preferred_element_type=F32).astype(BF)
    came = lax.all_to_all(sent, GROUP, split_axis=0, concat_axis=0, tiled=True)
    came = came.reshape(4, 2, 4, n_exp, CAP, width).transpose(3, 1, 0, 2, 4, 5)
    came = came.reshape(n_exp, 2, 16 * CAP, width)
    pair = n_exp // 2
    x_a, x_b = came[:pair], came[pair:]
    xa_down, xb_up = fetch(x_a, "x", -1), fetch(x_b, "x", 1)
    xa_up, xb_down = fetch(x_a, "x", 1), fetch(x_b, "x", -1)
    xa_far, xb_far = fetch(xa_down, "x", -1), fetch(xb_up, "x", 1)
    x_blocks = ((x_a, xa_up, xa_far, xa_down), (x_b, xb_up, xb_far, xb_down))

    h1, h2 = jnp.stack(cot[:2]), jnp.stack(cot[2:])
    tok_y = spread(spread_small(h1, "z"), "y")
    tok_z = spread(spread_small(h2, "y"), "z")

    meta = jnp.concatenate([routes_t.astype(F32), gates.T.astype(F32)], axis=0)
    meta = lax.all_gather(meta, ("y", "z"), axis=0, tiled=False).reshape(4, 4, -1, tok)
    top = routes.shape[1]
    mine = jnp.arange(n_exp)
    first = lambda core: ((y * 2 + core) * 4 + z) * n_exp
    chip_exp = jnp.concatenate([first(c) + mine, first(1 - c) + mine]).astype(F32)
    same = meta[:, :, :top, None, :] == chip_exp[None, None, None, :, None]
    chip_named = jnp.sum(same.astype(F32), axis=2)
    chip_gate = jnp.sum(jnp.where(same, meta[:, :, top:, None, :], 0.0), axis=2)
    chip_place = ranks(chip_named)
    to_rows = lambda a: a.transpose(0, 2, 1, 3)[:, :, :, None, None, :]
    here = jnp.arange(4)[:, None] == (z + jnp.arange(4))[None, :] % 4
    hit = (to_rows(chip_place) == jnp.arange(CAP, dtype=F32)[:, None, None]) & here[:, None, :, None]
    maps = jnp.where(hit, to_rows(chip_gate), 0.0).astype(BF)
    maps = maps.reshape(4, 2 * n_exp * 4 * CAP, 4 * tok)

    go1, gs1 = pick(pick_yfirst_kernel, ids, maps, tok_y, n_exp)
    go2, gs2 = pick(pick_zfirst_kernel, ids, maps, tok_z, n_exp)
    g_blocks = (go1, go2, fetch(gs1, "c", 1), fetch(gs2, "c", 1))

    weights = (w_gate, w_up, w_down)
    res_a = experts(ids, 0, x_blocks[0], g_blocks, weights, ())
    res_b = experts(ids, 1, x_blocks[1], g_blocks, weights, res_a[8:])
    grads = res_b[8:]

    back_a, back_b = list(res_a[4:8]), list(res_b[4:8])
    back_a[1] = add(back_a[1], fetch(back_a[2], "x", -1))
    back_b[3] = add(back_b[3], fetch(back_b[2], "x", 1))
    back = [
        add(b[0], fetch(b[1], "x", -1), fetch(b[3], "x", 1)) for b in (back_a, back_b)
    ]
    back = jnp.concatenate(back).reshape(n_exp, 2, 4, 4, CAP, width).transpose(2, 1, 3, 0, 4, 5)
    back = lax.all_to_all(
        back.reshape(slots, width), GROUP, split_axis=0, concat_axis=0, tiled=True
    )
    grad_tokens = tn(own_map, back).astype(BF)

    sib = [fetch(res[i], "c", 1) for i in (2, 3) for res in (res_a, res_b)]
    sums_y = sum_tokens(sum_yfirst_kernel, ids, maps, (res_a[0], res_b[0], sib[0], sib[1]))
    sums_z = sum_tokens(sum_zfirst_kernel, ids, maps, (res_a[1], res_b[1], sib[2], sib[3]))
    part1 = collect_small(collect(sums_y, "y"), "z")
    part2 = collect_small(collect(sums_z, "z"), "y")
    mixed = collect_small((part1[0], part1[1], part2[0], part2[1]), "x")
    return (mixed, grad_tokens) + tuple(grads)


def solution(mesh):
    split = Mesh(mesh.devices.reshape(4, 2, 4, 4), ("y", "c", "z", "x"))
    acts = P(GROUP, "x")
    rows = P(GROUP, None)
    wts = P(GROUP, "x", None)
    return jax.shard_map(
        body,
        mesh=split,
        in_specs=(acts, rows, rows, acts, wts, wts, wts),
        out_specs=(acts, acts, wts, wts, wts),
        check_vma=False,
    )
```

```python
import functools

import jax
import jax.numpy as jnp
from jax import lax
from jax.experimental import pallas as pl
from jax.experimental.pallas import tpu as pltpu
from jax.sharding import Mesh
from jax.sharding import PartitionSpec as P

BF = jnp.bfloat16
F32 = jnp.float32
CAP = 12
GROUP = ("y", "c", "z")
VMEM_LIMIT = 52 * 1024 * 1024


def fetch(a, axis, r):
    n = lax.axis_size(axis)
    return lax.ppermute(a, axis, [((i + r) % n, i) for i in range(n)])


def add(*terms):
    total = terms[0].astype(F32)
    for term in terms[1:]:
        total = total + term.astype(F32)
    return total.astype(BF)


def nt(a, b):
    return lax.dot_general(a, b, (((1,), (1,)), ((), ())), preferred_element_type=F32)


def tn(a, b):
    return lax.dot_general(a, b, (((0,), (0,)), ((), ())), preferred_element_type=F32)


def nn(a, b):
    return jnp.dot(a, b, preferred_element_type=F32)


def slot_map(ids_ref, meta, n_exp):
    tok = meta[0].shape[1]
    y, z, c = ids_ref[0], ids_ref[1], ids_ref[2]
    top = meta[0].shape[0] // 2
    both = 2 * n_exp
    line = lax.broadcasted_iota(jnp.int32, (both, tok), 0)
    core = jnp.where(line < n_exp, c, 1 - c)
    expert = (y * 2 + core) * 4 + z
    expert = (expert * n_exp + lax.rem(line, n_exp)).astype(F32)
    earlier = (
        lax.broadcasted_iota(jnp.int32, (tok, tok), 0) < lax.broadcasted_iota(jnp.int32, (tok, tok), 1)
    ).astype(BF)
    widen = (
        lax.broadcasted_iota(jnp.int32, (both * 4, both), 0) // 4
        == lax.broadcasted_iota(jnp.int32, (both * 4, both), 1)
    ).astype(BF)
    owner = lax.rem(lax.broadcasted_iota(jnp.int32, (both * 4, tok), 0), 4)
    slots = both * 4 * CAP
    repeat = (
        lax.broadcasted_iota(jnp.int32, (slots, both * 4), 0) // CAP
        == lax.broadcasted_iota(jnp.int32, (slots, both * 4), 1)
    ).astype(BF)
    slot = lax.rem(lax.broadcasted_iota(jnp.int32, (slots, tok), 0), CAP).astype(F32)
    columns = []
    for zr in range(4):
        data = meta[zr].astype(F32)
        named = jnp.zeros((both, tok), F32)
        gate = jnp.zeros((both, tok), F32)
        for k in range(top):
            same = data[k : k + 1] == expert
            named = jnp.where(same, 1.0, named)
            gate = jnp.where(same, data[top + k : top + k + 1], gate)
        rank = jnp.where(named > 0, nn(named.astype(BF), earlier), -1.0)
        here = owner == lax.rem(z + zr, 4)
        rank = jnp.where(here, nn(widen, rank.astype(BF)), -1.0).astype(BF)
        gate = nn(widen, gate.astype(BF)).astype(BF)
        columns.append(jnp.where(nn(repeat, rank) == slot, nn(repeat, gate), 0.0).astype(BF))
    return jnp.concatenate(columns, axis=1)


def pick_rows(y, yr, slots, token_blocks, own_ref, sib_ref):
    n_exp = own_ref.shape[0]
    span = own_ref.shape[1] // 4
    rows = pl.ds(pl.multiple_of(lax.rem(y + yr, 4) * span, 16), span)
    for f in range(2):
        picked = nn(slots, token_blocks[f]).astype(BF)
        width = picked.shape[1]
        for e in range(n_exp):
            own_ref[e, rows, f * width : (f + 1) * width] = picked[e * span : (e + 1) * span]
            lo = (n_exp + e) * span
            sib_ref[e, rows, f * width : (f + 1) * width] = picked[lo : lo + span]


def pick_yfirst_kernel(ids_ref, y0, y1, lo2, hi2, y3, own_ref, sib_ref, maps_ref):
    tok, n_exp = 128, own_ref.shape[0]
    for yr, refs in enumerate(((y0,), (y1,), (lo2, hi2), (y3,))):
        meta = [ref[i, 2 * tok :, :tok] for ref in refs for i in range(ref.shape[0])]
        slots = slot_map(ids_ref, meta, n_exp)
        maps_ref[yr] = slots
        blocks = [
            jnp.concatenate(
                [ref[i, f * tok : (f + 1) * tok] for ref in refs for i in range(ref.shape[0])], axis=0
            )
            for f in range(2)
        ]
        pick_rows(ids_ref[0], yr, slots, blocks, own_ref, sib_ref)


def pick_zfirst_kernel(ids_ref, maps_ref, z0, z1, lo2, hi2, z3, own_ref, sib_ref):
    for yr in range(4):
        far = (lo2, yr) if yr < 2 else (hi2, yr - 2)
        refs = ((z0, yr), (z1, yr), far, (z3, yr))
        blocks = [jnp.concatenate([ref[i, f] for ref, i in refs], axis=0) for f in range(2)]
        pick_rows(ids_ref[0], yr, maps_ref[yr], blocks, own_ref, sib_ref)


def pick(kernel, ids, arrays, n_exp, outs):
    vmem = pl.BlockSpec(memory_space=pltpu.VMEM)
    return pl.pallas_call(
        kernel,
        out_shape=outs,
        in_specs=[pl.BlockSpec(memory_space=pltpu.SMEM)] + [vmem] * len(arrays),
        out_specs=(vmem,) * len(outs),
        compiler_params=pltpu.CompilerParams(vmem_limit_bytes=VMEM_LIMIT),
        cost_estimate=pl.CostEstimate(flops=2 << 30, bytes_accessed=9 << 20, transcendentals=0),
    )(ids, *arrays)


def token_sums(y, maps_ref, own_refs, sib_refs, yr):
    span = own_refs[0].shape[1] // 4
    y_abs = lax.rem(y + yr, 4)
    rows = pl.ds(pl.multiple_of(y_abs * span, 16), span)
    parts = [ref[e, rows, :] for ref in own_refs + sib_refs for e in range(ref.shape[0])]
    return tn(maps_ref[yr], jnp.concatenate(parts, axis=0)).astype(BF)


def put(total, refs):
    tok, half = 128, total.shape[1] // 2
    for i, (ref, place) in enumerate(refs):
        for f in range(2):
            ref[place, f] = total[i * tok : (i + 1) * tok, f * half : (f + 1) * half]


def sum_yfirst_kernel(ids_ref, maps_ref, o0, o1, s0, s1, y0, y1, lo2, hi2, y3):
    dest = {
        0: [(y0, i) for i in range(4)],
        1: [(y1, i) for i in range(4)],
        2: [(lo2, 0), (lo2, 1), (hi2, 0), (hi2, 1)],
        3: [(y3, i) for i in range(4)],
    }
    for yr in (2, 1, 3, 0):
        put(token_sums(ids_ref[0], maps_ref, (o0, o1), (s0, s1), yr), dest[yr])


def sum_zfirst_kernel(ids_ref, maps_ref, o0, o1, s0, s1, z0, z1, lo2, hi2, z3):
    for yr in range(4):
        far = (lo2, yr) if yr < 2 else (hi2, yr - 2)
        put(
            token_sums(ids_ref[0], maps_ref, (o0, o1), (s0, s1), yr),
            [(z0, yr), (z1, yr), far, (z3, yr)],
        )


def sum_tokens(kernel, ids, maps, rows):
    whole = jax.ShapeDtypeStruct((4, 2, 128, rows[0].shape[2] // 2), BF)
    half = jax.ShapeDtypeStruct((2,) + whole.shape[1:], BF)
    vmem = pl.BlockSpec(memory_space=pltpu.VMEM)
    flops = 2 * 4 * maps.shape[1] * maps.shape[2] * rows[0].shape[2]
    return pl.pallas_call(
        kernel,
        out_shape=(whole, whole, half, half, whole),
        in_specs=[pl.BlockSpec(memory_space=pltpu.SMEM)] + [vmem] * 5,
        out_specs=(vmem,) * 5,
        compiler_params=pltpu.CompilerParams(vmem_limit_bytes=VMEM_LIMIT),
        cost_estimate=pl.CostEstimate(flops=flops, bytes_accessed=9 << 20, transcendentals=0),
    )(ids, maps, *rows)


def expert_kernel(n_alias, ids_ref, x_ref, *refs):
    (go1, go2, gs1, gs2, wg, wu, wd), refs = refs[:7], refs[7 + n_alias :]
    oo1, oo2, os1, os2, back_ref, dwg, dwu, dwd = refs
    c = ids_ref[2]
    me = ids_ref[3]
    n = x_ref.shape[0]
    half, width = x_ref.shape[3:]
    fixed = [slice(r * width, (r + 1) * width) for r in range(n)]
    moved = [pl.ds(pl.multiple_of(lax.rem(me + r, n) * width, width), width) for r in range(n)]
    x_rows = [jnp.concatenate([x_ref[r, 0, c], x_ref[r, 0, 1 - c]], axis=0) for r in range(n)]
    g_rows = []
    for own, sib in ((go1, gs1), (go2, gs2)):
        for f in range(2):
            g_rows.append(jnp.concatenate([own[0, :, fixed[f]], sib[0, :, fixed[f]]], axis=0))
    a = sum(nt(x_rows[r], wg[0, :, fixed[r]]) for r in range(n))
    b = sum(nt(x_rows[r], wu[0, :, fixed[r]]) for r in range(n))
    gh = sum(nt(g_rows[r], wd[0, :, moved[r]]) for r in range(n))
    s = jax.nn.sigmoid(a)
    act = a * s
    hidden = (act * b).astype(BF)
    da = (gh * b * s * (1.0 + a * (1.0 - s))).astype(BF)
    db = (gh * act).astype(BF)
    out_refs = ((oo1, os1), (oo1, os1), (oo2, os2), (oo2, os2))
    for r in range(n):
        out = nn(hidden, wd[0, :, moved[r]]).astype(BF)
        out_refs[r][0][0, :, fixed[r % 2]] = out[:half]
        out_refs[r][1][0, :, fixed[r % 2]] = out[half:]
        back = (nn(da, wg[0, :, fixed[r]]) + nn(db, wu[0, :, fixed[r]])).astype(BF)
        back_ref[r, 0, c] = back[:half]
        back_ref[r, 0, 1 - c] = back[half:]
        dwg[0, :, fixed[r]] = tn(da, x_rows[r]).astype(BF)
        dwu[0, :, fixed[r]] = tn(db, x_rows[r]).astype(BF)
        dwd[0, :, moved[r]] = tn(hidden, g_rows[r]).astype(BF)


def experts(ids, part, x_blocks, g_blocks, weights, grads):
    n = x_blocks.shape[1]
    base = part * n
    blocks = pl.BlockSpec(
        x_blocks.shape[:1] + (1,) + x_blocks.shape[2:], lambda i: (0, i, 0, 0, 0)
    )
    here = lambda a: pl.BlockSpec((1,) + a.shape[1:], lambda i: (i,) + (0,) * (a.ndim - 1))
    there = lambda a: pl.BlockSpec((1,) + a.shape[1:], lambda i: (base + i,) + (0,) * (a.ndim - 1))
    rows = jax.ShapeDtypeStruct((n,) + g_blocks[0].shape[1:], BF)
    back = jax.ShapeDtypeStruct(x_blocks.shape, BF)
    dw = jax.ShapeDtypeStruct(weights[0].shape, BF)
    first = 1 + 1 + 4 + 3
    flops = 9 * 2 * n * 2 * g_blocks[0].shape[1] * weights[0].shape[1] * weights[0].shape[2]
    return pl.pallas_call(
        functools.partial(expert_kernel, len(grads)),
        grid=(n,),
        out_shape=(rows,) * 4 + (back,) + (dw,) * 3,
        in_specs=[pl.BlockSpec(memory_space=pltpu.SMEM), blocks]
        + [there(a) for a in g_blocks]
        + [there(a) for a in weights]
        + [pl.BlockSpec(memory_space=pl.ANY)] * len(grads),
        out_specs=tuple([here(rows)] * 4 + [blocks] + [there(dw)] * 3),
        input_output_aliases={first + i: 5 + i for i in range(len(grads))},
        compiler_params=pltpu.CompilerParams(vmem_limit_bytes=VMEM_LIMIT),
        cost_estimate=pl.CostEstimate(flops=flops, bytes_accessed=22 << 20, transcendentals=0),
    )(ids, x_blocks, *g_blocks, *weights, *grads)


def spread_small(a, axis):
    return jnp.stack([a] + [fetch(a, axis, r) for r in (1, 2, 3)])


def spread(a, axis):
    up, down = fetch(a, axis, 1), fetch(a, axis, -1)
    half = a.shape[0] // 2
    return (a, up, fetch(up[:half], axis, 1), fetch(down[half:], axis, -1), down)


def collect(parts, axis):
    own, up, far_lo, far_hi, down = parts
    half = far_lo.shape[0]
    got_lo, got_hi = fetch(far_lo, axis, -1), fetch(far_hi, axis, 1)
    up = jnp.concatenate([add(up[:half], got_lo), up[half:]])
    down = jnp.concatenate([down[:half], add(down[half:], got_hi)])
    return add(own, fetch(up, axis, -1), fetch(down, axis, 1))


def collect_small(parts, axis):
    return add(parts[0], *[fetch(parts[r], axis, -r) for r in (1, 2, 3)])


def ranks(named):
    tok = named.shape[-1]
    earlier = jnp.arange(tok)[:, None] < jnp.arange(tok)[None, :]
    count = jnp.dot(named.astype(BF), earlier.astype(BF), preferred_element_type=F32)
    return jnp.where(named > 0, count, -1.0)


def after(first, *rest):
    return lax.optimization_barrier((first,) + rest)[1:]


def body(tokens, routes, gates, cotangent, w_gate, w_up, w_down):
    y, c, z, x = (lax.axis_index(a) for a in ("y", "c", "z", "x"))
    ids = jnp.stack([y, z, c, x]).astype(jnp.int32)
    n_exp = w_gate.shape[0]
    total_exp = n_exp * 32
    tok, width = tokens.shape

    cot = [cotangent] + [fetch(cotangent, "x", r) for r in (1, 2, 3)]

    routes_t = routes.T
    experts_all = jnp.arange(total_exp, dtype=jnp.int32)
    named = jnp.sum((routes_t[:, None, :] == experts_all[None, :, None]).astype(F32), axis=0)
    place = ranks(named).astype(BF)
    slots = total_exp * CAP
    slot = jnp.arange(slots, dtype=jnp.int32)
    repeat = (slot[:, None] // CAP == experts_all[None, :]).astype(BF)
    place_rep = jnp.dot(repeat, place, preferred_element_type=F32)
    own_map = (place_rep == (slot % CAP).astype(F32)[:, None]).astype(BF)

    sent = jnp.dot(own_map, tokens, preferred_element_type=F32).astype(BF)
    came = lax.all_to_all(sent, GROUP, split_axis=0, concat_axis=0, tiled=True)

    meta = jnp.concatenate([routes_t.astype(BF), gates.T], axis=0)
    meta = jnp.pad(meta, ((0, 0), (0, width - tok)))
    h1 = jnp.concatenate([cot[0], cot[1], meta])
    h2 = jnp.stack(cot[2:])
    near_z, near_y = spread_small(h1, "z"), spread_small(h2, "y")
    came, near_z, near_y = lax.optimization_barrier((came, near_z, near_y))

    came = came.reshape(4, 2, 4, n_exp, CAP, width).transpose(3, 1, 0, 2, 4, 5)
    came = came.reshape(n_exp, 2, 16 * CAP, width)
    pair = n_exp // 2
    x_a, x_b = came[:pair], came[pair:]
    x_a, x_b = lax.all_gather(x_a, "x"), lax.all_gather(x_b, "x")
    y_up, y_down = fetch(near_z, "y", 1), fetch(near_z, "y", -1)
    z_up, z_down = fetch(near_y, "z", 1), fetch(near_y, "z", -1)
    tok_y = (near_z, y_up, fetch(y_up[:2], "y", 1), fetch(y_down[2:], "y", -1), y_down)
    tok_z = (near_y, z_up, fetch(z_up[:2], "z", 1), fetch(z_down[2:], "z", -1), z_down)

    half = jax.ShapeDtypeStruct((n_exp, 16 * CAP, 2 * width), BF)
    maps = jax.ShapeDtypeStruct((4, 2 * n_exp * 4 * CAP, 4 * tok), BF)
    go1, gs1, maps = pick(pick_yfirst_kernel, ids, tok_y, n_exp, (half, half, maps))
    go2, gs2 = pick(pick_zfirst_kernel, ids, (maps,) + tok_z, n_exp, (half, half))
    g_blocks = (go1, go2, fetch(gs1, "c", 1), fetch(gs2, "c", 1))

    weights = (w_gate, w_up, w_down)
    res_a = experts(ids, 0, x_a, g_blocks, weights, ())
    sib_a = [fetch(res_a[i], "c", 1) for i in (2, 3)]
    res_b = experts(ids, 1, x_b, g_blocks, weights, res_a[5:])
    grads = res_b[5:]
    sib_b = [fetch(res_b[i], "c", 1) for i in (2, 3)]

    sums_y = sum_tokens(sum_yfirst_kernel, ids, maps, (res_a[0], res_b[0], sib_a[0], sib_b[0]))
    sums_z = sum_tokens(sum_zfirst_kernel, ids, maps, (res_a[1], res_b[1], sib_a[1], sib_b[1]))
    part1, part2 = collect(sums_y, "y"), collect(sums_z, "z")

    by_expert = own_map.reshape(-1, n_exp, CAP, tok)
    grad_tokens = 0.0
    for part, res in enumerate((res_a, res_b)):
        back = lax.psum_scatter(
            res[4].reshape(-1, width), "x", scatter_dimension=0, tiled=True
        )
        back = back.reshape(pair, 2, 4, 4, CAP, width).transpose(2, 1, 3, 0, 4, 5)
        back = lax.all_to_all(
            back.reshape(-1, width), GROUP, split_axis=0, concat_axis=0, tiled=True
        )
        some = by_expert[:, part * pair : (part + 1) * pair].reshape(-1, tok)
        grad_tokens = grad_tokens + tn(some, back)
    grad_tokens = grad_tokens.astype(BF)

    part1, part2 = collect_small(part1, "z"), collect_small(part2, "y")
    mixed = collect_small((part1[0], part1[1], part2[0], part2[1]), "x")
    return (mixed, grad_tokens) + tuple(grads)


def solution(mesh):
    split = Mesh(mesh.devices.reshape(4, 2, 4, 4), ("y", "c", "z", "x"))
    acts = P(GROUP, "x")
    rows = P(GROUP, None)
    wts = P(GROUP, "x", None)
    return jax.shard_map(
        body,
        mesh=split,
        in_specs=(acts, rows, rows, acts, wts, wts, wts),
        out_specs=(acts, acts, wts, wts, wts),
        check_vma=False,
    )
```

```python
import functools

import jax
import jax.numpy as jnp
from jax import lax
from jax.experimental import pallas as pl
from jax.experimental.pallas import tpu as pltpu
from jax.sharding import Mesh
from jax.sharding import PartitionSpec as P

BF = jnp.bfloat16
F32 = jnp.float32
CAP = 12
GROUP = ("y", "c", "z")
VMEM_LIMIT = 52 * 1024 * 1024


def fetch(a, axis, r):
    n = lax.axis_size(axis)
    return lax.ppermute(a, axis, [((i + r) % n, i) for i in range(n)])


def add(*terms):
    total = terms[0].astype(F32)
    for term in terms[1:]:
        total = total + term.astype(F32)
    return total.astype(BF)


def nt(a, b):
    return lax.dot_general(a, b, (((1,), (1,)), ((), ())), preferred_element_type=F32)


def tn(a, b):
    return lax.dot_general(a, b, (((0,), (0,)), ((), ())), preferred_element_type=F32)


def nn(a, b):
    return jnp.dot(a, b, preferred_element_type=F32)


def slot_map(ids_ref, meta, n_exp):
    tok = meta[0].shape[1]
    y, z, c = ids_ref[0], ids_ref[1], ids_ref[2]
    top = meta[0].shape[0] // 2
    both = 2 * n_exp
    line = lax.broadcasted_iota(jnp.int32, (both, tok), 0)
    core = jnp.where(line < n_exp, c, 1 - c)
    expert = (y * 2 + core) * 4 + z
    expert = (expert * n_exp + lax.rem(line, n_exp)).astype(F32)
    earlier = (
        lax.broadcasted_iota(jnp.int32, (tok, tok), 0) < lax.broadcasted_iota(jnp.int32, (tok, tok), 1)
    ).astype(BF)
    widen = (
        lax.broadcasted_iota(jnp.int32, (both * 4, both), 0) // 4
        == lax.broadcasted_iota(jnp.int32, (both * 4, both), 1)
    ).astype(BF)
    owner = lax.rem(lax.broadcasted_iota(jnp.int32, (both * 4, tok), 0), 4)
    slots = both * 4 * CAP
    repeat = (
        lax.broadcasted_iota(jnp.int32, (slots, both * 4), 0) // CAP
        == lax.broadcasted_iota(jnp.int32, (slots, both * 4), 1)
    ).astype(BF)
    slot = lax.rem(lax.broadcasted_iota(jnp.int32, (slots, tok), 0), CAP).astype(F32)
    columns = []
    for zr in range(4):
        data = meta[zr].astype(F32)
        named = jnp.zeros((both, tok), F32)
        gate = jnp.zeros((both, tok), F32)
        for k in range(top):
            same = data[k : k + 1] == expert
            named = jnp.where(same, 1.0, named)
            gate = jnp.where(same, data[top + k : top + k + 1], gate)
        rank = jnp.where(named > 0, nn(named.astype(BF), earlier), -1.0)
        here = owner == lax.rem(z + zr, 4)
        rank = jnp.where(here, nn(widen, rank.astype(BF)), -1.0).astype(BF)
        gate = nn(widen, gate.astype(BF)).astype(BF)
        columns.append(jnp.where(nn(repeat, rank) == slot, nn(repeat, gate), 0.0).astype(BF))
    return jnp.concatenate(columns, axis=1)


def pick_rows(y, yr, slots, token_blocks, own_ref, sib_ref):
    n_exp = own_ref.shape[0]
    span = own_ref.shape[1] // 4
    rows = pl.ds(pl.multiple_of(lax.rem(y + yr, 4) * span, 16), span)
    for f in range(2):
        picked = nn(slots, token_blocks[f]).astype(BF)
        width = picked.shape[1]
        for e in range(n_exp):
            own_ref[e, rows, f * width : (f + 1) * width] = picked[e * span : (e + 1) * span]
            lo = (n_exp + e) * span
            sib_ref[e, rows, f * width : (f + 1) * width] = picked[lo : lo + span]


def pick_yfirst_kernel(ids_ref, y0, y1, lo2, hi2, y3, own_ref, sib_ref, maps_ref):
    tok, n_exp = 128, own_ref.shape[0]
    for yr, refs in enumerate(((y0,), (y1,), (lo2, hi2), (y3,))):
        meta = [ref[i, 2 * tok :, :tok] for ref in refs for i in range(ref.shape[0])]
        slots = slot_map(ids_ref, meta, n_exp)
        maps_ref[yr] = slots
        blocks = [
            jnp.concatenate(
                [ref[i, f * tok : (f + 1) * tok] for ref in refs for i in range(ref.shape[0])], axis=0
            )
            for f in range(2)
        ]
        pick_rows(ids_ref[0], yr, slots, blocks, own_ref, sib_ref)


def pick_zfirst_kernel(ids_ref, maps_ref, z0, z1, lo2, hi2, z3, own_ref, sib_ref):
    for yr in range(4):
        far = (lo2, yr) if yr < 2 else (hi2, yr - 2)
        refs = ((z0, yr), (z1, yr), far, (z3, yr))
        blocks = [jnp.concatenate([ref[i, f] for ref, i in refs], axis=0) for f in range(2)]
        pick_rows(ids_ref[0], yr, maps_ref[yr], blocks, own_ref, sib_ref)


def pick(kernel, ids, arrays, n_exp, outs):
    vmem = pl.BlockSpec(memory_space=pltpu.VMEM)
    return pl.pallas_call(
        kernel,
        out_shape=outs,
        in_specs=[pl.BlockSpec(memory_space=pltpu.SMEM)] + [vmem] * len(arrays),
        out_specs=(vmem,) * len(outs),
        compiler_params=pltpu.CompilerParams(vmem_limit_bytes=VMEM_LIMIT),
        cost_estimate=pl.CostEstimate(flops=2 << 30, bytes_accessed=9 << 20, transcendentals=0),
    )(ids, *arrays)


def token_sums(y, maps_ref, own_refs, sib_refs, yr):
    span = own_refs[0].shape[1] // 4
    y_abs = lax.rem(y + yr, 4)
    rows = pl.ds(pl.multiple_of(y_abs * span, 16), span)
    parts = [ref[e, rows, :] for ref in own_refs + sib_refs for e in range(ref.shape[0])]
    return tn(maps_ref[yr], jnp.concatenate(parts, axis=0)).astype(BF)


def put(total, refs):
    tok, half = 128, total.shape[1] // 2
    for i, (ref, place) in enumerate(refs):
        for f in range(2):
            ref[place, f] = total[i * tok : (i + 1) * tok, f * half : (f + 1) * half]


def sum_yfirst_kernel(ids_ref, maps_ref, o0, o1, s0, s1, y0, y1, lo2, hi2, y3):
    dest = {
        0: [(y0, i) for i in range(4)],
        1: [(y1, i) for i in range(4)],
        2: [(lo2, 0), (lo2, 1), (hi2, 0), (hi2, 1)],
        3: [(y3, i) for i in range(4)],
    }
    for yr in (2, 1, 3, 0):
        put(token_sums(ids_ref[0], maps_ref, (o0, o1), (s0, s1), yr), dest[yr])


def sum_zfirst_kernel(ids_ref, maps_ref, o0, o1, s0, s1, z0, z1, lo2, hi2, z3):
    for yr in range(4):
        far = (lo2, yr) if yr < 2 else (hi2, yr - 2)
        put(
            token_sums(ids_ref[0], maps_ref, (o0, o1), (s0, s1), yr),
            [(z0, yr), (z1, yr), far, (z3, yr)],
        )


def sum_tokens(kernel, ids, maps, rows):
    whole = jax.ShapeDtypeStruct((4, 2, 128, rows[0].shape[2] // 2), BF)
    half = jax.ShapeDtypeStruct((2,) + whole.shape[1:], BF)
    vmem = pl.BlockSpec(memory_space=pltpu.VMEM)
    flops = 2 * 4 * maps.shape[1] * maps.shape[2] * rows[0].shape[2]
    return pl.pallas_call(
        kernel,
        out_shape=(whole, whole, half, half, whole),
        in_specs=[pl.BlockSpec(memory_space=pltpu.SMEM)] + [vmem] * 5,
        out_specs=(vmem,) * 5,
        compiler_params=pltpu.CompilerParams(vmem_limit_bytes=VMEM_LIMIT),
        cost_estimate=pl.CostEstimate(flops=flops, bytes_accessed=9 << 20, transcendentals=0),
    )(ids, maps, *rows)


def expert_kernel(n_alias, ids_ref, x_ref, *refs):
    (go1, go2, gs1, gs2, wg, wu, wd), refs = refs[:7], refs[7 + n_alias :]
    oo1, oo2, os1, os2, back_ref, dwg, dwu, dwd = refs
    c = ids_ref[2]
    me = ids_ref[3]
    n = x_ref.shape[0]
    half, width = x_ref.shape[3:]
    fixed = [slice(r * width, (r + 1) * width) for r in range(n)]
    moved = [pl.ds(pl.multiple_of(lax.rem(me + r, n) * width, width), width) for r in range(n)]
    x_rows = [jnp.concatenate([x_ref[r, 0, c], x_ref[r, 0, 1 - c]], axis=0) for r in range(n)]
    g_rows = []
    for own, sib in ((go1, gs1), (go2, gs2)):
        for f in range(2):
            g_rows.append(jnp.concatenate([own[0, :, fixed[f]], sib[0, :, fixed[f]]], axis=0))
    a = sum(nt(x_rows[r], wg[0, :, fixed[r]]) for r in range(n))
    b = sum(nt(x_rows[r], wu[0, :, fixed[r]]) for r in range(n))
    gh = sum(nt(g_rows[r], wd[0, :, moved[r]]) for r in range(n))
    s = jax.nn.sigmoid(a)
    act = a * s
    hidden = (act * b).astype(BF)
    da = (gh * b * s * (1.0 + a * (1.0 - s))).astype(BF)
    db = (gh * act).astype(BF)
    out_refs = ((oo1, os1), (oo1, os1), (oo2, os2), (oo2, os2))
    for r in range(n):
        out = nn(hidden, wd[0, :, moved[r]]).astype(BF)
        out_refs[r][0][0, :, fixed[r % 2]] = out[:half]
        out_refs[r][1][0, :, fixed[r % 2]] = out[half:]
        back = (nn(da, wg[0, :, fixed[r]]) + nn(db, wu[0, :, fixed[r]])).astype(BF)
        back_ref[r, 0, c] = back[:half]
        back_ref[r, 0, 1 - c] = back[half:]
        dwg[0, :, fixed[r]] = tn(da, x_rows[r]).astype(BF)
        dwu[0, :, fixed[r]] = tn(db, x_rows[r]).astype(BF)
        dwd[0, :, moved[r]] = tn(hidden, g_rows[r]).astype(BF)


def experts(ids, part, x_blocks, g_blocks, weights, grads):
    n = x_blocks.shape[1]
    base = part * n
    blocks = pl.BlockSpec(
        x_blocks.shape[:1] + (1,) + x_blocks.shape[2:], lambda i: (0, i, 0, 0, 0)
    )
    here = lambda a: pl.BlockSpec((1,) + a.shape[1:], lambda i: (i,) + (0,) * (a.ndim - 1))
    there = lambda a: pl.BlockSpec((1,) + a.shape[1:], lambda i: (base + i,) + (0,) * (a.ndim - 1))
    rows = jax.ShapeDtypeStruct((n,) + g_blocks[0].shape[1:], BF)
    back = jax.ShapeDtypeStruct(x_blocks.shape, BF)
    dw = jax.ShapeDtypeStruct(weights[0].shape, BF)
    first = 1 + 1 + 4 + 3
    flops = 9 * 2 * n * 2 * g_blocks[0].shape[1] * weights[0].shape[1] * weights[0].shape[2]
    return pl.pallas_call(
        functools.partial(expert_kernel, len(grads)),
        grid=(n,),
        out_shape=(rows,) * 4 + (back,) + (dw,) * 3,
        in_specs=[pl.BlockSpec(memory_space=pltpu.SMEM), blocks]
        + [there(a) for a in g_blocks]
        + [there(a) for a in weights]
        + [pl.BlockSpec(memory_space=pl.ANY)] * len(grads),
        out_specs=tuple([here(rows)] * 4 + [blocks] + [there(dw)] * 3),
        input_output_aliases={first + i: 5 + i for i in range(len(grads))},
        compiler_params=pltpu.CompilerParams(vmem_limit_bytes=VMEM_LIMIT),
        cost_estimate=pl.CostEstimate(flops=flops, bytes_accessed=22 << 20, transcendentals=0),
    )(ids, x_blocks, *g_blocks, *weights, *grads)


def spread_small(a, axis):
    return jnp.stack([a] + [fetch(a, axis, r) for r in (1, 2, 3)])


def collect_far(parts, axis):
    own, up, far_lo, far_hi, down = parts
    half = far_lo.shape[0]
    got_lo, got_hi = fetch(far_lo, axis, -1), fetch(far_hi, axis, 1)
    up = jnp.concatenate([add(up[:half], got_lo), up[half:]])
    down = jnp.concatenate([down[:half], add(down[half:], got_hi)])
    return own, up, down


def collect_near(parts, axis):
    own, up, down = parts
    return add(own, fetch(up, axis, -1), fetch(down, axis, 1))


def collect_small(parts, axis):
    return add(parts[0], *[fetch(parts[r], axis, -r) for r in (1, 2, 3)])


def ranks(named):
    tok = named.shape[-1]
    earlier = jnp.arange(tok)[:, None] < jnp.arange(tok)[None, :]
    count = jnp.dot(named.astype(BF), earlier.astype(BF), preferred_element_type=F32)
    return jnp.where(named > 0, count, -1.0)


def body(tokens, routes, gates, cotangent, w_gate, w_up, w_down):
    y, c, z, x = (lax.axis_index(a) for a in ("y", "c", "z", "x"))
    ids = jnp.stack([y, z, c, x]).astype(jnp.int32)
    n_exp = w_gate.shape[0]
    total_exp = n_exp * 32
    tok, width = tokens.shape

    cot = [cotangent] + [fetch(cotangent, "x", r) for r in (1, 2, 3)]

    routes_t = routes.T
    experts_all = jnp.arange(total_exp, dtype=jnp.int32)
    named = jnp.sum((routes_t[:, None, :] == experts_all[None, :, None]).astype(F32), axis=0)
    place = ranks(named).astype(BF)
    slots = total_exp * CAP
    slot = jnp.arange(slots, dtype=jnp.int32)
    repeat = (slot[:, None] // CAP == experts_all[None, :]).astype(BF)
    place_rep = jnp.dot(repeat, place, preferred_element_type=F32)
    own_map = (place_rep == (slot % CAP).astype(F32)[:, None]).astype(BF)

    pair = n_exp // 2
    by_expert = own_map.reshape(-1, n_exp, CAP, tok)
    half_maps = [by_expert[:, p * pair : (p + 1) * pair].reshape(-1, tok) for p in range(2)]
    send = [jnp.dot(m, tokens, preferred_element_type=F32).astype(BF) for m in half_maps]

    def exchange(a):
        return lax.all_to_all(a, GROUP, split_axis=0, concat_axis=0, tiled=True)

    def gather_rows(came):
        came = came.reshape(4, 2, 4, pair, CAP, width).transpose(3, 1, 0, 2, 4, 5)
        return lax.all_gather(came.reshape(pair, 2, 16 * CAP, width), "x")

    cot[1], cot[2], cot[3], send[0] = lax.optimization_barrier((cot[1], cot[2], cot[3], send[0]))
    came_a = exchange(send[0])

    meta = jnp.concatenate([routes_t.astype(BF), gates.T], axis=0)
    meta = jnp.pad(meta, ((0, 0), (0, width - tok)))
    h1 = jnp.concatenate([cot[0], cot[1], meta])
    h2 = jnp.stack(cot[2:])
    near_z, near_y = spread_small(h1, "z"), spread_small(h2, "y")
    near_z, send[1] = lax.optimization_barrier((near_z, send[1]))
    came_b = exchange(send[1])
    came_a, near_z, near_y = lax.optimization_barrier((came_a, near_z, near_y))
    x_a = gather_rows(came_a)
    y_up, y_down = fetch(near_z, "y", 1), fetch(near_z, "y", -1)
    z_up, z_down = fetch(near_y, "z", 1), fetch(near_y, "z", -1)
    came_b, y_up, y_down, z_up, z_down = lax.optimization_barrier(
        (came_b, y_up, y_down, z_up, z_down)
    )
    x_b = gather_rows(came_b)
    tok_y = (near_z, y_up, fetch(y_up[:2], "y", 1), fetch(y_down[2:], "y", -1), y_down)
    tok_z = (near_y, z_up, fetch(z_up[:2], "z", 1), fetch(z_down[2:], "z", -1), z_down)

    half = jax.ShapeDtypeStruct((n_exp, 16 * CAP, 2 * width), BF)
    maps = jax.ShapeDtypeStruct((4, 2 * n_exp * 4 * CAP, 4 * tok), BF)
    go1, gs1, maps = pick(pick_yfirst_kernel, ids, tok_y, n_exp, (half, half, maps))
    go2, gs2 = pick(pick_zfirst_kernel, ids, (maps,) + tok_z, n_exp, (half, half))
    g_blocks = (go1, go2, fetch(gs1, "c", 1), fetch(gs2, "c", 1))

    weights = (w_gate, w_up, w_down)
    res_a = experts(ids, 0, x_a, g_blocks, weights, ())
    sib_a = [fetch(res_a[i], "c", 1) for i in (2, 3)]
    res_b = experts(ids, 1, x_b, g_blocks, weights, res_a[5:])
    grads = res_b[5:]
    sib_b = [fetch(res_b[i], "c", 1) for i in (2, 3)]

    sums_y = sum_tokens(sum_yfirst_kernel, ids, maps, (res_a[0], res_b[0], sib_a[0], sib_b[0]))
    sums_z = sum_tokens(sum_zfirst_kernel, ids, maps, (res_a[1], res_b[1], sib_a[1], sib_b[1]))
    def scatter_rows(back):
        back = lax.psum_scatter(back.reshape(-1, width), "x", scatter_dimension=0, tiled=True)
        back = back.reshape(pair, 2, 4, 4, CAP, width).transpose(2, 1, 3, 0, 4, 5)
        return back.reshape(-1, width)

    back_a, back_b = scatter_rows(res_a[4]), scatter_rows(res_b[4])
    ends_y, ends_z = collect_far(sums_y, "y"), collect_far(sums_z, "z")
    back_a, ends_y, ends_z = lax.optimization_barrier((back_a, ends_y, ends_z))
    back_a = exchange(back_a)
    part1, part2 = collect_near(ends_y, "y"), collect_near(ends_z, "z")
    back_b, part1, part2 = lax.optimization_barrier((back_b, part1, part2))
    back_b = exchange(back_b)
    grad_tokens = (tn(half_maps[0], back_a) + tn(half_maps[1], back_b)).astype(BF)

    part1, part2 = collect_small(part1, "z"), collect_small(part2, "y")
    mixed = collect_small((part1[0], part1[1], part2[0], part2[1]), "x")
    return (mixed, grad_tokens) + tuple(grads)


def solution(mesh):
    split = Mesh(mesh.devices.reshape(4, 2, 4, 4), ("y", "c", "z", "x"))
    acts = P(GROUP, "x")
    rows = P(GROUP, None)
    wts = P(GROUP, "x", None)
    return jax.shard_map(
        body,
        mesh=split,
        in_specs=(acts, rows, rows, acts, wts, wts, wts),
        out_specs=(acts, acts, wts, wts, wts),
        check_vma=False,
    )
```

```python
import functools

import jax
import jax.numpy as jnp
from jax import lax
from jax.experimental import pallas as pl
from jax.experimental.pallas import tpu as pltpu
from jax.sharding import Mesh
from jax.sharding import PartitionSpec as P

BF = jnp.bfloat16
F32 = jnp.float32
CAP = 12
GROUP = ("y", "c", "z")
VMEM_LIMIT = 52 * 1024 * 1024


def fetch(a, axis, r):
    n = lax.axis_size(axis)
    return lax.ppermute(a, axis, [((i + r) % n, i) for i in range(n)])


def add(*terms):
    total = terms[0].astype(F32)
    for term in terms[1:]:
        total = total + term.astype(F32)
    return total.astype(BF)


def nt(a, b):
    return lax.dot_general(a, b, (((1,), (1,)), ((), ())), preferred_element_type=F32)


def tn(a, b):
    return lax.dot_general(a, b, (((0,), (0,)), ((), ())), preferred_element_type=F32)


def nn(a, b):
    return jnp.dot(a, b, preferred_element_type=F32)


def slot_map(ids_ref, meta, n_exp):
    tok = meta[0].shape[1]
    y, z, c = ids_ref[0], ids_ref[1], ids_ref[2]
    top = meta[0].shape[0] // 2
    both = 2 * n_exp
    line = lax.broadcasted_iota(jnp.int32, (both, tok), 0)
    core = jnp.where(line < n_exp, c, 1 - c)
    expert = (y * 2 + core) * 4 + z
    expert = (expert * n_exp + lax.rem(line, n_exp)).astype(F32)
    earlier = (
        lax.broadcasted_iota(jnp.int32, (tok, tok), 0) < lax.broadcasted_iota(jnp.int32, (tok, tok), 1)
    ).astype(BF)
    widen = (
        lax.broadcasted_iota(jnp.int32, (both * 4, both), 0) // 4
        == lax.broadcasted_iota(jnp.int32, (both * 4, both), 1)
    ).astype(BF)
    owner = lax.rem(lax.broadcasted_iota(jnp.int32, (both * 4, tok), 0), 4)
    slots = both * 4 * CAP
    repeat = (
        lax.broadcasted_iota(jnp.int32, (slots, both * 4), 0) // CAP
        == lax.broadcasted_iota(jnp.int32, (slots, both * 4), 1)
    ).astype(BF)
    slot = lax.rem(lax.broadcasted_iota(jnp.int32, (slots, tok), 0), CAP).astype(F32)
    columns = []
    for zz in range(4):
        data = meta[zz].astype(F32)
        named = jnp.zeros((both, tok), F32)
        gate = jnp.zeros((both, tok), F32)
        for k in range(top):
            same = data[k : k + 1] == expert
            named = jnp.where(same, 1.0, named)
            gate = jnp.where(same, data[top + k : top + k + 1], gate)
        rank = jnp.where(named > 0, nn(named.astype(BF), earlier), -1.0)
        here = owner == zz
        rank = jnp.where(here, nn(widen, rank.astype(BF)), -1.0).astype(BF)
        gate = nn(widen, gate.astype(BF)).astype(BF)
        columns.append(jnp.where(nn(repeat, rank) == slot, nn(repeat, gate), 0.0).astype(BF))
    return jnp.concatenate(columns, axis=1)


def pick_kernel(ids_ref, whole_ref, own_ref, sib_ref, maps_ref):
    n_exp, span = own_ref.shape[:2]
    tok, width = 128, whole_ref.shape[2]
    n = own_ref.shape[2] // width
    slots = slot_map(ids_ref, [whole_ref[z, n * tok :, :tok] for z in range(4)], n_exp)
    maps_ref[0] = slots
    for r in range(n):
        block = jnp.concatenate([whole_ref[z, r * tok : (r + 1) * tok] for z in range(4)], axis=0)
        picked = nn(slots, block).astype(BF)
        cols = slice(r * width, (r + 1) * width)
        for e in range(n_exp):
            own_ref[e, :, cols] = picked[e * span : (e + 1) * span]
            lo = (n_exp + e) * span
            sib_ref[e, :, cols] = picked[lo : lo + span]


def pick(ids, whole, n_exp):
    width = whole.shape[2]
    span = 4 * CAP
    rows = jax.ShapeDtypeStruct((n_exp, 4 * span, 4 * width), BF)
    maps = jax.ShapeDtypeStruct((4, 2 * n_exp * span, 4 * 128), BF)
    rows_spec = pl.BlockSpec((n_exp, span, 4 * width), lambda i: (0, i, 0))
    return pl.pallas_call(
        pick_kernel,
        grid=(4,),
        out_shape=(rows, rows, maps),
        in_specs=[
            pl.BlockSpec(memory_space=pltpu.SMEM),
            pl.BlockSpec((4,) + whole.shape[1:], lambda i: (i, 0, 0)),
        ],
        out_specs=(rows_spec, rows_spec, pl.BlockSpec((1,) + maps.shape[1:], lambda i: (i, 0, 0))),
        compiler_params=pltpu.CompilerParams(vmem_limit_bytes=VMEM_LIMIT),
        cost_estimate=pl.CostEstimate(flops=4 << 30, bytes_accessed=18 << 20, transcendentals=0),
    )(ids, whole)


def sum_kernel(ids_ref, map_ref, own_ref, sib_ref, *outs):
    by_y, by_z = outs[:5], outs[5:]
    yr = pl.program_id(0)
    z = ids_ref[1]
    n_exp = own_ref.shape[0]
    tok, width = 128, own_ref.shape[2] // 4
    rows = jnp.concatenate(
        [ref[e] for ref in (own_ref, sib_ref) for e in range(n_exp)], axis=0
    )
    for zr in range(4):
        there = pl.multiple_of(lax.rem(z + zr, 4) * tok, tok)
        total = tn(map_ref[0, :, pl.ds(there, tok)], rows).astype(BF)
        cut = [total[:, r * width : (r + 1) * width] for r in range(4)]
        y_dest = (by_y[0], by_y[1], by_y[2 + zr // 2], by_y[4])
        for i in range(4):

            @pl.when(yr == i)
            def _(i=i):
                at = zr % 2 if i == 2 else zr
                y_dest[i][at, 0], y_dest[i][at, 1] = cut[0], cut[1]

        if zr == 2:
            for part in range(2):

                @pl.when(yr // 2 == part)
                def _(part=part):
                    at = yr - 2 * part
                    by_z[2 + part][at, 0], by_z[2 + part][at, 1] = cut[2], cut[3]

        else:
            ref = by_z[(0, 1, None, 4)[zr]]
            ref[yr, 0], ref[yr, 1] = cut[2], cut[3]


def sum_tokens(ids, maps, own, sib):
    n_exp, rows, cols = own.shape
    whole = jax.ShapeDtypeStruct((4, 2, 128, cols // 4), BF)
    half = jax.ShapeDtypeStruct((2,) + whole.shape[1:], BF)
    outs = (whole, whole, half, half, whole) * 2
    at = lambda i, ids: lax.rem(ids[0] + i, 4)
    rows_spec = pl.BlockSpec((n_exp, rows // 4, cols), lambda i, ids: (0, at(i, ids), 0))
    keep = lambda a: pl.BlockSpec(a.shape, lambda i, ids: (0,) * 4)
    return pl.pallas_call(
        sum_kernel,
        grid_spec=pltpu.PrefetchScalarGridSpec(
            num_scalar_prefetch=1,
            grid=(4,),
            in_specs=[
                pl.BlockSpec((1,) + maps.shape[1:], lambda i, ids: (at(i, ids), 0, 0)),
                rows_spec,
                rows_spec,
            ],
            out_specs=tuple(keep(a) for a in outs),
        ),
        out_shape=outs,
        compiler_params=pltpu.CompilerParams(vmem_limit_bytes=VMEM_LIMIT),
        cost_estimate=pl.CostEstimate(flops=4 << 30, bytes_accessed=16 << 20, transcendentals=0),
    )(ids, maps, own, sib)


def moved_columns(me, n, width):
    return [pl.ds(pl.multiple_of(lax.rem(me + r, n) * width, width), width) for r in range(n)]


def x_rows_of(c, refs):
    x0, x1, lo, hi, x3 = refs
    both = lambda ref: jnp.concatenate([ref[0, c], ref[0, 1 - c]], axis=0)
    far = jnp.where(pl.program_id(0) < 2, both(lo), both(hi))
    return [both(x0), both(x1), far, both(x3)]


def forward_kernel(ids_ref, *refs):
    x_refs, refs = refs[:5], refs[5:]
    own, sib, wg, wu, wd, oo, os, hid_ref, da_ref, db_ref = refs
    half, cols = own.shape[1:]
    n, width = 4, cols // 4
    fixed = [slice(r * width, (r + 1) * width) for r in range(n)]
    moved = moved_columns(ids_ref[3], n, width)
    x_rows = x_rows_of(ids_ref[2], x_refs)
    g_rows = [jnp.concatenate([own[0, :, f], sib[0, :, f]], axis=0) for f in fixed]
    a = sum(nt(x_rows[r], wg[0, :, moved[r]]) for r in range(n))
    b = sum(nt(x_rows[r], wu[0, :, moved[r]]) for r in range(n))
    gh = sum(nt(g_rows[r], wd[0, :, moved[r]]) for r in range(n))
    s = jax.nn.sigmoid(a)
    act = a * s
    hidden = (act * b).astype(BF)
    hid_ref[0] = hidden
    da_ref[0] = (gh * b * s * (1.0 + a * (1.0 - s))).astype(BF)
    db_ref[0] = (gh * act).astype(BF)
    for r in range(n):
        out = nn(hidden, wd[0, :, moved[r]]).astype(BF)
        oo[0, :, fixed[r]] = out[:half]
        os[0, :, fixed[r]] = out[half:]


def back_kernel(ids_ref, da_ref, db_ref, wg, wu, back_ref):
    c = ids_ref[2]
    n = back_ref.shape[0]
    half, width = back_ref.shape[3:]
    da, db = da_ref[0], db_ref[0]
    for r in range(n):
        cols = slice(r * width, (r + 1) * width)
        back = (nn(da, wg[0, :, cols]) + nn(db, wu[0, :, cols])).astype(BF)
        back_ref[r, 0, c] = back[:half]
        back_ref[r, 0, 1 - c] = back[half:]


def weights_kernel(ids_ref, *refs):
    x_refs, refs = refs[:5], refs[5:]
    own, sib, hid_ref, da_ref, db_ref, dwg, dwu, dwd = refs
    cols = own.shape[2]
    n, width = 4, cols // 4
    fixed = [slice(r * width, (r + 1) * width) for r in range(n)]
    moved = moved_columns(ids_ref[3], n, width)
    x_rows = x_rows_of(ids_ref[2], x_refs)
    hidden, da, db = hid_ref[0], da_ref[0], db_ref[0]
    for r in range(n):
        g_rows = jnp.concatenate([own[0, :, fixed[r]], sib[0, :, fixed[r]]], axis=0)
        dwg[0, :, moved[r]] = tn(da, x_rows[r]).astype(BF)
        dwu[0, :, moved[r]] = tn(db, x_rows[r]).astype(BF)
        dwd[0, :, moved[r]] = tn(hidden, g_rows).astype(BF)


def each(a):
    return pl.BlockSpec((1,) + a.shape[1:], lambda i: (i,) + (0,) * (a.ndim - 1))


def each_x(blocks):
    specs = [each(a) for a in blocks]
    lo, hi = blocks[2], blocks[3]
    specs[2] = pl.BlockSpec((1,) + lo.shape[1:], lambda i: (jnp.minimum(i, 1), 0, 0, 0))
    specs[3] = pl.BlockSpec((1,) + hi.shape[1:], lambda i: (jnp.maximum(i - 2, 0), 0, 0, 0))
    return specs


def per_expert(kernel, ids, in_specs, args, outs, out_specs, products, mebibytes):
    n_exp = 4
    return pl.pallas_call(
        kernel,
        grid=(n_exp,),
        out_shape=outs,
        in_specs=[pl.BlockSpec(memory_space=pltpu.SMEM)] + in_specs,
        out_specs=out_specs,
        compiler_params=pltpu.CompilerParams(vmem_limit_bytes=VMEM_LIMIT),
        cost_estimate=pl.CostEstimate(
            flops=products * (1536 * 192 * 2048 * 3), bytes_accessed=mebibytes << 20, transcendentals=0
        ),
    )(ids, *args)


def forward(ids, x, g, weights):
    n_exp, rows, _ = g[0].shape
    mid = jax.ShapeDtypeStruct((n_exp, 2 * rows, weights[0].shape[1]), BF)
    out = jax.ShapeDtypeStruct(g[0].shape, BF)
    outs = (out, out, mid, mid, mid)
    args = tuple(x) + tuple(g) + tuple(weights)
    specs = each_x(x) + [each(a) for a in tuple(g) + tuple(weights)]
    return per_expert(forward_kernel, ids, specs, args, outs, tuple(each(a) for a in outs), 4, 30)


def backward(ids, mids, weights, shape):
    back = jax.ShapeDtypeStruct((4,) + shape, BF)
    args = tuple(mids) + tuple(weights)
    spec = pl.BlockSpec((4, 1) + shape[1:], lambda i: (0, i, 0, 0, 0))
    return per_expert(back_kernel, ids, [each(a) for a in args], args, back, spec, 2, 14)


def weight_grads(ids, x, g, mids, like):
    outs = (jax.ShapeDtypeStruct(like.shape, BF),) * 3
    args = tuple(x) + tuple(g) + tuple(mids)
    specs = each_x(x) + [each(a) for a in tuple(g) + tuple(mids)]
    return per_expert(weights_kernel, ids, specs, args, outs, tuple(each(a) for a in outs), 3, 24)


def collect_far(parts, axis):
    own, up, far_lo, far_hi, down = parts
    half = far_lo.shape[0]
    got_lo, got_hi = fetch(far_lo, axis, -1), fetch(far_hi, axis, 1)
    up = jnp.concatenate([add(up[:half], got_lo), up[half:]])
    down = jnp.concatenate([down[:half], add(down[half:], got_hi)])
    return own, up, down


def collect_near(parts, axis):
    own, up, down = parts
    return add(own, fetch(up, axis, -1), fetch(down, axis, 1))


def collect_small(parts, axis):
    return add(parts[0], *[fetch(parts[r], axis, -r) for r in (1, 2, 3)])


def ranks(named):
    tok = named.shape[-1]
    earlier = jnp.arange(tok)[:, None] < jnp.arange(tok)[None, :]
    count = jnp.dot(named.astype(BF), earlier.astype(BF), preferred_element_type=F32)
    return jnp.where(named > 0, count, -1.0)


def body(tokens, routes, gates, cotangent, w_gate, w_up, w_down):
    y, c, z, x = (lax.axis_index(a) for a in ("y", "c", "z", "x"))
    ids = jnp.stack([y, z, c, x]).astype(jnp.int32)
    n_exp = w_gate.shape[0]
    total_exp = n_exp * 32
    tok, width = tokens.shape
    weights = (w_gate, w_up, w_down)

    cot = [cotangent] + [fetch(cotangent, "x", r) for r in (1, 2, 3)]
    routes_t = routes.T
    meta = jnp.concatenate([routes_t.astype(BF), gates.T], axis=0)
    meta = jnp.pad(meta, ((0, 0), (0, width - tok)))
    whole = lax.all_gather(jnp.concatenate(cot + [meta]), ("y", "z"))

    experts_all = jnp.arange(total_exp, dtype=jnp.int32)
    named = jnp.sum((routes_t[:, None, :] == experts_all[None, :, None]).astype(F32), axis=0)
    place = ranks(named).astype(BF)
    slots = total_exp * CAP
    slot = jnp.arange(slots, dtype=jnp.int32)
    repeat = (slot[:, None] // CAP == experts_all[None, :]).astype(BF)
    place_rep = jnp.dot(repeat, place, preferred_element_type=F32)
    own_map = (place_rep == (slot % CAP).astype(F32)[:, None]).astype(BF)

    def exchange(a):
        return lax.all_to_all(a, GROUP, split_axis=0, concat_axis=0, tiled=True)

    came = exchange(jnp.dot(own_map, tokens, preferred_element_type=F32).astype(BF))
    came = came.reshape(4, 2, 4, n_exp, CAP, width).transpose(3, 1, 0, 2, 4, 5)
    came = came.reshape(n_exp, 2, 16 * CAP, width)
    up, down = fetch(came, "x", 1), fetch(came, "x", -1)
    whole, up, down = lax.optimization_barrier((whole, up, down))
    pair = n_exp // 2
    x_blocks = (came, up, fetch(down[:pair], "x", -1), fetch(up[pair:], "x", 1), down)

    own, sib, maps = pick(ids, whole, n_exp)
    sib, far_lo, far_hi = lax.optimization_barrier((sib, x_blocks[2], x_blocks[3]))
    x_blocks = (came, up, far_lo, far_hi, down)
    g_blocks = (own, fetch(sib, "c", 1))
    out_own, out_sib, hidden, grad_a, grad_b = forward(ids, x_blocks, g_blocks, weights)
    out_sib = fetch(out_sib, "c", 1)
    back = backward(ids, (grad_a, grad_b), weights[:2], came.shape)
    back = lax.psum_scatter(back.reshape(-1, width), "x", scatter_dimension=0, tiled=True)

    sums = sum_tokens(ids, maps, out_own, out_sib)
    ends_y, ends_z = collect_far(sums[:5], "y"), collect_far(sums[5:], "z")
    hidden, ends_y, ends_z = lax.optimization_barrier((hidden, ends_y, ends_z))
    grads = weight_grads(ids, x_blocks, g_blocks, (hidden, grad_a, grad_b), w_gate)
    part1, part2 = collect_near(ends_y, "y"), collect_near(ends_z, "z")

    back = back.reshape(n_exp, 2, 4, 4, CAP, width).transpose(2, 1, 3, 0, 4, 5)
    back = back.reshape(slots, width)
    grads, back, part1, part2 = lax.optimization_barrier((grads, back, part1, part2))
    back = exchange(back)
    part1, part2 = collect_small(part1, "z"), collect_small(part2, "y")
    back, part1, part2 = lax.optimization_barrier((back, part1, part2))
    mixed = collect_small((part1[0], part1[1], part2[0], part2[1]), "x")
    grad_tokens = tn(own_map, back).astype(BF)
    return (mixed, grad_tokens) + tuple(grads)


def solution(mesh):
    split = Mesh(mesh.devices.reshape(4, 2, 4, 4), ("y", "c", "z", "x"))
    acts = P(GROUP, "x")
    rows = P(GROUP, None)
    wts = P(GROUP, "x", None)
    return jax.shard_map(
        body,
        mesh=split,
        in_specs=(acts, rows, rows, acts, wts, wts, wts),
        out_specs=(acts, acts, wts, wts, wts),
        check_vma=False,
    )
```

```python
import functools

import jax
import jax.numpy as jnp
from jax import lax
from jax.experimental import pallas as pl
from jax.experimental.pallas import tpu as pltpu
from jax.sharding import Mesh
from jax.sharding import PartitionSpec as P

BF = jnp.bfloat16
F32 = jnp.float32
CAP = 12
GROUP = ("y", "c", "z")
VMEM_LIMIT = 52 * 1024 * 1024


def fetch(a, axis, r):
    n = lax.axis_size(axis)
    return lax.ppermute(a, axis, [((i + r) % n, i) for i in range(n)])


def add(*terms):
    total = terms[0].astype(F32)
    for term in terms[1:]:
        total = total + term.astype(F32)
    return total.astype(BF)


def nt(a, b):
    return lax.dot_general(a, b, (((1,), (1,)), ((), ())), preferred_element_type=F32)


def tn(a, b):
    return lax.dot_general(a, b, (((0,), (0,)), ((), ())), preferred_element_type=F32)


def nn(a, b):
    return jnp.dot(a, b, preferred_element_type=F32)


def slot_map(ids_ref, meta, n_exp):
    tok = meta[0].shape[1]
    y, z, c = ids_ref[0], ids_ref[1], ids_ref[2]
    top = meta[0].shape[0] // 2
    both = 2 * n_exp
    line = lax.broadcasted_iota(jnp.int32, (both, tok), 0)
    core = jnp.where(line < n_exp, c, 1 - c)
    expert = (y * 2 + core) * 4 + z
    expert = (expert * n_exp + lax.rem(line, n_exp)).astype(F32)
    earlier = (
        lax.broadcasted_iota(jnp.int32, (tok, tok), 0) < lax.broadcasted_iota(jnp.int32, (tok, tok), 1)
    ).astype(BF)
    widen = (
        lax.broadcasted_iota(jnp.int32, (both * 4, both), 0) // 4
        == lax.broadcasted_iota(jnp.int32, (both * 4, both), 1)
    ).astype(BF)
    owner = lax.rem(lax.broadcasted_iota(jnp.int32, (both * 4, tok), 0), 4)
    slots = both * 4 * CAP
    repeat = (
        lax.broadcasted_iota(jnp.int32, (slots, both * 4), 0) // CAP
        == lax.broadcasted_iota(jnp.int32, (slots, both * 4), 1)
    ).astype(BF)
    slot = lax.rem(lax.broadcasted_iota(jnp.int32, (slots, tok), 0), CAP).astype(F32)
    columns = []
    for zz in range(4):
        data = meta[zz].astype(F32)
        named = jnp.zeros((both, tok), F32)
        gate = jnp.zeros((both, tok), F32)
        for k in range(top):
            same = data[k : k + 1] == expert
            named = jnp.where(same, 1.0, named)
            gate = jnp.where(same, data[top + k : top + k + 1], gate)
        rank = jnp.where(named > 0, nn(named.astype(BF), earlier), -1.0)
        here = owner == zz
        rank = jnp.where(here, nn(widen, rank.astype(BF)), -1.0).astype(BF)
        gate = nn(widen, gate.astype(BF)).astype(BF)
        columns.append(jnp.where(nn(repeat, rank) == slot, nn(repeat, gate), 0.0).astype(BF))
    return jnp.concatenate(columns, axis=1)


def pick_kernel(ids_ref, whole_ref, own_ref, sib_ref, maps_ref):
    n_exp, span = own_ref.shape[:2]
    tok, width = 128, whole_ref.shape[2]
    n = own_ref.shape[2] // width
    slots = slot_map(ids_ref, [whole_ref[z, n * tok :, :tok] for z in range(4)], n_exp)
    maps_ref[0] = slots
    for r in range(n):
        block = jnp.concatenate([whole_ref[z, r * tok : (r + 1) * tok] for z in range(4)], axis=0)
        picked = nn(slots, block).astype(BF)
        cols = slice(r * width, (r + 1) * width)
        for e in range(n_exp):
            own_ref[e, :, cols] = picked[e * span : (e + 1) * span]
            lo = (n_exp + e) * span
            sib_ref[e, :, cols] = picked[lo : lo + span]


def pick(ids, whole, n_exp):
    width = whole.shape[2]
    span = 4 * CAP
    rows = jax.ShapeDtypeStruct((n_exp, 4 * span, 4 * width), BF)
    maps = jax.ShapeDtypeStruct((4, 2 * n_exp * span, 4 * 128), BF)
    rows_spec = pl.BlockSpec((n_exp, span, 4 * width), lambda i: (0, i, 0))
    return pl.pallas_call(
        pick_kernel,
        grid=(4,),
        out_shape=(rows, rows, maps),
        in_specs=[
            pl.BlockSpec(memory_space=pltpu.SMEM),
            pl.BlockSpec((4,) + whole.shape[1:], lambda i: (i, 0, 0)),
        ],
        out_specs=(rows_spec, rows_spec, pl.BlockSpec((1,) + maps.shape[1:], lambda i: (i, 0, 0))),
        compiler_params=pltpu.CompilerParams(vmem_limit_bytes=VMEM_LIMIT),
        cost_estimate=pl.CostEstimate(flops=4 << 30, bytes_accessed=18 << 20, transcendentals=0),
    )(ids, whole)


def sum_kernel(ids_ref, map_ref, own_ref, sib_ref, *outs):
    by_y, by_z = outs[:5], outs[5:]
    yr = pl.program_id(0)
    z = ids_ref[1]
    n_exp = own_ref.shape[0]
    tok, width = 128, own_ref.shape[2] // 4
    there = [pl.multiple_of(lax.rem(z + zr, 4) * tok, tok) for zr in range(4)]
    gates = jnp.concatenate([map_ref[0, :, pl.ds(t, tok)] for t in there], axis=1)
    for r in range(4):
        cols = slice(r * width, (r + 1) * width)
        rows = [ref[e, :, cols] for ref in (own_ref, sib_ref) for e in range(n_exp)]
        total = tn(gates, jnp.concatenate(rows, axis=0)).astype(BF)
        for zr in range(4):
            block = total[zr * tok : (zr + 1) * tok]
            if r >= 2:
                if zr != 2:
                    by_z[(0, 1, None, 4)[zr]][0, r - 2] = block
                for part in range(2 if zr == 2 else 0):

                    @pl.when(yr // 2 == part)
                    def _(part=part, block=block):
                        by_z[2 + part][0, r - 2] = block

                continue
            dest = (by_y[0], by_y[1], by_y[2 + zr // 2], by_y[4])
            for i in range(4):

                @pl.when(yr == i)
                def _(i=i, block=block):
                    dest[i][zr % 2 if i == 2 else zr, r] = block


def sum_tokens(ids, maps, own, sib):
    n_exp, rows, cols = own.shape
    whole = jax.ShapeDtypeStruct((4, 2, 128, cols // 4), BF)
    half = jax.ShapeDtypeStruct((2,) + whole.shape[1:], BF)
    outs = (whole, whole, half, half, whole) * 2
    at = lambda i, ids: lax.rem(ids[0] + i, 4)
    rows_spec = pl.BlockSpec((n_exp, rows // 4, cols), lambda i, ids: (0, at(i, ids), 0))
    keep = lambda a: pl.BlockSpec(a.shape, lambda i, ids: (0,) * 4)
    block = (1,) + whole.shape[1:]
    each_y = pl.BlockSpec(block, lambda i, ids: (i, 0, 0, 0))
    first = pl.BlockSpec(block, lambda i, ids: (jnp.minimum(i, 1), 0, 0, 0))
    last = pl.BlockSpec(block, lambda i, ids: (jnp.maximum(i - 2, 0), 0, 0, 0))
    return pl.pallas_call(
        sum_kernel,
        grid_spec=pltpu.PrefetchScalarGridSpec(
            num_scalar_prefetch=1,
            grid=(4,),
            in_specs=[
                pl.BlockSpec((1,) + maps.shape[1:], lambda i, ids: (at(i, ids), 0, 0)),
                rows_spec,
                rows_spec,
            ],
            out_specs=tuple(keep(a) for a in outs[:5]) + (each_y, each_y, first, last, each_y),
        ),
        out_shape=outs,
        compiler_params=pltpu.CompilerParams(vmem_limit_bytes=VMEM_LIMIT),
        cost_estimate=pl.CostEstimate(flops=4 << 30, bytes_accessed=16 << 20, transcendentals=0),
    )(ids, maps, own, sib)


def moved_columns(me, n, width):
    return [pl.ds(pl.multiple_of(lax.rem(me + r, n) * width, width), width) for r in range(n)]


def x_rows_of(c, refs):
    x0, x1, lo, hi, x3 = refs
    both = lambda ref: jnp.concatenate([ref[0, c], ref[0, 1 - c]], axis=0)
    far = jnp.where(pl.program_id(0) < 2, both(lo), both(hi))
    return [both(x0), both(x1), far, both(x3)]


def forward_kernel(ids_ref, *refs):
    x_refs, refs = refs[:5], refs[5:]
    wg, wu, wd, oo, os, hid_ref, slope_ref, act_ref = refs
    half, cols = oo.shape[1:]
    n, width = 4, cols // 4
    moved = moved_columns(ids_ref[3], n, width)
    x_rows = x_rows_of(ids_ref[2], x_refs)
    a = sum(nt(x_rows[r], wg[0, :, moved[r]]) for r in range(n))
    b = sum(nt(x_rows[r], wu[0, :, moved[r]]) for r in range(n))
    s = jax.nn.sigmoid(a)
    act = a * s
    hidden = (act * b).astype(BF)
    hid_ref[0] = hidden
    slope_ref[0] = b * s * (1.0 + a * (1.0 - s))
    act_ref[0] = act
    for r in range(n):
        out = nn(hidden, wd[0, :, moved[r]]).astype(BF)
        oo[0, :, r * width : (r + 1) * width] = out[:half]
        os[0, :, r * width : (r + 1) * width] = out[half:]


def back_kernel(ids_ref, own, sib, slope_ref, act_ref, wg, wu, wd, da_ref, db_ref, back_ref):
    c = ids_ref[2]
    n = back_ref.shape[0]
    half, width = back_ref.shape[3:]
    moved = moved_columns(ids_ref[3], n, width)
    fixed = [slice(r * width, (r + 1) * width) for r in range(n)]
    g_rows = [jnp.concatenate([own[0, :, f], sib[0, :, f]], axis=0) for f in fixed]
    gh = sum(nt(g_rows[r], wd[0, :, moved[r]]) for r in range(n))
    da = (gh * slope_ref[0]).astype(BF)
    db = (gh * act_ref[0]).astype(BF)
    da_ref[0] = da
    db_ref[0] = db
    for r in range(n):
        back = (nn(da, wg[0, :, fixed[r]]) + nn(db, wu[0, :, fixed[r]])).astype(BF)
        back_ref[r, 0, c] = back[:half]
        back_ref[r, 0, 1 - c] = back[half:]


def weights_kernel(ids_ref, *refs):
    x_refs, refs = refs[:5], refs[5:]
    own, sib, hid_ref, da_ref, db_ref, dwg, dwu, dwd = refs
    cols = own.shape[2]
    n, width = 4, cols // 4
    fixed = [slice(r * width, (r + 1) * width) for r in range(n)]
    moved = moved_columns(ids_ref[3], n, width)
    x_rows = x_rows_of(ids_ref[2], x_refs)
    hidden, da, db = hid_ref[0], da_ref[0], db_ref[0]
    for r in range(n):
        g_rows = jnp.concatenate([own[0, :, fixed[r]], sib[0, :, fixed[r]]], axis=0)
        dwg[0, :, moved[r]] = tn(da, x_rows[r]).astype(BF)
        dwu[0, :, moved[r]] = tn(db, x_rows[r]).astype(BF)
        dwd[0, :, moved[r]] = tn(hidden, g_rows).astype(BF)


def each(a):
    return pl.BlockSpec((1,) + a.shape[1:], lambda i: (i,) + (0,) * (a.ndim - 1))


def each_x(blocks):
    specs = [each(a) for a in blocks]
    lo, hi = blocks[2], blocks[3]
    specs[2] = pl.BlockSpec((1,) + lo.shape[1:], lambda i: (jnp.minimum(i, 1), 0, 0, 0))
    specs[3] = pl.BlockSpec((1,) + hi.shape[1:], lambda i: (jnp.maximum(i - 2, 0), 0, 0, 0))
    return specs


def per_expert(kernel, ids, in_specs, args, outs, out_specs, products, mebibytes):
    n_exp = 4
    return pl.pallas_call(
        kernel,
        grid=(n_exp,),
        out_shape=outs,
        in_specs=[pl.BlockSpec(memory_space=pltpu.SMEM)] + in_specs,
        out_specs=out_specs,
        compiler_params=pltpu.CompilerParams(vmem_limit_bytes=VMEM_LIMIT),
        cost_estimate=pl.CostEstimate(
            flops=products * (1536 * 192 * 2048 * 3), bytes_accessed=mebibytes << 20, transcendentals=0
        ),
    )(ids, *args)


def forward(ids, x, weights):
    n_exp, _, rows, width = x[0].shape
    mid = jax.ShapeDtypeStruct((n_exp, 2 * rows, weights[0].shape[1]), BF)
    wide = jax.ShapeDtypeStruct(mid.shape, F32)
    out = jax.ShapeDtypeStruct((n_exp, rows, 4 * width), BF)
    outs = (out, out, mid, wide, wide)
    args = tuple(x) + tuple(weights)
    specs = each_x(x) + [each(a) for a in weights]
    return per_expert(forward_kernel, ids, specs, args, outs, tuple(each(a) for a in outs), 3, 26)


def backward(ids, g, slope, act, weights, mid, shape):
    outs = (mid, mid, jax.ShapeDtypeStruct((4,) + shape, BF))
    args = tuple(g) + (slope, act) + tuple(weights)
    spec = pl.BlockSpec((4, 1) + shape[1:], lambda i: (0, i, 0, 0, 0))
    out_specs = (each(mid), each(mid), spec)
    return per_expert(back_kernel, ids, [each(a) for a in args], args, outs, out_specs, 3, 26)


def weight_grads(ids, x, g, mids, like):
    outs = (jax.ShapeDtypeStruct(like.shape, BF),) * 3
    args = tuple(x) + tuple(g) + tuple(mids)
    specs = each_x(x) + [each(a) for a in tuple(g) + tuple(mids)]
    return per_expert(weights_kernel, ids, specs, args, outs, tuple(each(a) for a in outs), 3, 24)


def collect_far(parts, axis):
    own, up, far_lo, far_hi, down = parts
    half = far_lo.shape[0]
    got_lo, got_hi = fetch(far_lo, axis, -1), fetch(far_hi, axis, 1)
    up = jnp.concatenate([add(up[:half], got_lo), up[half:]])
    down = jnp.concatenate([down[:half], add(down[half:], got_hi)])
    return own, up, down


def collect_near(parts, axis):
    own, up, down = parts
    return add(own, fetch(up, axis, -1), fetch(down, axis, 1))


def collect_small(parts, axis):
    return add(parts[0], *[fetch(parts[r], axis, -r) for r in (1, 2, 3)])


def ranks(named):
    tok = named.shape[-1]
    earlier = jnp.arange(tok)[:, None] < jnp.arange(tok)[None, :]
    count = jnp.dot(named.astype(BF), earlier.astype(BF), preferred_element_type=F32)
    return jnp.where(named > 0, count, -1.0)


def body(tokens, routes, gates, cotangent, w_gate, w_up, w_down):
    y, c, z, x = (lax.axis_index(a) for a in ("y", "c", "z", "x"))
    ids = jnp.stack([y, z, c, x]).astype(jnp.int32)
    n_exp = w_gate.shape[0]
    total_exp = n_exp * 32
    tok, width = tokens.shape
    weights = (w_gate, w_up, w_down)

    cot = [cotangent] + [fetch(cotangent, "x", r) for r in (1, 2, 3)]
    routes_t = routes.T
    experts_all = jnp.arange(total_exp, dtype=jnp.int32)
    named = jnp.sum((routes_t[:, None, :] == experts_all[None, :, None]).astype(F32), axis=0)
    place = ranks(named).astype(BF)
    slots = total_exp * CAP
    slot = jnp.arange(slots, dtype=jnp.int32)
    repeat = (slot[:, None] // CAP == experts_all[None, :]).astype(BF)
    place_rep = jnp.dot(repeat, place, preferred_element_type=F32)
    own_map = (place_rep == (slot % CAP).astype(F32)[:, None]).astype(BF)

    def exchange(a):
        return lax.all_to_all(a, GROUP, split_axis=0, concat_axis=0, tiled=True)

    came = exchange(jnp.dot(own_map, tokens, preferred_element_type=F32).astype(BF))

    meta = jnp.concatenate([routes_t.astype(BF), gates.T], axis=0)
    meta = jnp.pad(meta, ((0, 0), (0, width - tok)))
    whole = jnp.concatenate(cot + [meta])
    came, whole = lax.optimization_barrier((came, whole))
    whole = lax.all_gather(whole, ("y", "z"))

    came = came.reshape(4, 2, 4, n_exp, CAP, width).transpose(3, 1, 0, 2, 4, 5)
    came = came.reshape(n_exp, 2, 16 * CAP, width)
    up, down = fetch(came, "x", 1), fetch(came, "x", -1)
    pair = n_exp // 2
    x_blocks = (came, up, fetch(down[:pair], "x", -1), fetch(up[pair:], "x", 1), down)
    out_own, out_sib, hidden, slope, act = forward(ids, x_blocks, weights)

    whole, out_sib = lax.optimization_barrier((whole, out_sib))
    own, sib, maps = pick(ids, whole, n_exp)
    sib, out_sib = lax.optimization_barrier((sib, fetch(out_sib, "c", 1)))

    sums = sum_tokens(ids, maps, out_own, out_sib)
    sib, sums = lax.optimization_barrier((fetch(sib, "c", 1), sums))
    ends_y, ends_z = collect_far(sums[:5], "y"), collect_far(sums[5:], "z")
    g_blocks = (own, sib)
    mid = jax.ShapeDtypeStruct(hidden.shape, BF)
    grad_a, grad_b, back = backward(ids, g_blocks, slope, act, weights, mid, came.shape)
    back = lax.psum_scatter(back.reshape(-1, width), "x", scatter_dimension=0, tiled=True)
    grad_a, ends_y, ends_z = lax.optimization_barrier((grad_a, ends_y, ends_z))
    grads = weight_grads(ids, x_blocks, g_blocks, (hidden, grad_a, grad_b), w_gate)
    part1, part2 = collect_near(ends_y, "y"), collect_near(ends_z, "z")
    grads, part1, part2 = lax.optimization_barrier((grads, part1, part2))
    part1, part2 = collect_small(part1, "z"), collect_small(part2, "y")
    mixed = collect_small((part1[0], part1[1], part2[0], part2[1]), "x")

    back = back.reshape(n_exp, 2, 4, 4, CAP, width).transpose(2, 1, 3, 0, 4, 5)
    back = exchange(back.reshape(slots, width))
    grad_tokens = tn(own_map, back).astype(BF)
    return (mixed, grad_tokens) + tuple(grads)


def solution(mesh):
    split = Mesh(mesh.devices.reshape(4, 2, 4, 4), ("y", "c", "z", "x"))
    acts = P(GROUP, "x")
    rows = P(GROUP, None)
    wts = P(GROUP, "x", None)
    return jax.shard_map(
        body,
        mesh=split,
        in_specs=(acts, rows, rows, acts, wts, wts, wts),
        out_specs=(acts, acts, wts, wts, wts),
        check_vma=False,
    )
```

```python
import functools

import jax
import jax.numpy as jnp
from jax import lax
from jax.experimental import pallas as pl
from jax.experimental.pallas import tpu as pltpu
from jax.sharding import Mesh
from jax.sharding import PartitionSpec as P

BF = jnp.bfloat16
F32 = jnp.float32
CAP = 12
GROUP = ("y", "c", "z")
VMEM_LIMIT = 52 * 1024 * 1024


def fetch(a, axis, r):
    n = lax.axis_size(axis)
    return lax.ppermute(a, axis, [((i + r) % n, i) for i in range(n)])


def add(*terms):
    total = terms[0].astype(F32)
    for term in terms[1:]:
        total = total + term.astype(F32)
    return total.astype(BF)


def nt(a, b):
    return lax.dot_general(a, b, (((1,), (1,)), ((), ())), preferred_element_type=F32)


def tn(a, b):
    return lax.dot_general(a, b, (((0,), (0,)), ((), ())), preferred_element_type=F32)


def nn(a, b):
    return jnp.dot(a, b, preferred_element_type=F32)


def slot_map(ids_ref, meta, n_exp):
    tok = meta[0].shape[1]
    y, z, c = ids_ref[0], ids_ref[1], ids_ref[2]
    top = meta[0].shape[0] // 2
    both = 2 * n_exp
    line = lax.broadcasted_iota(jnp.int32, (both, tok), 0)
    core = jnp.where(line < n_exp, c, 1 - c)
    expert = (y * 2 + core) * 4 + z
    expert = (expert * n_exp + lax.rem(line, n_exp)).astype(F32)
    earlier = (
        lax.broadcasted_iota(jnp.int32, (tok, tok), 0) < lax.broadcasted_iota(jnp.int32, (tok, tok), 1)
    ).astype(BF)
    widen = (
        lax.broadcasted_iota(jnp.int32, (both * 4, both), 0) // 4
        == lax.broadcasted_iota(jnp.int32, (both * 4, both), 1)
    ).astype(BF)
    owner = lax.rem(lax.broadcasted_iota(jnp.int32, (both * 4, tok), 0), 4)
    slots = both * 4 * CAP
    repeat = (
        lax.broadcasted_iota(jnp.int32, (slots, both * 4), 0) // CAP
        == lax.broadcasted_iota(jnp.int32, (slots, both * 4), 1)
    ).astype(BF)
    slot = lax.rem(lax.broadcasted_iota(jnp.int32, (slots, tok), 0), CAP).astype(F32)
    columns = []
    for zz in range(4):
        data = meta[zz].astype(F32)
        named = jnp.zeros((both, tok), F32)
        gate = jnp.zeros((both, tok), F32)
        for k in range(top):
            same = data[k : k + 1] == expert
            named = jnp.where(same, 1.0, named)
            gate = jnp.where(same, data[top + k : top + k + 1], gate)
        rank = jnp.where(named > 0, nn(named.astype(BF), earlier), -1.0)
        here = owner == zz
        rank = jnp.where(here, nn(widen, rank.astype(BF)), -1.0).astype(BF)
        gate = nn(widen, gate.astype(BF)).astype(BF)
        columns.append(jnp.where(nn(repeat, rank) == slot, nn(repeat, gate), 0.0).astype(BF))
    return jnp.concatenate(columns, axis=1)


def pick_kernel(ids_ref, whole_ref, own_ref, sib_ref, maps_ref):
    n_exp, span = own_ref.shape[:2]
    tok, width = 128, whole_ref.shape[2]
    n = own_ref.shape[2] // width
    slots = slot_map(ids_ref, [whole_ref[z, n * tok :, :tok] for z in range(4)], n_exp)
    maps_ref[0] = slots
    for r in range(n):
        block = jnp.concatenate([whole_ref[z, r * tok : (r + 1) * tok] for z in range(4)], axis=0)
        picked = nn(slots, block).astype(BF)
        cols = slice(r * width, (r + 1) * width)
        for e in range(n_exp):
            own_ref[e, :, cols] = picked[e * span : (e + 1) * span]
            lo = (n_exp + e) * span
            sib_ref[e, :, cols] = picked[lo : lo + span]


def pick(ids, whole, n_exp):
    width = whole.shape[2]
    span = 4 * CAP
    rows = jax.ShapeDtypeStruct((n_exp, 4 * span, 4 * width), BF)
    maps = jax.ShapeDtypeStruct((4, 2 * n_exp * span, 4 * 128), BF)
    rows_spec = pl.BlockSpec((n_exp, span, 4 * width), lambda i: (0, i, 0))
    return pl.pallas_call(
        pick_kernel,
        grid=(4,),
        out_shape=(rows, rows, maps),
        in_specs=[
            pl.BlockSpec(memory_space=pltpu.SMEM),
            pl.BlockSpec((4,) + whole.shape[1:], lambda i: (i, 0, 0)),
        ],
        out_specs=(rows_spec, rows_spec, pl.BlockSpec((1,) + maps.shape[1:], lambda i: (i, 0, 0))),
        compiler_params=pltpu.CompilerParams(vmem_limit_bytes=VMEM_LIMIT),
        cost_estimate=pl.CostEstimate(flops=4 << 30, bytes_accessed=18 << 20, transcendentals=0),
    )(ids, whole)


def sum_kernel(ids_ref, map_ref, own_ref, sib_ref, *outs):
    by_y, by_z = outs[:5], outs[5:]
    yr = pl.program_id(0)
    z = ids_ref[1]
    n_exp = own_ref.shape[0]
    tok, width = 128, own_ref.shape[2] // 4
    there = [pl.multiple_of(lax.rem(z + zr, 4) * tok, tok) for zr in range(4)]
    gates = jnp.concatenate([map_ref[0, :, pl.ds(t, tok)] for t in there], axis=1)
    for r in range(4):
        cols = slice(r * width, (r + 1) * width)
        rows = [ref[e, :, cols] for ref in (own_ref, sib_ref) for e in range(n_exp)]
        total = tn(gates, jnp.concatenate(rows, axis=0)).astype(BF)
        for zr in range(4):
            block = total[zr * tok : (zr + 1) * tok]
            if r >= 2:
                if zr != 2:
                    by_z[(0, 1, None, 4)[zr]][0, r - 2] = block
                for part in range(2 if zr == 2 else 0):

                    @pl.when(yr // 2 == part)
                    def _(part=part, block=block):
                        by_z[2 + part][0, r - 2] = block

                continue
            dest = (by_y[0], by_y[1], by_y[2 + zr // 2], by_y[4])
            for i in range(4):

                @pl.when(yr == i)
                def _(i=i, block=block):
                    dest[i][zr % 2 if i == 2 else zr, r] = block


def sum_tokens(ids, maps, own, sib):
    n_exp, rows, cols = own.shape
    whole = jax.ShapeDtypeStruct((4, 2, 128, cols // 4), BF)
    half = jax.ShapeDtypeStruct((2,) + whole.shape[1:], BF)
    outs = (whole, whole, half, half, whole) * 2
    at = lambda i, ids: lax.rem(ids[0] + i, 4)
    rows_spec = pl.BlockSpec((n_exp, rows // 4, cols), lambda i, ids: (0, at(i, ids), 0))
    keep = lambda a: pl.BlockSpec(a.shape, lambda i, ids: (0,) * 4)
    block = (1,) + whole.shape[1:]
    each_y = pl.BlockSpec(block, lambda i, ids: (i, 0, 0, 0))
    first = pl.BlockSpec(block, lambda i, ids: (jnp.minimum(i, 1), 0, 0, 0))
    last = pl.BlockSpec(block, lambda i, ids: (jnp.maximum(i - 2, 0), 0, 0, 0))
    return pl.pallas_call(
        sum_kernel,
        grid_spec=pltpu.PrefetchScalarGridSpec(
            num_scalar_prefetch=1,
            grid=(4,),
            in_specs=[
                pl.BlockSpec((1,) + maps.shape[1:], lambda i, ids: (at(i, ids), 0, 0)),
                rows_spec,
                rows_spec,
            ],
            out_specs=tuple(keep(a) for a in outs[:5]) + (each_y, each_y, first, last, each_y),
        ),
        out_shape=outs,
        compiler_params=pltpu.CompilerParams(vmem_limit_bytes=VMEM_LIMIT),
        cost_estimate=pl.CostEstimate(flops=4 << 30, bytes_accessed=16 << 20, transcendentals=0),
    )(ids, maps, own, sib)


def moved_columns(me, n, width):
    return [pl.ds(pl.multiple_of(lax.rem(me + r, n) * width, width), width) for r in range(n)]


def x_rows_of(c, refs):
    x0, x1, lo, hi, x3 = refs
    both = lambda ref: jnp.concatenate([ref[0, c], ref[0, 1 - c]], axis=0)
    far = jnp.where(pl.program_id(0) < 2, both(lo), both(hi))
    return [both(x0), both(x1), far, both(x3)]


def forward_kernel(ids_ref, *refs):
    x_refs, refs = refs[:5], refs[5:]
    wg, wu, wd, oo, os, hid_ref, slope_ref, act_ref = refs
    half, cols = oo.shape[1:]
    n, width = 4, cols // 4
    moved = moved_columns(ids_ref[3], n, width)
    x_rows = x_rows_of(ids_ref[2], x_refs)
    a = sum(nt(x_rows[r], wg[0, :, moved[r]]) for r in range(n))
    b = sum(nt(x_rows[r], wu[0, :, moved[r]]) for r in range(n))
    s = jax.nn.sigmoid(a)
    act = a * s
    hidden = (act * b).astype(BF)
    hid_ref[0] = hidden
    slope_ref[0] = b * s * (1.0 + a * (1.0 - s))
    act_ref[0] = act
    for r in range(n):
        out = nn(hidden, wd[0, :, moved[r]]).astype(BF)
        oo[0, :, r * width : (r + 1) * width] = out[:half]
        os[0, :, r * width : (r + 1) * width] = out[half:]


def back_kernel(ids_ref, own, sib, slope_ref, act_ref, wg, wu, wd, da_ref, db_ref, back_ref):
    c = ids_ref[2]
    n = back_ref.shape[0]
    half, width = back_ref.shape[3:]
    moved = moved_columns(ids_ref[3], n, width)
    fixed = [slice(r * width, (r + 1) * width) for r in range(n)]
    g_rows = [jnp.concatenate([own[0, :, f], sib[0, :, f]], axis=0) for f in fixed]
    gh = sum(nt(g_rows[r], wd[0, :, moved[r]]) for r in range(n))
    da = (gh * slope_ref[0]).astype(BF)
    db = (gh * act_ref[0]).astype(BF)
    da_ref[0] = da
    db_ref[0] = db
    for r in range(n):
        back = (nn(da, wg[0, :, fixed[r]]) + nn(db, wu[0, :, fixed[r]])).astype(BF)
        back_ref[r, 0, c] = back[:half]
        back_ref[r, 0, 1 - c] = back[half:]


def weights_kernel(ids_ref, *refs):
    x_refs, refs = refs[:5], refs[5:]
    own, sib, hid_ref, da_ref, db_ref, dwg, dwu, dwd = refs
    cols = own.shape[2]
    n, width = 4, cols // 4
    fixed = [slice(r * width, (r + 1) * width) for r in range(n)]
    moved = moved_columns(ids_ref[3], n, width)
    x_rows = x_rows_of(ids_ref[2], x_refs)
    hidden, da, db = hid_ref[0], da_ref[0], db_ref[0]
    for r in range(n):
        g_rows = jnp.concatenate([own[0, :, fixed[r]], sib[0, :, fixed[r]]], axis=0)
        dwg[0, :, moved[r]] = tn(da, x_rows[r]).astype(BF)
        dwu[0, :, moved[r]] = tn(db, x_rows[r]).astype(BF)
        dwd[0, :, moved[r]] = tn(hidden, g_rows).astype(BF)


def each(a):
    return pl.BlockSpec((1,) + a.shape[1:], lambda i: (i,) + (0,) * (a.ndim - 1))


def each_x(blocks):
    specs = [each(a) for a in blocks]
    lo, hi = blocks[2], blocks[3]
    specs[2] = pl.BlockSpec((1,) + lo.shape[1:], lambda i: (jnp.minimum(i, 1), 0, 0, 0))
    specs[3] = pl.BlockSpec((1,) + hi.shape[1:], lambda i: (jnp.maximum(i - 2, 0), 0, 0, 0))
    return specs


def per_expert(kernel, ids, in_specs, args, outs, out_specs, products, mebibytes):
    n_exp = 4
    return pl.pallas_call(
        kernel,
        grid=(n_exp,),
        out_shape=outs,
        in_specs=[pl.BlockSpec(memory_space=pltpu.SMEM)] + in_specs,
        out_specs=out_specs,
        compiler_params=pltpu.CompilerParams(vmem_limit_bytes=VMEM_LIMIT),
        cost_estimate=pl.CostEstimate(
            flops=products * (1536 * 192 * 2048 * 3), bytes_accessed=mebibytes << 20, transcendentals=0
        ),
    )(ids, *args)


def forward(ids, x, weights):
    n_exp, _, rows, width = x[0].shape
    mid = jax.ShapeDtypeStruct((n_exp, 2 * rows, weights[0].shape[1]), BF)
    wide = jax.ShapeDtypeStruct(mid.shape, F32)
    out = jax.ShapeDtypeStruct((n_exp, rows, 4 * width), BF)
    outs = (out, out, mid, wide, wide)
    args = tuple(x) + tuple(weights)
    specs = each_x(x) + [each(a) for a in weights]
    return per_expert(forward_kernel, ids, specs, args, outs, tuple(each(a) for a in outs), 3, 26)


def backward(ids, g, slope, act, weights, mid, shape):
    outs = (mid, mid, jax.ShapeDtypeStruct((4,) + shape, BF))
    args = tuple(g) + (slope, act) + tuple(weights)
    spec = pl.BlockSpec((4, 1) + shape[1:], lambda i: (0, i, 0, 0, 0))
    out_specs = (each(mid), each(mid), spec)
    return per_expert(back_kernel, ids, [each(a) for a in args], args, outs, out_specs, 3, 26)


def weight_grads(ids, x, g, mids, like):
    outs = (jax.ShapeDtypeStruct(like.shape, BF),) * 3
    args = tuple(x) + tuple(g) + tuple(mids)
    specs = each_x(x) + [each(a) for a in tuple(g) + tuple(mids)]
    return per_expert(weights_kernel, ids, specs, args, outs, tuple(each(a) for a in outs), 3, 24)


def regroup_matrix(span):
    n = 4 * span
    line = lax.broadcasted_iota(jnp.int32, (n, n), 0)
    col = lax.broadcasted_iota(jnp.int32, (n, n), 1)
    swapped = (lax.rem(line // CAP, 4) * 4 + line // span) * CAP + lax.rem(line, CAP)
    return (swapped == col).astype(BF)


def by_expert_kernel(rows_ref, out_ref):
    span = out_ref.shape[2]
    rows = nn(regroup_matrix(span), rows_ref[0]).astype(BF)
    for e in range(out_ref.shape[0]):
        out_ref[e, 0] = rows[e * span : (e + 1) * span]


def by_group_kernel(rows_ref, out_ref):
    span = rows_ref.shape[2]
    rows = jnp.concatenate([rows_ref[e, 0] for e in range(rows_ref.shape[0])], axis=0)
    out_ref[0] = tn(regroup_matrix(span), rows).astype(BF)


def regroup(rows, to_experts):
    width = rows.shape[-1]
    span = 4 * CAP
    flat = pl.BlockSpec((1, 4 * span, width), lambda i: (i, 0, 0))
    deep = pl.BlockSpec((4, 1, span, width), lambda i: (0, lax.rem(i, 2), i // 2, 0))
    cost = pl.CostEstimate(flops=2 * 1536 * 192 * width, bytes_accessed=3 << 20, transcendentals=0)
    if to_experts:
        shape = jax.ShapeDtypeStruct((4, 2, 4 * span, width), BF)
        return pl.pallas_call(
            by_expert_kernel, grid=(8,), out_shape=shape, in_specs=[flat], out_specs=deep,
            cost_estimate=cost,
        )(rows.reshape(8, 4 * span, width))
    shape = jax.ShapeDtypeStruct((8, 4 * span, width), BF)
    return pl.pallas_call(
        by_group_kernel, grid=(8,), out_shape=shape, in_specs=[deep], out_specs=flat,
        cost_estimate=cost,
    )(rows.reshape(4, 2, 4 * span, width)).reshape(-1, width)


def collect_far(parts, axis):
    own, up, far_lo, far_hi, down = parts
    half = far_lo.shape[0]
    got_lo, got_hi = fetch(far_lo, axis, -1), fetch(far_hi, axis, 1)
    up = jnp.concatenate([add(up[:half], got_lo), up[half:]])
    down = jnp.concatenate([down[:half], add(down[half:], got_hi)])
    return own, up, down


def collect_near(parts, axis):
    own, up, down = parts
    return add(own, fetch(up, axis, -1), fetch(down, axis, 1))


def collect_small(parts, axis):
    return add(parts[0], *[fetch(parts[r], axis, -r) for r in (1, 2, 3)])


def ranks(named):
    tok = named.shape[-1]
    earlier = jnp.arange(tok)[:, None] < jnp.arange(tok)[None, :]
    count = jnp.dot(named.astype(BF), earlier.astype(BF), preferred_element_type=F32)
    return jnp.where(named > 0, count, -1.0)


def body(tokens, routes, gates, cotangent, w_gate, w_up, w_down):
    y, c, z, x = (lax.axis_index(a) for a in ("y", "c", "z", "x"))
    ids = jnp.stack([y, z, c, x]).astype(jnp.int32)
    n_exp = w_gate.shape[0]
    total_exp = n_exp * 32
    tok, width = tokens.shape
    weights = (w_gate, w_up, w_down)

    routes_t = routes.T
    experts_all = jnp.arange(total_exp, dtype=jnp.int32)
    named = jnp.sum((routes_t[:, None, :] == experts_all[None, :, None]).astype(F32), axis=0)
    place = ranks(named).astype(BF)
    slots = total_exp * CAP
    slot = jnp.arange(slots, dtype=jnp.int32)
    repeat = (slot[:, None] // CAP == experts_all[None, :]).astype(BF)
    place_rep = jnp.dot(repeat, place, preferred_element_type=F32)
    own_map = (place_rep == (slot % CAP).astype(F32)[:, None]).astype(BF)

    def exchange(a):
        return lax.all_to_all(a, GROUP, split_axis=0, concat_axis=0, tiled=True)

    sent = jnp.dot(own_map, tokens, preferred_element_type=F32).astype(BF)
    sent, cotangent = lax.optimization_barrier((sent, cotangent))
    came = regroup(exchange(sent), True)
    up, down = fetch(came, "x", 1), fetch(came, "x", -1)
    pair = n_exp // 2
    far_lo, far_hi = fetch(down[:pair], "x", -1), fetch(up[pair:], "x", 1)

    cot = [cotangent] + [fetch(cotangent, "x", r) for r in (1, 2, 3)]
    meta = jnp.concatenate([routes_t.astype(BF), gates.T], axis=0)
    meta = jnp.pad(meta, ((0, 0), (0, width - tok)))
    whole = lax.all_gather(jnp.concatenate(cot + [meta]), ("y", "z"))
    whole, up, down = lax.optimization_barrier((whole, up, down))
    own, sib, maps = pick(ids, whole, n_exp)

    sib, far_lo, far_hi = lax.optimization_barrier((sib, far_lo, far_hi))
    x_blocks = (came, up, far_lo, far_hi, down)
    out_own, out_sib, hidden, slope, act = forward(ids, x_blocks, weights)
    out_sib, sib = lax.optimization_barrier((out_sib, fetch(sib, "c", 1)))
    g_blocks = (own, sib)
    mid = jax.ShapeDtypeStruct(hidden.shape, BF)
    grad_a, grad_b, back = backward(ids, g_blocks, slope, act, weights, mid, came.shape)
    back = lax.psum_scatter(back.reshape(-1, width), "x", scatter_dimension=0, tiled=True)

    out_sib, grad_a = lax.optimization_barrier((fetch(out_sib, "c", 1), grad_a))
    sums = sum_tokens(ids, maps, out_own, out_sib)
    ends_y, ends_z = collect_far(sums[:5], "y"), collect_far(sums[5:], "z")
    hidden, ends_y, ends_z = lax.optimization_barrier((hidden, ends_y, ends_z))
    grads = weight_grads(ids, x_blocks, g_blocks, (hidden, grad_a, grad_b), w_gate)
    part1, part2 = collect_near(ends_y, "y"), collect_near(ends_z, "z")
    grads, part1, part2 = lax.optimization_barrier((grads, part1, part2))
    part1, part2 = collect_small(part1, "z"), collect_small(part2, "y")

    back, part1 = lax.optimization_barrier((back, part1))
    back = exchange(regroup(back, False))
    mixed = collect_small((part1[0], part1[1], part2[0], part2[1]), "x")
    grad_tokens = tn(own_map, back).astype(BF)
    return (mixed, grad_tokens) + tuple(grads)


def solution(mesh):
    split = Mesh(mesh.devices.reshape(4, 2, 4, 4), ("y", "c", "z", "x"))
    acts = P(GROUP, "x")
    rows = P(GROUP, None)
    wts = P(GROUP, "x", None)
    return jax.shard_map(
        body,
        mesh=split,
        in_specs=(acts, rows, rows, acts, wts, wts, wts),
        out_specs=(acts, acts, wts, wts, wts),
        check_vma=False,
    )
```

```python
import functools

import jax
import jax.numpy as jnp
from jax import lax
from jax.experimental import pallas as pl
from jax.experimental.pallas import tpu as pltpu
from jax.sharding import Mesh
from jax.sharding import PartitionSpec as P

BF = jnp.bfloat16
F32 = jnp.float32
CAP = 12
GROUP = ("y", "c", "z")
VMEM_LIMIT = 52 * 1024 * 1024


def fetch(a, axis, r):
    n = lax.axis_size(axis)
    return lax.ppermute(a, axis, [((i + r) % n, i) for i in range(n)])


def add(*terms):
    total = terms[0].astype(F32)
    for term in terms[1:]:
        total = total + term.astype(F32)
    return total.astype(BF)


def nt(a, b):
    return lax.dot_general(a, b, (((1,), (1,)), ((), ())), preferred_element_type=F32)


def tn(a, b):
    return lax.dot_general(a, b, (((0,), (0,)), ((), ())), preferred_element_type=F32)


def nn(a, b):
    return jnp.dot(a, b, preferred_element_type=F32)


def slot_map(ids_ref, meta, n_exp):
    tok = meta[0].shape[1]
    y, z, c = ids_ref[0], ids_ref[1], ids_ref[2]
    top = meta[0].shape[0] // 2
    both = 2 * n_exp
    line = lax.broadcasted_iota(jnp.int32, (both, tok), 0)
    core = jnp.where(line < n_exp, c, 1 - c)
    expert = (y * 2 + core) * 4 + z
    expert = (expert * n_exp + lax.rem(line, n_exp)).astype(F32)
    earlier = (
        lax.broadcasted_iota(jnp.int32, (tok, tok), 0) < lax.broadcasted_iota(jnp.int32, (tok, tok), 1)
    ).astype(BF)
    widen = (
        lax.broadcasted_iota(jnp.int32, (both * 4, both), 0) // 4
        == lax.broadcasted_iota(jnp.int32, (both * 4, both), 1)
    ).astype(BF)
    owner = lax.rem(lax.broadcasted_iota(jnp.int32, (both * 4, tok), 0), 4)
    slots = both * 4 * CAP
    repeat = (
        lax.broadcasted_iota(jnp.int32, (slots, both * 4), 0) // CAP
        == lax.broadcasted_iota(jnp.int32, (slots, both * 4), 1)
    ).astype(BF)
    slot = lax.rem(lax.broadcasted_iota(jnp.int32, (slots, tok), 0), CAP).astype(F32)
    columns = []
    for zz in range(4):
        data = meta[zz].astype(F32)
        named = jnp.zeros((both, tok), F32)
        gate = jnp.zeros((both, tok), F32)
        for k in range(top):
            same = data[k : k + 1] == expert
            named = jnp.where(same, 1.0, named)
            gate = jnp.where(same, data[top + k : top + k + 1], gate)
        rank = jnp.where(named > 0, nn(named.astype(BF), earlier), -1.0)
        here = owner == zz
        rank = jnp.where(here, nn(widen, rank.astype(BF)), -1.0).astype(BF)
        gate = nn(widen, gate.astype(BF)).astype(BF)
        columns.append(jnp.where(nn(repeat, rank) == slot, nn(repeat, gate), 0.0).astype(BF))
    return jnp.concatenate(columns, axis=1)


def pick_kernel(ids_ref, whole_ref, own_ref, sib_ref, maps_ref):
    n_exp, span = own_ref.shape[:2]
    tok, width = 128, whole_ref.shape[2]
    n = own_ref.shape[2] // width
    slots = slot_map(ids_ref, [whole_ref[z, n * tok :, :tok] for z in range(4)], n_exp)
    maps_ref[0] = slots
    for r in range(n):
        block = jnp.concatenate([whole_ref[z, r * tok : (r + 1) * tok] for z in range(4)], axis=0)
        picked = nn(slots, block).astype(BF)
        cols = slice(r * width, (r + 1) * width)
        for e in range(n_exp):
            own_ref[e, :, cols] = picked[e * span : (e + 1) * span]
            lo = (n_exp + e) * span
            sib_ref[e, :, cols] = picked[lo : lo + span]


def pick(ids, whole, n_exp):
    width = whole.shape[2]
    span = 4 * CAP
    rows = jax.ShapeDtypeStruct((n_exp, 4 * span, 4 * width), BF)
    maps = jax.ShapeDtypeStruct((4, 2 * n_exp * span, 4 * 128), BF)
    rows_spec = pl.BlockSpec((n_exp, span, 4 * width), lambda i: (0, i, 0))
    return pl.pallas_call(
        pick_kernel,
        grid=(4,),
        out_shape=(rows, rows, maps),
        in_specs=[
            pl.BlockSpec(memory_space=pltpu.SMEM),
            pl.BlockSpec((4,) + whole.shape[1:], lambda i: (i, 0, 0)),
        ],
        out_specs=(rows_spec, rows_spec, pl.BlockSpec((1,) + maps.shape[1:], lambda i: (i, 0, 0))),
        compiler_params=pltpu.CompilerParams(vmem_limit_bytes=VMEM_LIMIT),
        cost_estimate=pl.CostEstimate(flops=4 << 30, bytes_accessed=18 << 20, transcendentals=0),
    )(ids, whole)


def gates_of(ids_ref, map_ref, which):
    tok = 128
    there = [pl.multiple_of(lax.rem(ids_ref[1] + zr, 4) * tok, tok) for zr in which]
    return jnp.concatenate([map_ref[0, :, pl.ds(t, tok)] for t in there], axis=1)


def rows_of(own_ref, sib_ref):
    return jnp.concatenate(
        [ref[e] for ref in (own_ref, sib_ref) for e in range(own_ref.shape[0])], axis=0
    )


def sum_far_kernel(
    ids_ref, map_ref, own_ref, sib_ref, map2_ref, own2_ref, sib2_ref, y_lo, y_hi, z_lo, z_hi
):
    yr = pl.program_id(0)
    tok, width = y_lo.shape[2:]
    gates = gates_of(ids_ref, map_ref, (2,))
    total = tn(gates, rows_of(own_ref, sib_ref)).astype(BF)
    for part, ref in enumerate((z_lo, z_hi)):

        @pl.when(yr // 2 == part)
        def _(ref=ref):
            ref[0, 0], ref[0, 1] = total[:, :width], total[:, width:]

    @pl.when(yr == 0)
    def _():
        rows = rows_of(own2_ref, sib2_ref)
        for part, ref in enumerate((y_lo, y_hi)):
            gates = gates_of(ids_ref, map2_ref, (2 * part, 2 * part + 1))
            total = tn(gates, rows).astype(BF)
            for i in range(2):
                for f in range(2):
                    ref[i, f] = total[i * tok : (i + 1) * tok, f * width : (f + 1) * width]


def sum_near_kernel(ids_ref, map_ref, own_ref, sib_ref, y0, y1, y3, z0, z1, z3):
    yr = pl.program_id(0)
    tok, width = y0.shape[2:]
    rows = rows_of(own_ref, sib_ref)
    near = tn(gates_of(ids_ref, map_ref, (0, 1, 3)), rows[:, 2 * width :]).astype(BF)
    for i, ref in enumerate((z0, z1, z3)):
        for f in range(2):
            ref[0, f] = near[i * tok : (i + 1) * tok, f * width : (f + 1) * width]

    @pl.when(yr != 2)
    def _():
        total = tn(gates_of(ids_ref, map_ref, range(4)), rows[:, : 2 * width]).astype(BF)
        for i, ref in ((0, y0), (1, y1), (3, y3)):

            @pl.when(yr == i)
            def _(ref=ref):
                for zr in range(4):
                    for f in range(2):
                        ref[zr, f] = total[zr * tok : (zr + 1) * tok, f * width : (f + 1) * width]


def sum_tokens(ids, maps, own, sib, far):
    n_exp, rows, cols = own.shape
    whole = jax.ShapeDtypeStruct((4, 2, 128, cols // 4), BF)
    half = jax.ShapeDtypeStruct((2,) + whole.shape[1:], BF)
    at = lambda i, ids: lax.rem(ids[0] + i, 4)
    block = (1,) + whole.shape[1:]
    keep = lambda a: pl.BlockSpec(a.shape, lambda i, ids: (0,) * 4)
    each_y = pl.BlockSpec(block, lambda i, ids: (i, 0, 0, 0))
    first = pl.BlockSpec(block, lambda i, ids: (jnp.minimum(i, 1), 0, 0, 0))
    last = pl.BlockSpec(block, lambda i, ids: (jnp.maximum(i - 2, 0), 0, 0, 0))
    one_map = (1,) + maps.shape[1:]
    map_y = pl.BlockSpec(one_map, lambda i, ids: (at(i, ids), 0, 0))
    map_2 = pl.BlockSpec(one_map, lambda i, ids: (at(2, ids), 0, 0))
    rows_y = pl.BlockSpec((n_exp, rows // 4, cols), lambda i, ids: (0, at(i, ids), 0))
    some = (n_exp, rows // 4, cols // 2)
    rows_z = pl.BlockSpec(some, lambda i, ids: (0, at(i, ids), 1))
    rows_2 = pl.BlockSpec(some, lambda i, ids: (0, at(2, ids), 0))

    def call(kernel, in_specs, args, outs, out_specs, flops):
        return pl.pallas_call(
            kernel,
            grid_spec=pltpu.PrefetchScalarGridSpec(
                num_scalar_prefetch=1, grid=(4,), in_specs=in_specs, out_specs=out_specs
            ),
            out_shape=outs,
            compiler_params=pltpu.CompilerParams(vmem_limit_bytes=VMEM_LIMIT),
            cost_estimate=pl.CostEstimate(flops=flops, bytes_accessed=flops >> 8, transcendentals=0),
        )(ids, *args)

    if far:
        return call(
            sum_far_kernel,
            [map_y, rows_z, rows_z, map_2, rows_2, rows_2],
            (maps, own, sib) * 2,
            (half,) * 4,
            (keep(half), keep(half), first, last),
            1 << 30,
        )
    return call(
        sum_near_kernel,
        [map_y, rows_y, rows_y],
        (maps, own, sib),
        (whole,) * 6,
        (keep(whole),) * 3 + (each_y,) * 3,
        3 << 30,
    )


def moved_columns(me, n, width):
    return [pl.ds(pl.multiple_of(lax.rem(me + r, n) * width, width), width) for r in range(n)]


def x_rows_of(c, refs):
    x0, x1, lo, hi, x3 = refs
    both = lambda ref: jnp.concatenate([ref[0, c], ref[0, 1 - c]], axis=0)
    far = jnp.where(pl.program_id(0) < 2, both(lo), both(hi))
    return [both(x0), both(x1), far, both(x3)]


def forward_kernel(ids_ref, *refs):
    x_refs, refs = refs[:5], refs[5:]
    wg, wu, wd, oo, os, hid_ref, slope_ref, act_ref = refs
    half, cols = oo.shape[1:]
    n, width = 4, cols // 4
    moved = moved_columns(ids_ref[3], n, width)
    x_rows = x_rows_of(ids_ref[2], x_refs)
    a = sum(nt(x_rows[r], wg[0, :, moved[r]]) for r in range(n))
    b = sum(nt(x_rows[r], wu[0, :, moved[r]]) for r in range(n))
    s = jax.nn.sigmoid(a)
    act = a * s
    hidden = (act * b).astype(BF)
    hid_ref[0] = hidden
    slope_ref[0] = b * s * (1.0 + a * (1.0 - s))
    act_ref[0] = act
    for r in range(n):
        out = nn(hidden, wd[0, :, moved[r]]).astype(BF)
        oo[0, :, r * width : (r + 1) * width] = out[:half]
        os[0, :, r * width : (r + 1) * width] = out[half:]


def back_kernel(ids_ref, own, sib, slope_ref, act_ref, wg, wu, wd, da_ref, db_ref, back_ref):
    c = ids_ref[2]
    n = back_ref.shape[0]
    half, width = back_ref.shape[3:]
    moved = moved_columns(ids_ref[3], n, width)
    fixed = [slice(r * width, (r + 1) * width) for r in range(n)]
    g_rows = [jnp.concatenate([own[0, :, f], sib[0, :, f]], axis=0) for f in fixed]
    gh = sum(nt(g_rows[r], wd[0, :, moved[r]]) for r in range(n))
    da = (gh * slope_ref[0]).astype(BF)
    db = (gh * act_ref[0]).astype(BF)
    da_ref[0] = da
    db_ref[0] = db
    for r in range(n):
        back = (nn(da, wg[0, :, fixed[r]]) + nn(db, wu[0, :, fixed[r]])).astype(BF)
        back_ref[r, 0, c] = back[:half]
        back_ref[r, 0, 1 - c] = back[half:]


def weights_kernel(ids_ref, *refs):
    x_refs, refs = refs[:5], refs[5:]
    own, sib, hid_ref, da_ref, db_ref, dwg, dwu, dwd = refs
    cols = own.shape[2]
    n, width = 4, cols // 4
    fixed = [slice(r * width, (r + 1) * width) for r in range(n)]
    moved = moved_columns(ids_ref[3], n, width)
    x_rows = x_rows_of(ids_ref[2], x_refs)
    hidden, da, db = hid_ref[0], da_ref[0], db_ref[0]
    for r in range(n):
        g_rows = jnp.concatenate([own[0, :, fixed[r]], sib[0, :, fixed[r]]], axis=0)
        dwg[0, :, moved[r]] = tn(da, x_rows[r]).astype(BF)
        dwu[0, :, moved[r]] = tn(db, x_rows[r]).astype(BF)
        dwd[0, :, moved[r]] = tn(hidden, g_rows).astype(BF)


def each(a):
    return pl.BlockSpec((1,) + a.shape[1:], lambda i: (i,) + (0,) * (a.ndim - 1))


def each_x(blocks):
    specs = [each(a) for a in blocks]
    lo, hi = blocks[2], blocks[3]
    specs[2] = pl.BlockSpec((1,) + lo.shape[1:], lambda i: (jnp.minimum(i, 1), 0, 0, 0))
    specs[3] = pl.BlockSpec((1,) + hi.shape[1:], lambda i: (jnp.maximum(i - 2, 0), 0, 0, 0))
    return specs


def per_expert(kernel, ids, in_specs, args, outs, out_specs, products, mebibytes):
    n_exp = 4
    return pl.pallas_call(
        kernel,
        grid=(n_exp,),
        out_shape=outs,
        in_specs=[pl.BlockSpec(memory_space=pltpu.SMEM)] + in_specs,
        out_specs=out_specs,
        compiler_params=pltpu.CompilerParams(vmem_limit_bytes=VMEM_LIMIT),
        cost_estimate=pl.CostEstimate(
            flops=products * (1536 * 192 * 2048 * 3), bytes_accessed=mebibytes << 20, transcendentals=0
        ),
    )(ids, *args)


def forward(ids, x, weights):
    n_exp, _, rows, width = x[0].shape
    mid = jax.ShapeDtypeStruct((n_exp, 2 * rows, weights[0].shape[1]), BF)
    wide = jax.ShapeDtypeStruct(mid.shape, F32)
    out = jax.ShapeDtypeStruct((n_exp, rows, 4 * width), BF)
    outs = (out, out, mid, wide, wide)
    args = tuple(x) + tuple(weights)
    specs = each_x(x) + [each(a) for a in weights]
    return per_expert(forward_kernel, ids, specs, args, outs, tuple(each(a) for a in outs), 3, 26)


def backward(ids, g, slope, act, weights, mid, shape):
    outs = (mid, mid, jax.ShapeDtypeStruct((4,) + shape, BF))
    args = tuple(g) + (slope, act) + tuple(weights)
    spec = pl.BlockSpec((4, 1) + shape[1:], lambda i: (0, i, 0, 0, 0))
    out_specs = (each(mid), each(mid), spec)
    return per_expert(back_kernel, ids, [each(a) for a in args], args, outs, out_specs, 3, 26)


def weight_grads(ids, x, g, mids, like):
    outs = (jax.ShapeDtypeStruct(like.shape, BF),) * 3
    args = tuple(x) + tuple(g) + tuple(mids)
    specs = each_x(x) + [each(a) for a in tuple(g) + tuple(mids)]
    return per_expert(weights_kernel, ids, specs, args, outs, tuple(each(a) for a in outs), 3, 24)


def collect_far(parts, axis):
    own, up, far_lo, far_hi, down = parts
    half = far_lo.shape[0]
    got_lo, got_hi = fetch(far_lo, axis, -1), fetch(far_hi, axis, 1)
    up = jnp.concatenate([add(up[:half], got_lo), up[half:]])
    down = jnp.concatenate([down[:half], add(down[half:], got_hi)])
    return own, up, down


def collect_near(parts, axis):
    own, up, down = parts
    return add(own, fetch(up, axis, -1), fetch(down, axis, 1))


def collect_small(parts, axis):
    return add(parts[0], *[fetch(parts[r], axis, -r) for r in (1, 2, 3)])


def ranks(named):
    tok = named.shape[-1]
    earlier = jnp.arange(tok)[:, None] < jnp.arange(tok)[None, :]
    count = jnp.dot(named.astype(BF), earlier.astype(BF), preferred_element_type=F32)
    return jnp.where(named > 0, count, -1.0)


def body(tokens, routes, gates, cotangent, w_gate, w_up, w_down):
    y, c, z, x = (lax.axis_index(a) for a in ("y", "c", "z", "x"))
    ids = jnp.stack([y, z, c, x]).astype(jnp.int32)
    n_exp = w_gate.shape[0]
    total_exp = n_exp * 32
    tok, width = tokens.shape
    weights = (w_gate, w_up, w_down)

    cot = [cotangent] + [fetch(cotangent, "x", r) for r in (1, 2, 3)]
    routes_t = routes.T
    experts_all = jnp.arange(total_exp, dtype=jnp.int32)
    named = jnp.sum((routes_t[:, None, :] == experts_all[None, :, None]).astype(F32), axis=0)
    place = ranks(named).astype(BF)
    slots = total_exp * CAP
    slot = jnp.arange(slots, dtype=jnp.int32)
    repeat = (slot[:, None] // CAP == experts_all[None, :]).astype(BF)
    place_rep = jnp.dot(repeat, place, preferred_element_type=F32)
    own_map = (place_rep == (slot % CAP).astype(F32)[:, None]).astype(BF)

    def exchange(a):
        return lax.all_to_all(a, GROUP, split_axis=0, concat_axis=0, tiled=True)

    came = exchange(jnp.dot(own_map, tokens, preferred_element_type=F32).astype(BF))

    meta = jnp.concatenate([routes_t.astype(BF), gates.T], axis=0)
    meta = jnp.pad(meta, ((0, 0), (0, width - tok)))
    whole = jnp.concatenate(cot + [meta])
    came, whole = lax.optimization_barrier((came, whole))
    whole = lax.all_gather(whole, ("y", "z"))

    came = came.reshape(4, 2, 4, n_exp, CAP, width).transpose(3, 1, 0, 2, 4, 5)
    came = came.reshape(n_exp, 2, 16 * CAP, width)
    up, down = fetch(came, "x", 1), fetch(came, "x", -1)
    pair = n_exp // 2
    x_blocks = (came, up, fetch(down[:pair], "x", -1), fetch(up[pair:], "x", 1), down)
    out_own, out_sib, hidden, slope, act = forward(ids, x_blocks, weights)

    whole, out_sib = lax.optimization_barrier((whole, out_sib))
    own, sib, maps = pick(ids, whole, n_exp)
    sib, out_sib = lax.optimization_barrier((sib, fetch(out_sib, "c", 1)))

    far = sum_tokens(ids, maps, out_own, out_sib, True)
    sib, far = lax.optimization_barrier((fetch(sib, "c", 1), far))
    g_blocks = (own, sib)
    mid = jax.ShapeDtypeStruct(hidden.shape, BF)
    grad_a, grad_b, back = backward(ids, g_blocks, slope, act, weights, mid, came.shape)
    back = lax.psum_scatter(back.reshape(-1, width), "x", scatter_dimension=0, tiled=True)

    out_sib, grad_a = lax.optimization_barrier((out_sib, grad_a))
    near = sum_tokens(ids, maps, out_own, out_sib, False)
    ends_y = collect_far((near[0], near[1], far[0], far[1], near[2]), "y")
    ends_z = collect_far((near[3], near[4], far[2], far[3], near[5]), "z")
    hidden, ends_y, ends_z = lax.optimization_barrier((hidden, ends_y, ends_z))
    grads = weight_grads(ids, x_blocks, g_blocks, (hidden, grad_a, grad_b), w_gate)
    part1, part2 = collect_near(ends_y, "y"), collect_near(ends_z, "z")
    grads, part1, part2 = lax.optimization_barrier((grads, part1, part2))
    part1, part2 = collect_small(part1, "z"), collect_small(part2, "y")

    back, part1, part2 = lax.optimization_barrier((back, part1, part2))
    back = back.reshape(n_exp, 2, 4, 4, CAP, width).transpose(2, 1, 3, 0, 4, 5)
    back = exchange(back.reshape(slots, width))
    mixed = collect_small((part1[0], part1[1], part2[0], part2[1]), "x")
    grad_tokens = tn(own_map, back).astype(BF)
    return (mixed, grad_tokens) + tuple(grads)


def solution(mesh):
    split = Mesh(mesh.devices.reshape(4, 2, 4, 4), ("y", "c", "z", "x"))
    acts = P(GROUP, "x")
    rows = P(GROUP, None)
    wts = P(GROUP, "x", None)
    return jax.shard_map(
        body,
        mesh=split,
        in_specs=(acts, rows, rows, acts, wts, wts, wts),
        out_specs=(acts, acts, wts, wts, wts),
        check_vma=False,
    )
```

```python
import functools

import jax
import jax.numpy as jnp
from jax import lax
from jax.experimental import pallas as pl
from jax.experimental.pallas import tpu as pltpu
from jax.sharding import Mesh
from jax.sharding import PartitionSpec as P

BF = jnp.bfloat16
F32 = jnp.float32
CAP = 12
GROUP = ("y", "c", "z")
VMEM_LIMIT = 30 * 1024 * 1024


def fetch(a, axis, r):
    n = lax.axis_size(axis)
    return lax.ppermute(a, axis, [((i + r) % n, i) for i in range(n)])


def add(*terms):
    total = terms[0].astype(F32)
    for term in terms[1:]:
        total = total + term.astype(F32)
    return total.astype(BF)


def nt(a, b):
    return lax.dot_general(a, b, (((1,), (1,)), ((), ())), preferred_element_type=F32)


def tn(a, b):
    return lax.dot_general(a, b, (((0,), (0,)), ((), ())), preferred_element_type=F32)


def nn(a, b):
    return jnp.dot(a, b, preferred_element_type=F32)


def slot_map(ids_ref, meta, n_exp):
    tok = meta[0].shape[1]
    y, z, c = ids_ref[0], ids_ref[1], ids_ref[2]
    top = meta[0].shape[0] // 2
    both = 2 * n_exp
    line = lax.broadcasted_iota(jnp.int32, (both, tok), 0)
    core = jnp.where(line < n_exp, c, 1 - c)
    expert = (y * 2 + core) * 4 + z
    expert = (expert * n_exp + lax.rem(line, n_exp)).astype(F32)
    earlier = (
        lax.broadcasted_iota(jnp.int32, (tok, tok), 0) < lax.broadcasted_iota(jnp.int32, (tok, tok), 1)
    ).astype(BF)
    widen = (
        lax.broadcasted_iota(jnp.int32, (both * 4, both), 0) // 4
        == lax.broadcasted_iota(jnp.int32, (both * 4, both), 1)
    ).astype(BF)
    owner = lax.rem(lax.broadcasted_iota(jnp.int32, (both * 4, tok), 0), 4)
    slots = both * 4 * CAP
    repeat = (
        lax.broadcasted_iota(jnp.int32, (slots, both * 4), 0) // CAP
        == lax.broadcasted_iota(jnp.int32, (slots, both * 4), 1)
    ).astype(BF)
    slot = lax.rem(lax.broadcasted_iota(jnp.int32, (slots, 1), 0), CAP).astype(F32)
    places, gates = [], []
    for zz in range(4):
        data = meta[zz].astype(F32)
        named = jnp.zeros((both, tok), F32)
        gate = jnp.zeros((both, tok), F32)
        for k in range(top):
            same = data[k : k + 1] == expert
            named = jnp.where(same, 1.0, named)
            gate = jnp.where(same, data[top + k : top + k + 1], gate)
        rank = jnp.where(named > 0, nn(named.astype(BF), earlier), -1.0)
        here = owner == zz
        places.append(jnp.where(here, nn(widen, rank.astype(BF)), -1.0).astype(BF))
        gates.append(nn(widen, gate.astype(BF)).astype(BF))
    place = nn(repeat, jnp.concatenate(places, axis=1))
    gate = nn(repeat, jnp.concatenate(gates, axis=1))
    return jnp.where(place == slot, gate, 0.0).astype(BF)


def pick_kernel(ids_ref, whole_ref, own_ref, sib_ref, maps_ref):
    n_exp, span = own_ref.shape[:2]
    tok, width = 128, whole_ref.shape[2]
    n = own_ref.shape[2] // width
    slots = slot_map(ids_ref, [whole_ref[z, n * tok :, :tok] for z in range(4)], n_exp)
    maps_ref[0] = slots
    for r in range(n):
        block = jnp.concatenate([whole_ref[z, r * tok : (r + 1) * tok] for z in range(4)], axis=0)
        picked = nn(slots, block).astype(BF)
        cols = slice(r * width, (r + 1) * width)
        for e in range(n_exp):
            own_ref[e, :, cols] = picked[e * span : (e + 1) * span]
            lo = (n_exp + e) * span
            sib_ref[e, :, cols] = picked[lo : lo + span]


def pick(ids, whole, n_exp):
    width = whole.shape[2]
    span = 4 * CAP
    rows = jax.ShapeDtypeStruct((n_exp, 4 * span, 4 * width), BF)
    maps = jax.ShapeDtypeStruct((4, 2 * n_exp * span, 4 * 128), BF)
    rows_spec = pl.BlockSpec((n_exp, span, 4 * width), lambda i: (0, i, 0))
    return pl.pallas_call(
        pick_kernel,
        grid=(4,),
        out_shape=(rows, rows, maps),
        in_specs=[
            pl.BlockSpec(memory_space=pltpu.SMEM),
            pl.BlockSpec((4,) + whole.shape[1:], lambda i: (i, 0, 0)),
        ],
        out_specs=(rows_spec, rows_spec, pl.BlockSpec((1,) + maps.shape[1:], lambda i: (i, 0, 0))),
        compiler_params=pltpu.CompilerParams(vmem_limit_bytes=VMEM_LIMIT),
        cost_estimate=pl.CostEstimate(flops=4 << 30, bytes_accessed=18 << 20, transcendentals=0),
    )(ids, whole)


def gates_of(ids_ref, map_ref, which):
    tok = 128
    there = [pl.multiple_of(lax.rem(ids_ref[1] + zr, 4) * tok, tok) for zr in which]
    return jnp.concatenate([map_ref[0, :, pl.ds(t, tok)] for t in there], axis=1)


def rows_of(own_ref, sib_ref):
    return jnp.concatenate(
        [ref[e] for ref in (own_ref, sib_ref) for e in range(own_ref.shape[0])], axis=0
    )


def sum_far_kernel(
    ids_ref, map_ref, own_ref, sib_ref, map2_ref, own2_ref, sib2_ref, y_lo, y_hi, z_lo, z_hi
):
    yr = pl.program_id(0)
    tok, width = y_lo.shape[2:]
    gates = gates_of(ids_ref, map_ref, (2,))
    total = tn(gates, rows_of(own_ref, sib_ref)).astype(BF)
    for part, ref in enumerate((z_lo, z_hi)):

        @pl.when(yr // 2 == part)
        def _(ref=ref):
            ref[0, 0], ref[0, 1] = total[:, :width], total[:, width:]

    @pl.when(yr == 0)
    def _():
        rows = rows_of(own2_ref, sib2_ref)
        for part, ref in enumerate((y_lo, y_hi)):
            gates = gates_of(ids_ref, map2_ref, (2 * part, 2 * part + 1))
            total = tn(gates, rows).astype(BF)
            for i in range(2):
                for f in range(2):
                    ref[i, f] = total[i * tok : (i + 1) * tok, f * width : (f + 1) * width]


def sum_near_kernel(ids_ref, map_ref, own_ref, sib_ref, y0, y1, y3, z0, z1, z3):
    yr = pl.program_id(0)
    tok, width = y0.shape[2:]
    rows = rows_of(own_ref, sib_ref)
    near = tn(gates_of(ids_ref, map_ref, (0, 1, 3)), rows[:, 2 * width :]).astype(BF)
    for i, ref in enumerate((z0, z1, z3)):
        for f in range(2):
            ref[0, f] = near[i * tok : (i + 1) * tok, f * width : (f + 1) * width]

    @pl.when(yr != 2)
    def _():
        total = tn(gates_of(ids_ref, map_ref, range(4)), rows[:, : 2 * width]).astype(BF)
        for i, ref in ((0, y0), (1, y1), (3, y3)):

            @pl.when(yr == i)
            def _(ref=ref):
                for zr in range(4):
                    for f in range(2):
                        ref[zr, f] = total[zr * tok : (zr + 1) * tok, f * width : (f + 1) * width]


def sum_tokens(ids, maps, own, sib, far):
    n_exp, rows, cols = own.shape
    whole = jax.ShapeDtypeStruct((4, 2, 128, cols // 4), BF)
    half = jax.ShapeDtypeStruct((2,) + whole.shape[1:], BF)
    at = lambda i, ids: lax.rem(ids[0] + i, 4)
    block = (1,) + whole.shape[1:]
    keep = lambda a: pl.BlockSpec(a.shape, lambda i, ids: (0,) * 4)
    each_y = pl.BlockSpec(block, lambda i, ids: (i, 0, 0, 0))
    first = pl.BlockSpec(block, lambda i, ids: (jnp.minimum(i, 1), 0, 0, 0))
    last = pl.BlockSpec(block, lambda i, ids: (jnp.maximum(i - 2, 0), 0, 0, 0))
    one_map = (1,) + maps.shape[1:]
    map_y = pl.BlockSpec(one_map, lambda i, ids: (at(i, ids), 0, 0))
    map_2 = pl.BlockSpec(one_map, lambda i, ids: (at(2, ids), 0, 0))
    rows_y = pl.BlockSpec((n_exp, rows // 4, cols), lambda i, ids: (0, at(i, ids), 0))
    some = (n_exp, rows // 4, cols // 2)
    rows_z = pl.BlockSpec(some, lambda i, ids: (0, at(i, ids), 1))
    rows_2 = pl.BlockSpec(some, lambda i, ids: (0, at(2, ids), 0))

    def call(kernel, in_specs, args, outs, out_specs, flops):
        return pl.pallas_call(
            kernel,
            grid_spec=pltpu.PrefetchScalarGridSpec(
                num_scalar_prefetch=1, grid=(4,), in_specs=in_specs, out_specs=out_specs
            ),
            out_shape=outs,
            compiler_params=pltpu.CompilerParams(vmem_limit_bytes=VMEM_LIMIT),
            cost_estimate=pl.CostEstimate(flops=flops, bytes_accessed=flops >> 8, transcendentals=0),
        )(ids, *args)

    if far:
        return call(
            sum_far_kernel,
            [map_y, rows_z, rows_z, map_2, rows_2, rows_2],
            (maps, own, sib) * 2,
            (half,) * 4,
            (keep(half), keep(half), first, last),
            1 << 30,
        )
    return call(
        sum_near_kernel,
        [map_y, rows_y, rows_y],
        (maps, own, sib),
        (whole,) * 6,
        (keep(whole),) * 3 + (each_y,) * 3,
        3 << 30,
    )


def moved_columns(me, n, width):
    return [pl.ds(pl.multiple_of(lax.rem(me + r, n) * width, width), width) for r in range(n)]


def both_cores(c, ref):
    return jnp.concatenate([ref[0, c], ref[0, 1 - c]], axis=0)


def far_rows(c, lo, hi):
    return jnp.where(pl.program_id(0) < 2, both_cores(c, lo), both_cores(c, hi))


def x_rows_of(c, refs):
    x0, x1, lo, hi, x3 = refs
    return [both_cores(c, x0), both_cores(c, x1), far_rows(c, lo, hi), both_cores(c, x3)]


def near_kernel(ids_ref, x0, x1, x3, wg, wu, a_ref, b_ref):
    c = ids_ref[2]
    n, width = 4, x0.shape[3]
    moved = moved_columns(ids_ref[3], n, width)
    blocks = [(0, both_cores(c, x0)), (1, both_cores(c, x1)), (3, both_cores(c, x3))]
    a_ref[0] = sum(nt(rows, wg[0, :, moved[r]]) for r, rows in blocks)
    b_ref[0] = sum(nt(rows, wu[0, :, moved[r]]) for r, rows in blocks)


def forward_kernel(ids_ref, lo, hi, a_ref, b_ref, wg2, wu2, wd, oo, os, hid_ref, slope_ref, act_ref):
    half, cols = oo.shape[1:]
    n, width = 4, cols // 4
    moved = moved_columns(ids_ref[3], n, width)
    far = far_rows(ids_ref[2], lo, hi)
    a = a_ref[0] + nt(far, wg2[0])
    b = b_ref[0] + nt(far, wu2[0])
    s = jax.nn.sigmoid(a)
    act = a * s
    hidden = (act * b).astype(BF)
    hid_ref[0] = hidden
    slope_ref[0] = b * s * (1.0 + a * (1.0 - s))
    act_ref[0] = act
    for r in range(n):
        out = nn(hidden, wd[0, :, moved[r]]).astype(BF)
        oo[0, :, r * width : (r + 1) * width] = out[:half]
        os[0, :, r * width : (r + 1) * width] = out[half:]


def back_kernel(ids_ref, own, sib, slope_ref, act_ref, wg, wu, wd, da_ref, db_ref, back_ref):
    c = ids_ref[2]
    n = back_ref.shape[0]
    half, width = back_ref.shape[3:]
    moved = moved_columns(ids_ref[3], n, width)
    fixed = [slice(r * width, (r + 1) * width) for r in range(n)]
    g_rows = [jnp.concatenate([own[0, :, f], sib[0, :, f]], axis=0) for f in fixed]
    gh = sum(nt(g_rows[r], wd[0, :, moved[r]]) for r in range(n))
    da = (gh * slope_ref[0]).astype(BF)
    db = (gh * act_ref[0]).astype(BF)
    da_ref[0] = da
    db_ref[0] = db
    for r in range(n):
        back = (nn(da, wg[0, :, fixed[r]]) + nn(db, wu[0, :, fixed[r]])).astype(BF)
        back_ref[r, 0, c] = back[:half]
        back_ref[r, 0, 1 - c] = back[half:]


def weights_kernel(ids_ref, *refs):
    x_refs, refs = refs[:5], refs[5:]
    own, sib, hid_ref, da_ref, db_ref, dwg, dwu, dwd = refs
    cols = own.shape[2]
    n, width = 4, cols // 4
    fixed = [slice(r * width, (r + 1) * width) for r in range(n)]
    moved = moved_columns(ids_ref[3], n, width)
    x_rows = x_rows_of(ids_ref[2], x_refs)
    hidden, da, db = hid_ref[0], da_ref[0], db_ref[0]
    for r in range(n):
        g_rows = jnp.concatenate([own[0, :, fixed[r]], sib[0, :, fixed[r]]], axis=0)
        dwg[0, :, moved[r]] = tn(da, x_rows[r]).astype(BF)
        dwu[0, :, moved[r]] = tn(db, x_rows[r]).astype(BF)
        dwd[0, :, moved[r]] = tn(hidden, g_rows).astype(BF)


def each(a):
    return pl.BlockSpec((1,) + a.shape[1:], lambda i, *_: (i,) + (0,) * (len(a.shape) - 1))


def each_far(lo, hi):
    return [
        pl.BlockSpec((1,) + lo.shape[1:], lambda i, *_: (jnp.minimum(i, 1), 0, 0, 0)),
        pl.BlockSpec((1,) + hi.shape[1:], lambda i, *_: (jnp.maximum(i - 2, 0), 0, 0, 0)),
    ]


def each_x(blocks):
    specs = [each(a) for a in blocks]
    return specs[:2] + each_far(blocks[2], blocks[3]) + specs[4:]


def per_expert(kernel, ids, in_specs, args, outs, out_specs, products, mebibytes):
    return pl.pallas_call(
        kernel,
        grid_spec=pltpu.PrefetchScalarGridSpec(
            num_scalar_prefetch=1, grid=(4,), in_specs=in_specs, out_specs=out_specs
        ),
        out_shape=outs,
        compiler_params=pltpu.CompilerParams(vmem_limit_bytes=VMEM_LIMIT),
        cost_estimate=pl.CostEstimate(
            flops=products * (1536 * 192 * 2048 * 3), bytes_accessed=mebibytes << 20, transcendentals=0
        ),
    )(ids, *args)


def near_products(ids, x, weights):
    n_exp, _, rows, _ = x[0].shape
    wide = jax.ShapeDtypeStruct((n_exp, 2 * rows, weights[0].shape[1]), F32)
    args = tuple(x) + tuple(weights)
    specs = [each(a) for a in args]
    return per_expert(near_kernel, ids, specs, args, (wide, wide), (each(wide),) * 2, 2, 14)


def forward(ids, far, near, weights):
    n_exp, _, rows, width = far[0].shape
    n_exp *= 2
    wide = near[0]
    mid = jax.ShapeDtypeStruct(wide.shape, BF)
    out = jax.ShapeDtypeStruct((n_exp, rows, 4 * width), BF)
    outs = (out, out, mid, wide, wide)
    wg, wu, wd = weights
    one = pl.BlockSpec(
        (1, wg.shape[1], width), lambda i, ids: (i, 0, lax.rem(ids[3] + 2, 4))
    )
    specs = each_far(*far) + [each(wide), each(wide), one, one, each(wd)]
    args = tuple(far) + tuple(near) + (wg, wu, wd)
    outs = tuple(jax.ShapeDtypeStruct(o.shape, o.dtype) for o in outs)
    return per_expert(forward_kernel, ids, specs, args, outs, tuple(each(a) for a in outs), 2, 18)


def backward(ids, g, slope, act, weights, mid, shape):
    outs = (mid, mid, jax.ShapeDtypeStruct((4,) + shape, BF))
    args = tuple(g) + (slope, act) + tuple(weights)
    spec = pl.BlockSpec((4, 1) + shape[1:], lambda i, *_: (0, i, 0, 0, 0))
    out_specs = (each(mid), each(mid), spec)
    return per_expert(back_kernel, ids, [each(a) for a in args], args, outs, out_specs, 3, 26)


def weight_grads(ids, x, g, mids, like):
    outs = (jax.ShapeDtypeStruct(like.shape, BF),) * 3
    args = tuple(x) + tuple(g) + tuple(mids)
    specs = each_x(x) + [each(a) for a in tuple(g) + tuple(mids)]
    return per_expert(weights_kernel, ids, specs, args, outs, tuple(each(a) for a in outs), 3, 24)


def collect_far(parts, got):
    own, up, down = parts
    got_lo, got_hi = got
    half = got_lo.shape[0]
    up = jnp.concatenate([add(up[:half], got_lo), up[half:]])
    down = jnp.concatenate([down[:half], add(down[half:], got_hi)])
    return own, up, down


def collect_near(parts, axis):
    own, up, down = parts
    return add(own, fetch(up, axis, -1), fetch(down, axis, 1))


def collect_small(parts, axis):
    return add(parts[0], *[fetch(parts[r], axis, -r) for r in (1, 2, 3)])


def ranks(named):
    tok = named.shape[-1]
    earlier = jnp.arange(tok)[:, None] < jnp.arange(tok)[None, :]
    count = jnp.dot(named.astype(BF), earlier.astype(BF), preferred_element_type=F32)
    return jnp.where(named > 0, count, -1.0)


def body(tokens, routes, gates, cotangent, w_gate, w_up, w_down):
    y, c, z, x = (lax.axis_index(a) for a in ("y", "c", "z", "x"))
    ids = jnp.stack([y, z, c, x]).astype(jnp.int32)
    n_exp = w_gate.shape[0]
    total_exp = n_exp * 32
    tok, width = tokens.shape
    weights = (w_gate, w_up, w_down)

    cot = [cotangent] + [fetch(cotangent, "x", r) for r in (1, 2, 3)]
    routes_t = routes.T
    experts_all = jnp.arange(total_exp, dtype=jnp.int32)
    named = jnp.sum((routes_t[:, None, :] == experts_all[None, :, None]).astype(F32), axis=0)
    place = ranks(named).astype(BF)
    slots = total_exp * CAP
    slot = jnp.arange(slots, dtype=jnp.int32)
    repeat = (slot[:, None] // CAP == experts_all[None, :]).astype(BF)
    place_rep = jnp.dot(repeat, place, preferred_element_type=F32)
    own_map = (place_rep == (slot % CAP).astype(F32)[:, None]).astype(BF)

    def exchange(a):
        return lax.all_to_all(a, GROUP, split_axis=0, concat_axis=0, tiled=True)

    came = exchange(jnp.dot(own_map, tokens, preferred_element_type=F32).astype(BF))

    meta = jnp.concatenate([routes_t.astype(BF), gates.T], axis=0)
    meta = jnp.pad(meta, ((0, 0), (0, width - tok)))
    whole = jnp.concatenate(cot + [meta])
    came, whole = lax.optimization_barrier((came, whole))
    whole = lax.all_gather(whole, ("y", "z"))

    came = came.reshape(4, 2, 4, n_exp, CAP, width).transpose(3, 1, 0, 2, 4, 5)
    came = came.reshape(n_exp, 2, 16 * CAP, width)
    up, down = fetch(came, "x", 1), fetch(came, "x", -1)
    pair = n_exp // 2
    near = near_products(ids, (came, up, down), weights[:2])
    far = (fetch(down[:pair], "x", -1), fetch(up[pair:], "x", 1))
    x_blocks = (came, up) + far + (down,)
    out_own, out_sib, hidden, slope, act = forward(ids, far, near, weights)

    whole, out_sib = lax.optimization_barrier((whole, out_sib))
    own, sib, maps = pick(ids, whole, n_exp)
    sib, out_sib = lax.optimization_barrier((sib, fetch(out_sib, "c", 1)))

    far = sum_tokens(ids, maps, out_own, out_sib, True)
    sib, far = lax.optimization_barrier((fetch(sib, "c", 1), far))
    got_y = (fetch(far[0], "y", -1), fetch(far[1], "y", 1))
    got_z = (fetch(far[2], "z", -1), fetch(far[3], "z", 1))
    g_blocks = (own, sib)
    mid = jax.ShapeDtypeStruct(hidden.shape, BF)
    grad_a, grad_b, back = backward(ids, g_blocks, slope, act, weights, mid, came.shape)
    back = lax.psum_scatter(back.reshape(-1, width), "x", scatter_dimension=0, tiled=True)

    out_sib, grad_a = lax.optimization_barrier((out_sib, grad_a))
    near = sum_tokens(ids, maps, out_own, out_sib, False)
    near, got_y, got_z = lax.optimization_barrier((near, got_y, got_z))
    ends_y, ends_z = collect_far(near[:3], got_y), collect_far(near[3:], got_z)
    hidden, ends_y, ends_z = lax.optimization_barrier((hidden, ends_y, ends_z))
    grads = weight_grads(ids, x_blocks, g_blocks, (hidden, grad_a, grad_b), w_gate)
    part1, part2 = collect_near(ends_y, "y"), collect_near(ends_z, "z")
    grads, part1, part2 = lax.optimization_barrier((grads, part1, part2))
    part1, part2 = collect_small(part1, "z"), collect_small(part2, "y")

    back, part1, part2 = lax.optimization_barrier((back, part1, part2))
    back = back.reshape(n_exp, 2, 4, 4, CAP, width).transpose(2, 1, 3, 0, 4, 5)
    back = exchange(back.reshape(slots, width))
    mixed = collect_small((part1[0], part1[1], part2[0], part2[1]), "x")
    grad_tokens = tn(own_map, back).astype(BF)
    return (mixed, grad_tokens) + tuple(grads)


def solution(mesh):
    split = Mesh(mesh.devices.reshape(4, 2, 4, 4), ("y", "c", "z", "x"))
    acts = P(GROUP, "x")
    rows = P(GROUP, None)
    wts = P(GROUP, "x", None)
    return jax.shard_map(
        body,
        mesh=split,
        in_specs=(acts, rows, rows, acts, wts, wts, wts),
        out_specs=(acts, acts, wts, wts, wts),
        check_vma=False,
    )
```

```python
import functools

import jax
import jax.numpy as jnp
from jax import lax
from jax.experimental import pallas as pl
from jax.experimental.pallas import tpu as pltpu
from jax.sharding import Mesh
from jax.sharding import PartitionSpec as P

BF = jnp.bfloat16
F32 = jnp.float32
CAP = 12
GROUP = ("y", "c", "z")
VMEM_LIMIT = 30 * 1024 * 1024


def fetch(a, axis, r):
    n = lax.axis_size(axis)
    return lax.ppermute(a, axis, [((i + r) % n, i) for i in range(n)])


def add(*terms):
    total = terms[0].astype(F32)
    for term in terms[1:]:
        total = total + term.astype(F32)
    return total.astype(BF)


def nt(a, b):
    return lax.dot_general(a, b, (((1,), (1,)), ((), ())), preferred_element_type=F32)


def tn(a, b):
    return lax.dot_general(a, b, (((0,), (0,)), ((), ())), preferred_element_type=F32)


def nn(a, b):
    return jnp.dot(a, b, preferred_element_type=F32)


def slot_map(ids_ref, meta, n_exp):
    tok = meta[0].shape[1]
    y, z, c = ids_ref[0], ids_ref[1], ids_ref[2]
    top = meta[0].shape[0] // 2
    both = 2 * n_exp
    line = lax.broadcasted_iota(jnp.int32, (both, tok), 0)
    core = jnp.where(line < n_exp, c, 1 - c)
    expert = (y * 2 + core) * 4 + z
    expert = (expert * n_exp + lax.rem(line, n_exp)).astype(F32)
    earlier = (
        lax.broadcasted_iota(jnp.int32, (tok, tok), 0) < lax.broadcasted_iota(jnp.int32, (tok, tok), 1)
    ).astype(BF)
    widen = (
        lax.broadcasted_iota(jnp.int32, (both * 4, both), 0) // 4
        == lax.broadcasted_iota(jnp.int32, (both * 4, both), 1)
    ).astype(BF)
    owner = lax.rem(lax.broadcasted_iota(jnp.int32, (both * 4, tok), 0), 4)
    slots = both * 4 * CAP
    repeat = (
        lax.broadcasted_iota(jnp.int32, (slots, both * 4), 0) // CAP
        == lax.broadcasted_iota(jnp.int32, (slots, both * 4), 1)
    ).astype(BF)
    slot = lax.rem(lax.broadcasted_iota(jnp.int32, (slots, 1), 0), CAP).astype(F32)
    places, gates = [], []
    for zz in range(4):
        data = meta[zz].astype(F32)
        named = jnp.zeros((both, tok), F32)
        gate = jnp.zeros((both, tok), F32)
        for k in range(top):
            same = data[k : k + 1] == expert
            named = jnp.where(same, 1.0, named)
            gate = jnp.where(same, data[top + k : top + k + 1], gate)
        rank = jnp.where(named > 0, nn(named.astype(BF), earlier), -1.0)
        here = owner == zz
        places.append(jnp.where(here, nn(widen, rank.astype(BF)), -1.0).astype(BF))
        gates.append(nn(widen, gate.astype(BF)).astype(BF))
    place = nn(repeat, jnp.concatenate(places, axis=1))
    gate = nn(repeat, jnp.concatenate(gates, axis=1))
    return jnp.where(place == slot, gate, 0.0).astype(BF)


def pick_kernel(ids_ref, whole_ref, own_ref, sib_ref, maps_ref):
    n_exp, span = own_ref.shape[:2]
    tok, width = 128, whole_ref.shape[2]
    n = own_ref.shape[2] // width
    slots = slot_map(ids_ref, [whole_ref[z, n * tok :, :tok] for z in range(4)], n_exp)
    maps_ref[0] = slots
    for r in range(n):
        block = jnp.concatenate([whole_ref[z, r * tok : (r + 1) * tok] for z in range(4)], axis=0)
        picked = nn(slots, block).astype(BF)
        cols = slice(r * width, (r + 1) * width)
        for e in range(n_exp):
            own_ref[e, :, cols] = picked[e * span : (e + 1) * span]
            lo = (n_exp + e) * span
            sib_ref[e, :, cols] = picked[lo : lo + span]


def pick(ids, whole, n_exp):
    width = whole.shape[2]
    span = 4 * CAP
    rows = jax.ShapeDtypeStruct((n_exp, 4 * span, 4 * width), BF)
    maps = jax.ShapeDtypeStruct((4, 2 * n_exp * span, 4 * 128), BF)
    rows_spec = pl.BlockSpec((n_exp, span, 4 * width), lambda i: (0, i, 0))
    return pl.pallas_call(
        pick_kernel,
        grid=(4,),
        out_shape=(rows, rows, maps),
        in_specs=[
            pl.BlockSpec(memory_space=pltpu.SMEM),
            pl.BlockSpec((4,) + whole.shape[1:], lambda i: (i, 0, 0)),
        ],
        out_specs=(rows_spec, rows_spec, pl.BlockSpec((1,) + maps.shape[1:], lambda i: (i, 0, 0))),
        compiler_params=pltpu.CompilerParams(vmem_limit_bytes=VMEM_LIMIT),
        cost_estimate=pl.CostEstimate(flops=4 << 30, bytes_accessed=18 << 20, transcendentals=0),
    )(ids, whole)


def gates_of(ids_ref, map_ref, which):
    tok = 128
    there = [pl.multiple_of(lax.rem(ids_ref[1] + zr, 4) * tok, tok) for zr in which]
    return jnp.concatenate([map_ref[0, :, pl.ds(t, tok)] for t in there], axis=1)


def rows_of(own_ref, sib_ref):
    return jnp.concatenate(
        [ref[e] for ref in (own_ref, sib_ref) for e in range(own_ref.shape[0])], axis=0
    )


def sum_far_kernel(
    ids_ref, map_ref, own_ref, sib_ref, map2_ref, own2_ref, sib2_ref, y_lo, y_hi, z_lo, z_hi
):
    yr = pl.program_id(0)
    tok, width = y_lo.shape[2:]
    gates = gates_of(ids_ref, map_ref, (2,))
    total = tn(gates, rows_of(own_ref, sib_ref)).astype(BF)
    for part, ref in enumerate((z_lo, z_hi)):

        @pl.when(yr // 2 == part)
        def _(ref=ref):
            ref[0, 0], ref[0, 1] = total[:, :width], total[:, width:]

    @pl.when(yr == 0)
    def _():
        rows = rows_of(own2_ref, sib2_ref)
        for part, ref in enumerate((y_lo, y_hi)):
            gates = gates_of(ids_ref, map2_ref, (2 * part, 2 * part + 1))
            total = tn(gates, rows).astype(BF)
            for i in range(2):
                for f in range(2):
                    ref[i, f] = total[i * tok : (i + 1) * tok, f * width : (f + 1) * width]


def sum_near_kernel(ids_ref, map_ref, own_ref, sib_ref, y0, y1, y3, z0, z1, z3):
    yr = pl.program_id(0)
    tok, width = y0.shape[2:]
    rows = rows_of(own_ref, sib_ref)
    near = tn(gates_of(ids_ref, map_ref, (0, 1, 3)), rows[:, 2 * width :]).astype(BF)
    for i, ref in enumerate((z0, z1, z3)):
        for f in range(2):
            ref[0, f] = near[i * tok : (i + 1) * tok, f * width : (f + 1) * width]

    @pl.when(yr != 2)
    def _():
        total = tn(gates_of(ids_ref, map_ref, range(4)), rows[:, : 2 * width]).astype(BF)
        for i, ref in ((0, y0), (1, y1), (3, y3)):

            @pl.when(yr == i)
            def _(ref=ref):
                for zr in range(4):
                    for f in range(2):
                        ref[zr, f] = total[zr * tok : (zr + 1) * tok, f * width : (f + 1) * width]


def sum_tokens(ids, maps, own, sib, far):
    n_exp, rows, cols = own.shape
    whole = jax.ShapeDtypeStruct((4, 2, 128, cols // 4), BF)
    half = jax.ShapeDtypeStruct((2,) + whole.shape[1:], BF)
    at = lambda i, ids: lax.rem(ids[0] + i, 4)
    block = (1,) + whole.shape[1:]
    keep = lambda a: pl.BlockSpec(a.shape, lambda i, ids: (0,) * 4)
    each_y = pl.BlockSpec(block, lambda i, ids: (i, 0, 0, 0))
    first = pl.BlockSpec(block, lambda i, ids: (jnp.minimum(i, 1), 0, 0, 0))
    last = pl.BlockSpec(block, lambda i, ids: (jnp.maximum(i - 2, 0), 0, 0, 0))
    one_map = (1,) + maps.shape[1:]
    map_y = pl.BlockSpec(one_map, lambda i, ids: (at(i, ids), 0, 0))
    map_2 = pl.BlockSpec(one_map, lambda i, ids: (at(2, ids), 0, 0))
    rows_y = pl.BlockSpec((n_exp, rows // 4, cols), lambda i, ids: (0, at(i, ids), 0))
    some = (n_exp, rows // 4, cols // 2)
    rows_z = pl.BlockSpec(some, lambda i, ids: (0, at(i, ids), 1))
    rows_2 = pl.BlockSpec(some, lambda i, ids: (0, at(2, ids), 0))

    def call(kernel, in_specs, args, outs, out_specs, flops):
        return pl.pallas_call(
            kernel,
            grid_spec=pltpu.PrefetchScalarGridSpec(
                num_scalar_prefetch=1, grid=(4,), in_specs=in_specs, out_specs=out_specs
            ),
            out_shape=outs,
            compiler_params=pltpu.CompilerParams(vmem_limit_bytes=VMEM_LIMIT),
            cost_estimate=pl.CostEstimate(flops=flops, bytes_accessed=flops >> 8, transcendentals=0),
        )(ids, *args)

    if far:
        return call(
            sum_far_kernel,
            [map_y, rows_z, rows_z, map_2, rows_2, rows_2],
            (maps, own, sib) * 2,
            (half,) * 4,
            (keep(half), keep(half), first, last),
            1 << 30,
        )
    return call(
        sum_near_kernel,
        [map_y, rows_y, rows_y],
        (maps, own, sib),
        (whole,) * 6,
        (keep(whole),) * 3 + (each_y,) * 3,
        3 << 30,
    )


def moved_columns(me, n, width):
    return [pl.ds(pl.multiple_of(lax.rem(me + r, n) * width, width), width) for r in range(n)]


def both_cores(c, ref):
    return jnp.concatenate([ref[0, c], ref[0, 1 - c]], axis=0)


def far_rows(c, lo, hi):
    return jnp.where(pl.program_id(0) < 2, both_cores(c, lo), both_cores(c, hi))


def x_rows_of(c, refs):
    x0, x1, lo, hi, x3 = refs
    return [both_cores(c, x0), both_cores(c, x1), far_rows(c, lo, hi), both_cores(c, x3)]


def near_kernel(ids_ref, x0, x1, x3, wg, wu, a_ref, b_ref):
    c = ids_ref[2]
    n, width = 4, x0.shape[3]
    moved = moved_columns(ids_ref[3], n, width)
    blocks = [(0, both_cores(c, x0)), (1, both_cores(c, x1)), (3, both_cores(c, x3))]
    a_ref[0] = sum(nt(rows, wg[0, :, moved[r]]) for r, rows in blocks)
    b_ref[0] = sum(nt(rows, wu[0, :, moved[r]]) for r, rows in blocks)


def forward_kernel(ids_ref, lo, hi, a_ref, b_ref, wg2, wu2, wd, oo, os, hid_ref, slope_ref, act_ref):
    half, cols = oo.shape[1:]
    n, width = 4, cols // 4
    moved = moved_columns(ids_ref[3], n, width)
    far = far_rows(ids_ref[2], lo, hi)
    a = a_ref[0] + nt(far, wg2[0])
    b = b_ref[0] + nt(far, wu2[0])
    s = jax.nn.sigmoid(a)
    act = a * s
    hidden = (act * b).astype(BF)
    hid_ref[0] = hidden
    slope_ref[0] = b * s * (1.0 + a * (1.0 - s))
    act_ref[0] = act
    for r in range(n):
        out = nn(hidden, wd[0, :, moved[r]]).astype(BF)
        oo[0, :, r * width : (r + 1) * width] = out[:half]
        os[0, :, r * width : (r + 1) * width] = out[half:]


def back_kernel(ids_ref, own, sib, slope_ref, act_ref, wg, wu, wd, da_ref, db_ref, back_ref):
    c = ids_ref[2]
    n = back_ref.shape[0]
    half, width = back_ref.shape[3:]
    moved = moved_columns(ids_ref[3], n, width)
    fixed = [slice(r * width, (r + 1) * width) for r in range(n)]
    g_rows = [jnp.concatenate([own[0, :, f], sib[0, :, f]], axis=0) for f in fixed]
    gh = sum(nt(g_rows[r], wd[0, :, moved[r]]) for r in range(n))
    da = (gh * slope_ref[0]).astype(BF)
    db = (gh * act_ref[0]).astype(BF)
    da_ref[0] = da
    db_ref[0] = db
    for r in range(n):
        back = (nn(da, wg[0, :, fixed[r]]) + nn(db, wu[0, :, fixed[r]])).astype(BF)
        back_ref[r, 0, c] = back[:half]
        back_ref[r, 0, 1 - c] = back[half:]


def weights_kernel(ids_ref, *refs):
    x_refs, refs = refs[:5], refs[5:]
    own, sib, hid_ref, da_ref, db_ref, dwg, dwu, dwd = refs
    cols = own.shape[2]
    n, width = 4, cols // 4
    fixed = [slice(r * width, (r + 1) * width) for r in range(n)]
    moved = moved_columns(ids_ref[3], n, width)
    x_rows = x_rows_of(ids_ref[2], x_refs)
    hidden, da, db = hid_ref[0], da_ref[0], db_ref[0]
    for r in range(n):
        g_rows = jnp.concatenate([own[0, :, fixed[r]], sib[0, :, fixed[r]]], axis=0)
        dwg[0, :, moved[r]] = tn(da, x_rows[r]).astype(BF)
        dwu[0, :, moved[r]] = tn(db, x_rows[r]).astype(BF)
        dwd[0, :, moved[r]] = tn(hidden, g_rows).astype(BF)


def each(a):
    return pl.BlockSpec((1,) + a.shape[1:], lambda i, *_: (i,) + (0,) * (len(a.shape) - 1))


def each_far(lo, hi):
    return [
        pl.BlockSpec((1,) + lo.shape[1:], lambda i, *_: (jnp.minimum(i, 1), 0, 0, 0)),
        pl.BlockSpec((1,) + hi.shape[1:], lambda i, *_: (jnp.maximum(i - 2, 0), 0, 0, 0)),
    ]


def each_x(blocks):
    specs = [each(a) for a in blocks]
    return specs[:2] + each_far(blocks[2], blocks[3]) + specs[4:]


def per_expert(kernel, ids, in_specs, args, outs, out_specs, products, mebibytes):
    return pl.pallas_call(
        kernel,
        grid_spec=pltpu.PrefetchScalarGridSpec(
            num_scalar_prefetch=1, grid=(4,), in_specs=in_specs, out_specs=out_specs
        ),
        out_shape=outs,
        compiler_params=pltpu.CompilerParams(vmem_limit_bytes=VMEM_LIMIT),
        cost_estimate=pl.CostEstimate(
            flops=products * (1536 * 192 * 2048 * 3), bytes_accessed=mebibytes << 20, transcendentals=0
        ),
    )(ids, *args)


def near_products(ids, x, weights):
    n_exp, _, rows, _ = x[0].shape
    wide = jax.ShapeDtypeStruct((n_exp, 2 * rows, weights[0].shape[1]), F32)
    args = tuple(x) + tuple(weights)
    specs = [each(a) for a in args]
    return per_expert(near_kernel, ids, specs, args, (wide, wide), (each(wide),) * 2, 2, 14)


def forward(ids, far, near, weights):
    n_exp, _, rows, width = far[0].shape
    n_exp *= 2
    wide = near[0]
    mid = jax.ShapeDtypeStruct(wide.shape, BF)
    out = jax.ShapeDtypeStruct((n_exp, rows, 4 * width), BF)
    outs = (out, out, mid, wide, wide)
    wg, wu, wd = weights
    one = pl.BlockSpec(
        (1, wg.shape[1], width), lambda i, ids: (i, 0, lax.rem(ids[3] + 2, 4))
    )
    specs = each_far(*far) + [each(wide), each(wide), one, one, each(wd)]
    args = tuple(far) + tuple(near) + (wg, wu, wd)
    outs = tuple(jax.ShapeDtypeStruct(o.shape, o.dtype) for o in outs)
    return per_expert(forward_kernel, ids, specs, args, outs, tuple(each(a) for a in outs), 2, 18)


def backward(ids, g, slope, act, weights, mid, shape):
    outs = (mid, mid, jax.ShapeDtypeStruct((4,) + shape, BF))
    args = tuple(g) + (slope, act) + tuple(weights)
    spec = pl.BlockSpec((4, 1) + shape[1:], lambda i, *_: (0, i, 0, 0, 0))
    out_specs = (each(mid), each(mid), spec)
    return per_expert(back_kernel, ids, [each(a) for a in args], args, outs, out_specs, 3, 26)


def weight_grads(ids, x, g, mids, like):
    outs = (jax.ShapeDtypeStruct(like.shape, BF),) * 3
    args = tuple(x) + tuple(g) + tuple(mids)
    specs = each_x(x) + [each(a) for a in tuple(g) + tuple(mids)]
    return per_expert(weights_kernel, ids, specs, args, outs, tuple(each(a) for a in outs), 3, 24)


def regroup_matrix(span):
    n = 4 * span
    line = lax.broadcasted_iota(jnp.int32, (n, 1), 0)
    col = lax.broadcasted_iota(jnp.int32, (n, n), 1)
    swapped = (lax.rem(line // CAP, 4) * 4 + line // span) * CAP + lax.rem(line, CAP)
    return (swapped == col).astype(BF)


def by_expert_kernel(rows_ref, out_ref):
    span = out_ref.shape[2] // 4
    matrix = regroup_matrix(span)
    for i in range(rows_ref.shape[0]):
        rows = nn(matrix, rows_ref[i]).astype(BF)
        y, c = i // 2, i % 2
        for e in range(out_ref.shape[0]):
            out_ref[e, c, y * span : (y + 1) * span] = rows[e * span : (e + 1) * span]


def by_group_kernel(rows_ref, out_ref):
    span = rows_ref.shape[2] // 4
    matrix = regroup_matrix(span)
    for i in range(out_ref.shape[0]):
        y, c = i // 2, i % 2
        rows = [rows_ref[e, c, y * span : (y + 1) * span] for e in range(rows_ref.shape[0])]
        out_ref[i] = tn(matrix, jnp.concatenate(rows, axis=0)).astype(BF)


def regroup(rows, n_exp, to_experts):
    width = rows.shape[-1]
    flat, deep = (8, 4 * n_exp * CAP, width), (n_exp, 2, 16 * CAP, width)
    vmem = pl.BlockSpec(memory_space=pltpu.VMEM)
    return pl.pallas_call(
        by_expert_kernel if to_experts else by_group_kernel,
        out_shape=jax.ShapeDtypeStruct(deep if to_experts else flat, BF),
        in_specs=[vmem],
        out_specs=vmem,
        compiler_params=pltpu.CompilerParams(vmem_limit_bytes=VMEM_LIMIT),
        cost_estimate=pl.CostEstimate(flops=1 << 29, bytes_accessed=3 << 20, transcendentals=0),
    )(rows.reshape(flat if to_experts else deep))


def collect_far(parts, got):
    own, up, down = parts
    got_lo, got_hi = got
    half = got_lo.shape[0]
    up = jnp.concatenate([add(up[:half], got_lo), up[half:]])
    down = jnp.concatenate([down[:half], add(down[half:], got_hi)])
    return own, up, down


def collect_near(parts, axis):
    own, up, down = parts
    return add(own, fetch(up, axis, -1), fetch(down, axis, 1))


def collect_small(parts, axis):
    return add(parts[0], *[fetch(parts[r], axis, -r) for r in (1, 2, 3)])


def ranks(named):
    tok = named.shape[-1]
    earlier = jnp.arange(tok)[:, None] < jnp.arange(tok)[None, :]
    count = jnp.dot(named.astype(BF), earlier.astype(BF), preferred_element_type=F32)
    return jnp.where(named > 0, count, -1.0)


def body(tokens, routes, gates, cotangent, w_gate, w_up, w_down):
    y, c, z, x = (lax.axis_index(a) for a in ("y", "c", "z", "x"))
    ids = jnp.stack([y, z, c, x]).astype(jnp.int32)
    n_exp = w_gate.shape[0]
    total_exp = n_exp * 32
    tok, width = tokens.shape
    weights = (w_gate, w_up, w_down)

    cot = [cotangent] + [fetch(cotangent, "x", r) for r in (1, 2, 3)]
    routes_t = routes.T
    experts_all = jnp.arange(total_exp, dtype=jnp.int32)
    named = jnp.sum((routes_t[:, None, :] == experts_all[None, :, None]).astype(F32), axis=0)
    place = ranks(named).astype(BF)
    slots = total_exp * CAP
    slot = jnp.arange(slots, dtype=jnp.int32)
    repeat = (slot[:, None] // CAP == experts_all[None, :]).astype(BF)
    place_rep = jnp.dot(repeat, place, preferred_element_type=F32)
    own_map = (place_rep == (slot % CAP).astype(F32)[:, None]).astype(BF)

    def exchange(a):
        return lax.all_to_all(a, GROUP, split_axis=0, concat_axis=0, tiled=True)

    came = exchange(jnp.dot(own_map, tokens, preferred_element_type=F32).astype(BF))

    meta = jnp.concatenate([routes_t.astype(BF), gates.T], axis=0)
    meta = jnp.pad(meta, ((0, 0), (0, width - tok)))
    whole = jnp.concatenate(cot + [meta])
    came, whole = lax.optimization_barrier((came, whole))
    whole = lax.all_gather(whole, ("y", "z"))

    came = regroup(came, n_exp, True)
    up, down = fetch(came, "x", 1), fetch(came, "x", -1)
    pair = n_exp // 2
    near = near_products(ids, (came, up, down), weights[:2])
    far = (fetch(down[:pair], "x", -1), fetch(up[pair:], "x", 1))
    x_blocks = (came, up) + far + (down,)
    out_own, out_sib, hidden, slope, act = forward(ids, far, near, weights)

    whole, out_sib = lax.optimization_barrier((whole, out_sib))
    own, sib, maps = pick(ids, whole, n_exp)
    sib, out_sib = lax.optimization_barrier((sib, fetch(out_sib, "c", 1)))

    far = sum_tokens(ids, maps, out_own, out_sib, True)
    sib, far = lax.optimization_barrier((fetch(sib, "c", 1), far))
    got_y = (fetch(far[0], "y", -1), fetch(far[1], "y", 1))
    got_z = (fetch(far[2], "z", -1), fetch(far[3], "z", 1))
    g_blocks = (own, sib)
    mid = jax.ShapeDtypeStruct(hidden.shape, BF)
    grad_a, grad_b, back = backward(ids, g_blocks, slope, act, weights, mid, came.shape)
    back = lax.psum_scatter(back.reshape(-1, width), "x", scatter_dimension=0, tiled=True)

    out_sib, grad_a = lax.optimization_barrier((out_sib, grad_a))
    near = sum_tokens(ids, maps, out_own, out_sib, False)
    near, got_y, got_z = lax.optimization_barrier((near, got_y, got_z))
    ends_y, ends_z = collect_far(near[:3], got_y), collect_far(near[3:], got_z)
    hidden, ends_y, ends_z = lax.optimization_barrier((hidden, ends_y, ends_z))
    grads = weight_grads(ids, x_blocks, g_blocks, (hidden, grad_a, grad_b), w_gate)
    part1, part2 = collect_near(ends_y, "y"), collect_near(ends_z, "z")
    grads, part1, part2 = lax.optimization_barrier((grads, part1, part2))
    part1, part2 = collect_small(part1, "z"), collect_small(part2, "y")

    back, part1, part2 = lax.optimization_barrier((back, part1, part2))
    back = exchange(regroup(back, n_exp, False).reshape(slots, width))
    mixed = collect_small((part1[0], part1[1], part2[0], part2[1]), "x")
    grad_tokens = tn(own_map, back).astype(BF)
    return (mixed, grad_tokens) + tuple(grads)


def solution(mesh):
    split = Mesh(mesh.devices.reshape(4, 2, 4, 4), ("y", "c", "z", "x"))
    acts = P(GROUP, "x")
    rows = P(GROUP, None)
    wts = P(GROUP, "x", None)
    return jax.shard_map(
        body,
        mesh=split,
        in_specs=(acts, rows, rows, acts, wts, wts, wts),
        out_specs=(acts, acts, wts, wts, wts),
        check_vma=False,
    )
```

```python
import functools

import jax
import jax.numpy as jnp
from jax import lax
from jax.experimental import pallas as pl
from jax.experimental.pallas import tpu as pltpu
from jax.sharding import Mesh
from jax.sharding import PartitionSpec as P

BF = jnp.bfloat16
F32 = jnp.float32
CAP = 12
GROUP = ("y", "c", "z")
VMEM_LIMIT = 20 * 1024 * 1024


def fetch(a, axis, r):
    n = lax.axis_size(axis)
    return lax.ppermute(a, axis, [((i + r) % n, i) for i in range(n)])


def add(*terms):
    total = terms[0].astype(F32)
    for term in terms[1:]:
        total = total + term.astype(F32)
    return total.astype(BF)


def nt(a, b):
    return lax.dot_general(a, b, (((1,), (1,)), ((), ())), preferred_element_type=F32)


def tn(a, b):
    return lax.dot_general(a, b, (((0,), (0,)), ((), ())), preferred_element_type=F32)


def nn(a, b):
    return jnp.dot(a, b, preferred_element_type=F32)


def slot_map(ids_ref, meta, n_exp):
    tok = meta[0].shape[1]
    y, z, c = ids_ref[0], ids_ref[1], ids_ref[2]
    top = meta[0].shape[0] // 2
    both = 2 * n_exp
    line = lax.broadcasted_iota(jnp.int32, (both, tok), 0)
    core = jnp.where(line < n_exp, c, 1 - c)
    expert = (y * 2 + core) * 4 + z
    expert = (expert * n_exp + lax.rem(line, n_exp)).astype(F32)
    earlier = (
        lax.broadcasted_iota(jnp.int32, (tok, tok), 0) < lax.broadcasted_iota(jnp.int32, (tok, tok), 1)
    ).astype(BF)
    widen = (
        lax.broadcasted_iota(jnp.int32, (both * 4, both), 0) // 4
        == lax.broadcasted_iota(jnp.int32, (both * 4, both), 1)
    ).astype(BF)
    owner = lax.rem(lax.broadcasted_iota(jnp.int32, (both * 4, tok), 0), 4)
    slots = both * 4 * CAP
    repeat = (
        lax.broadcasted_iota(jnp.int32, (slots, both * 4), 0) // CAP
        == lax.broadcasted_iota(jnp.int32, (slots, both * 4), 1)
    ).astype(BF)
    slot = lax.rem(lax.broadcasted_iota(jnp.int32, (slots, 1), 0), CAP).astype(F32)
    places, gates = [], []
    for zz in range(4):
        data = meta[zz].astype(F32)
        named = jnp.zeros((both, tok), F32)
        gate = jnp.zeros((both, tok), F32)
        for k in range(top):
            same = data[k : k + 1] == expert
            named = jnp.where(same, 1.0, named)
            gate = jnp.where(same, data[top + k : top + k + 1], gate)
        rank = jnp.where(named > 0, nn(named.astype(BF), earlier), -1.0)
        here = owner == zz
        places.append(jnp.where(here, nn(widen, rank.astype(BF)), -1.0).astype(BF))
        gates.append(nn(widen, gate.astype(BF)).astype(BF))
    place = nn(repeat, jnp.concatenate(places, axis=1))
    gate = nn(repeat, jnp.concatenate(gates, axis=1))
    return jnp.where(place == slot, gate, 0.0).astype(BF)


def pick_kernel(ids_ref, whole_ref, own_ref, sib_ref, maps_ref):
    n_exp, span = own_ref.shape[:2]
    tok, width = 128, whole_ref.shape[2]
    n = own_ref.shape[2] // width
    slots = slot_map(ids_ref, [whole_ref[z, n * tok :, :tok] for z in range(4)], n_exp)
    maps_ref[0] = slots
    for r in range(n):
        block = jnp.concatenate([whole_ref[z, r * tok : (r + 1) * tok] for z in range(4)], axis=0)
        picked = nn(slots, block).astype(BF)
        cols = slice(r * width, (r + 1) * width)
        for e in range(n_exp):
            own_ref[e, :, cols] = picked[e * span : (e + 1) * span]
            lo = (n_exp + e) * span
            sib_ref[e, :, cols] = picked[lo : lo + span]


def pick(ids, whole, n_exp):
    width = whole.shape[2]
    span = 4 * CAP
    rows = jax.ShapeDtypeStruct((n_exp, 4 * span, 4 * width), BF)
    maps = jax.ShapeDtypeStruct((4, 2 * n_exp * span, 4 * 128), BF)
    rows_spec = pl.BlockSpec((n_exp, span, 4 * width), lambda i: (0, i, 0))
    return pl.pallas_call(
        pick_kernel,
        grid=(4,),
        out_shape=(rows, rows, maps),
        in_specs=[
            pl.BlockSpec(memory_space=pltpu.SMEM),
            pl.BlockSpec((4,) + whole.shape[1:], lambda i: (i, 0, 0)),
        ],
        out_specs=(rows_spec, rows_spec, pl.BlockSpec((1,) + maps.shape[1:], lambda i: (i, 0, 0))),
        compiler_params=pltpu.CompilerParams(vmem_limit_bytes=VMEM_LIMIT),
        cost_estimate=pl.CostEstimate(flops=4 << 30, bytes_accessed=18 << 20, transcendentals=0),
    )(ids, whole)


def gates_of(ids_ref, map_ref, which):
    tok = 128
    there = [pl.multiple_of(lax.rem(ids_ref[1] + zr, 4) * tok, tok) for zr in which]
    return jnp.concatenate([map_ref[0, :, pl.ds(t, tok)] for t in there], axis=1)


def rows_of(own_ref, sib_ref):
    return jnp.concatenate(
        [ref[e] for ref in (own_ref, sib_ref) for e in range(own_ref.shape[0])], axis=0
    )


def sum_far_kernel(
    ids_ref, map_ref, own_ref, sib_ref, map2_ref, own2_ref, sib2_ref, y_lo, y_hi, z_lo, z_hi
):
    yr = pl.program_id(0)
    tok, width = y_lo.shape[2:]
    gates = gates_of(ids_ref, map_ref, (2,))
    total = tn(gates, rows_of(own_ref, sib_ref)).astype(BF)
    for part, ref in enumerate((z_lo, z_hi)):

        @pl.when(yr // 2 == part)
        def _(ref=ref):
            ref[0, 0], ref[0, 1] = total[:, :width], total[:, width:]

    @pl.when(yr == 0)
    def _():
        rows = rows_of(own2_ref, sib2_ref)
        for part, ref in enumerate((y_lo, y_hi)):
            gates = gates_of(ids_ref, map2_ref, (2 * part, 2 * part + 1))
            total = tn(gates, rows).astype(BF)
            for i in range(2):
                for f in range(2):
                    ref[i, f] = total[i * tok : (i + 1) * tok, f * width : (f + 1) * width]


def sum_near_kernel(ids_ref, map_ref, own_ref, sib_ref, y0, y1, y3, z0, z1, z3):
    yr = pl.program_id(0)
    tok, width = y0.shape[2:]
    rows = rows_of(own_ref, sib_ref)
    near = tn(gates_of(ids_ref, map_ref, (0, 1, 3)), rows[:, 2 * width :]).astype(BF)
    for i, ref in enumerate((z0, z1, z3)):
        for f in range(2):
            ref[0, f] = near[i * tok : (i + 1) * tok, f * width : (f + 1) * width]

    @pl.when(yr != 2)
    def _():
        total = tn(gates_of(ids_ref, map_ref, range(4)), rows[:, : 2 * width]).astype(BF)
        for i, ref in ((0, y0), (1, y1), (3, y3)):

            @pl.when(yr == i)
            def _(ref=ref):
                for zr in range(4):
                    for f in range(2):
                        ref[zr, f] = total[zr * tok : (zr + 1) * tok, f * width : (f + 1) * width]


def sum_tokens(ids, maps, own, sib, far):
    n_exp, rows, cols = own.shape
    whole = jax.ShapeDtypeStruct((4, 2, 128, cols // 4), BF)
    half = jax.ShapeDtypeStruct((2,) + whole.shape[1:], BF)
    at = lambda i, ids: lax.rem(ids[0] + i, 4)
    block = (1,) + whole.shape[1:]
    keep = lambda a: pl.BlockSpec(a.shape, lambda i, ids: (0,) * 4)
    each_y = pl.BlockSpec(block, lambda i, ids: (i, 0, 0, 0))
    first = pl.BlockSpec(block, lambda i, ids: (jnp.minimum(i, 1), 0, 0, 0))
    last = pl.BlockSpec(block, lambda i, ids: (jnp.maximum(i - 2, 0), 0, 0, 0))
    one_map = (1,) + maps.shape[1:]
    map_y = pl.BlockSpec(one_map, lambda i, ids: (at(i, ids), 0, 0))
    map_2 = pl.BlockSpec(one_map, lambda i, ids: (at(2, ids), 0, 0))
    rows_y = pl.BlockSpec((n_exp, rows // 4, cols), lambda i, ids: (0, at(i, ids), 0))
    some = (n_exp, rows // 4, cols // 2)
    rows_z = pl.BlockSpec(some, lambda i, ids: (0, at(i, ids), 1))
    rows_2 = pl.BlockSpec(some, lambda i, ids: (0, at(2, ids), 0))

    def call(kernel, in_specs, args, outs, out_specs, flops):
        return pl.pallas_call(
            kernel,
            grid_spec=pltpu.PrefetchScalarGridSpec(
                num_scalar_prefetch=1, grid=(4,), in_specs=in_specs, out_specs=out_specs
            ),
            out_shape=outs,
            compiler_params=pltpu.CompilerParams(vmem_limit_bytes=VMEM_LIMIT),
            cost_estimate=pl.CostEstimate(flops=flops, bytes_accessed=flops >> 8, transcendentals=0),
        )(ids, *args)

    if far:
        return call(
            sum_far_kernel,
            [map_y, rows_z, rows_z, map_2, rows_2, rows_2],
            (maps, own, sib) * 2,
            (half,) * 4,
            (keep(half), keep(half), first, last),
            1 << 30,
        )
    return call(
        sum_near_kernel,
        [map_y, rows_y, rows_y],
        (maps, own, sib),
        (whole,) * 6,
        (keep(whole),) * 3 + (each_y,) * 3,
        3 << 30,
    )


def moved_columns(me, n, width):
    return [pl.ds(pl.multiple_of(lax.rem(me + r, n) * width, width), width) for r in range(n)]


def both_cores(c, ref):
    return jnp.concatenate([ref[0, c], ref[0, 1 - c]], axis=0)


def far_rows(c, lo, hi):
    return jnp.where(pl.program_id(0) < 2, both_cores(c, lo), both_cores(c, hi))


def x_rows_of(c, refs):
    x0, x1, lo, hi, x3 = refs
    return [both_cores(c, x0), both_cores(c, x1), far_rows(c, lo, hi), both_cores(c, x3)]


def near_kernel(ids_ref, x0, x1, x3, wg, wu, a_ref, b_ref):
    c = ids_ref[2]
    n, width = 4, x0.shape[3]
    moved = moved_columns(ids_ref[3], n, width)
    blocks = [(0, both_cores(c, x0)), (1, both_cores(c, x1)), (3, both_cores(c, x3))]
    a_ref[0] = sum(nt(rows, wg[0, :, moved[r]]) for r, rows in blocks)
    b_ref[0] = sum(nt(rows, wu[0, :, moved[r]]) for r, rows in blocks)


def forward_kernel(ids_ref, lo, hi, a_ref, b_ref, wg2, wu2, wd, oo, os, hid_ref, slope_ref, act_ref):
    half, cols = oo.shape[1:]
    n, width = 4, cols // 4
    moved = moved_columns(ids_ref[3], n, width)
    far = far_rows(ids_ref[2], lo, hi)
    a = a_ref[0] + nt(far, wg2[0])
    b = b_ref[0] + nt(far, wu2[0])
    s = jax.nn.sigmoid(a)
    act = a * s
    hidden = (act * b).astype(BF)
    hid_ref[0] = hidden
    slope_ref[0] = b * s * (1.0 + a * (1.0 - s))
    act_ref[0] = act
    for r in range(n):
        out = nn(hidden, wd[0, :, moved[r]]).astype(BF)
        oo[0, :, r * width : (r + 1) * width] = out[:half]
        os[0, :, r * width : (r + 1) * width] = out[half:]


def back_kernel(ids_ref, own, sib, slope_ref, act_ref, wg, wu, wd, da_ref, db_ref, back_ref):
    c = ids_ref[2]
    n = back_ref.shape[0]
    half, width = back_ref.shape[3:]
    moved = moved_columns(ids_ref[3], n, width)
    fixed = [slice(r * width, (r + 1) * width) for r in range(n)]
    g_rows = [jnp.concatenate([own[0, :, f], sib[0, :, f]], axis=0) for f in fixed]
    gh = sum(nt(g_rows[r], wd[0, :, moved[r]]) for r in range(n))
    da = (gh * slope_ref[0]).astype(BF)
    db = (gh * act_ref[0]).astype(BF)
    da_ref[0] = da
    db_ref[0] = db
    for r in range(n):
        back = (nn(da, wg[0, :, fixed[r]]) + nn(db, wu[0, :, fixed[r]])).astype(BF)
        back_ref[r, 0, c] = back[:half]
        back_ref[r, 0, 1 - c] = back[half:]


def weights_kernel(ids_ref, *refs):
    x_refs, refs = refs[:5], refs[5:]
    own, sib, hid_ref, da_ref, db_ref, dwg, dwu, dwd = refs
    cols = own.shape[2]
    n, width = 4, cols // 4
    fixed = [slice(r * width, (r + 1) * width) for r in range(n)]
    moved = moved_columns(ids_ref[3], n, width)
    x_rows = x_rows_of(ids_ref[2], x_refs)
    hidden, da, db = hid_ref[0], da_ref[0], db_ref[0]
    for r in range(n):
        g_rows = jnp.concatenate([own[0, :, fixed[r]], sib[0, :, fixed[r]]], axis=0)
        dwg[0, :, moved[r]] = tn(da, x_rows[r]).astype(BF)
        dwu[0, :, moved[r]] = tn(db, x_rows[r]).astype(BF)
        dwd[0, :, moved[r]] = tn(hidden, g_rows).astype(BF)


def each(a):
    return pl.BlockSpec((1,) + a.shape[1:], lambda i, *_: (i,) + (0,) * (len(a.shape) - 1))


def each_far(lo, hi):
    return [
        pl.BlockSpec((1,) + lo.shape[1:], lambda i, *_: (jnp.minimum(i, 1), 0, 0, 0)),
        pl.BlockSpec((1,) + hi.shape[1:], lambda i, *_: (jnp.maximum(i - 2, 0), 0, 0, 0)),
    ]


def each_x(blocks):
    specs = [each(a) for a in blocks]
    return specs[:2] + each_far(blocks[2], blocks[3]) + specs[4:]


def per_expert(kernel, ids, in_specs, args, outs, out_specs, products, mebibytes):
    return pl.pallas_call(
        kernel,
        grid_spec=pltpu.PrefetchScalarGridSpec(
            num_scalar_prefetch=1, grid=(4,), in_specs=in_specs, out_specs=out_specs
        ),
        out_shape=outs,
        compiler_params=pltpu.CompilerParams(vmem_limit_bytes=VMEM_LIMIT),
        cost_estimate=pl.CostEstimate(
            flops=products * (1536 * 192 * 2048 * 3), bytes_accessed=mebibytes << 20, transcendentals=0
        ),
    )(ids, *args)


def near_products(ids, x, weights):
    n_exp, _, rows, _ = x[0].shape
    wide = jax.ShapeDtypeStruct((n_exp, 2 * rows, weights[0].shape[1]), F32)
    args = tuple(x) + tuple(weights)
    specs = [each(a) for a in args]
    return per_expert(near_kernel, ids, specs, args, (wide, wide), (each(wide),) * 2, 2, 14)


def forward(ids, far, near, weights):
    n_exp, _, rows, width = far[0].shape
    n_exp *= 2
    wide = near[0]
    mid = jax.ShapeDtypeStruct(wide.shape, BF)
    out = jax.ShapeDtypeStruct((n_exp, rows, 4 * width), BF)
    outs = (out, out, mid, wide, wide)
    wg, wu, wd = weights
    one = pl.BlockSpec(
        (1, wg.shape[1], width), lambda i, ids: (i, 0, lax.rem(ids[3] + 2, 4))
    )
    specs = each_far(*far) + [each(wide), each(wide), one, one, each(wd)]
    args = tuple(far) + tuple(near) + (wg, wu, wd)
    outs = tuple(jax.ShapeDtypeStruct(o.shape, o.dtype) for o in outs)
    return per_expert(forward_kernel, ids, specs, args, outs, tuple(each(a) for a in outs), 2, 18)


def backward(ids, g, slope, act, weights, mid, shape):
    outs = (mid, mid, jax.ShapeDtypeStruct((4,) + shape, BF))
    args = tuple(g) + (slope, act) + tuple(weights)
    spec = pl.BlockSpec((4, 1) + shape[1:], lambda i, *_: (0, i, 0, 0, 0))
    out_specs = (each(mid), each(mid), spec)
    return per_expert(back_kernel, ids, [each(a) for a in args], args, outs, out_specs, 3, 26)


def weight_grads(ids, x, g, mids, like):
    outs = (jax.ShapeDtypeStruct(like.shape, BF),) * 3
    args = tuple(x) + tuple(g) + tuple(mids)
    specs = each_x(x) + [each(a) for a in tuple(g) + tuple(mids)]
    return per_expert(weights_kernel, ids, specs, args, outs, tuple(each(a) for a in outs), 3, 24)


def regroup_matrix(span):
    n = 4 * span
    line = lax.broadcasted_iota(jnp.int32, (n, 1), 0)
    col = lax.broadcasted_iota(jnp.int32, (n, n), 1)
    swapped = (lax.rem(line // CAP, 4) * 4 + line // span) * CAP + lax.rem(line, CAP)
    return (swapped == col).astype(BF)


def by_expert_kernel(rows_ref, out_ref):
    span = out_ref.shape[2] // 4
    matrix = regroup_matrix(span)
    for i in range(rows_ref.shape[0]):
        rows = nn(matrix, rows_ref[i]).astype(BF)
        y, c = i // 2, i % 2
        for e in range(out_ref.shape[0]):
            out_ref[e, c, y * span : (y + 1) * span] = rows[e * span : (e + 1) * span]


def by_group_kernel(rows_ref, out_ref):
    span = rows_ref.shape[2] // 4
    matrix = regroup_matrix(span)
    for i in range(out_ref.shape[0]):
        y, c = i // 2, i % 2
        rows = [rows_ref[e, c, y * span : (y + 1) * span] for e in range(rows_ref.shape[0])]
        out_ref[i] = tn(matrix, jnp.concatenate(rows, axis=0)).astype(BF)


def regroup(rows, n_exp, to_experts):
    width = rows.shape[-1]
    flat, deep = (8, 4 * n_exp * CAP, width), (n_exp, 2, 16 * CAP, width)
    vmem = pl.BlockSpec(memory_space=pltpu.VMEM)
    return pl.pallas_call(
        by_expert_kernel if to_experts else by_group_kernel,
        out_shape=jax.ShapeDtypeStruct(deep if to_experts else flat, BF),
        in_specs=[vmem],
        out_specs=vmem,
        compiler_params=pltpu.CompilerParams(vmem_limit_bytes=VMEM_LIMIT),
        cost_estimate=pl.CostEstimate(flops=1 << 29, bytes_accessed=3 << 20, transcendentals=0),
    )(rows.reshape(flat if to_experts else deep))


def collect_far(parts, got):
    own, up, down = parts
    got_lo, got_hi = got
    half = got_lo.shape[0]
    up = jnp.concatenate([add(up[:half], got_lo), up[half:]])
    down = jnp.concatenate([down[:half], add(down[half:], got_hi)])
    return own, up, down


def collect_near(parts, axis):
    own, up, down = parts
    return add(own, fetch(up, axis, -1), fetch(down, axis, 1))


def collect_small(parts, axis):
    return add(parts[0], *[fetch(parts[r], axis, -r) for r in (1, 2, 3)])


def ranks(named):
    tok = named.shape[-1]
    earlier = jnp.arange(tok)[:, None] < jnp.arange(tok)[None, :]
    count = jnp.dot(named.astype(BF), earlier.astype(BF), preferred_element_type=F32)
    return jnp.where(named > 0, count, -1.0)


def body(tokens, routes, gates, cotangent, w_gate, w_up, w_down):
    y, c, z, x = (lax.axis_index(a) for a in ("y", "c", "z", "x"))
    ids = jnp.stack([y, z, c, x]).astype(jnp.int32)
    n_exp = w_gate.shape[0]
    total_exp = n_exp * 32
    tok, width = tokens.shape
    weights = (w_gate, w_up, w_down)

    cot = [cotangent] + [fetch(cotangent, "x", r) for r in (1, 2, 3)]
    routes_t = routes.T
    experts_all = jnp.arange(total_exp, dtype=jnp.int32)
    named = jnp.sum((routes_t[:, None, :] == experts_all[None, :, None]).astype(F32), axis=0)
    place = ranks(named).astype(BF)
    slots = total_exp * CAP
    slot = jnp.arange(slots, dtype=jnp.int32)
    repeat = (slot[:, None] // CAP == experts_all[None, :]).astype(BF)
    place_rep = jnp.dot(repeat, place, preferred_element_type=F32)
    own_map = (place_rep == (slot % CAP).astype(F32)[:, None]).astype(BF)

    def exchange(a):
        return lax.all_to_all(a, GROUP, split_axis=0, concat_axis=0, tiled=True)

    came = exchange(jnp.dot(own_map, tokens, preferred_element_type=F32).astype(BF))

    meta = jnp.concatenate([routes_t.astype(BF), gates.T], axis=0)
    meta = jnp.pad(meta, ((0, 0), (0, width - tok)))
    whole = jnp.concatenate(cot + [meta])
    came, whole = lax.optimization_barrier((came, whole))
    whole = lax.all_gather(whole, ("y", "z"))

    came = regroup(came, n_exp, True)
    up, down = fetch(came, "x", 1), fetch(came, "x", -1)
    pair = n_exp // 2
    near = near_products(ids, (came, up, down), weights[:2])
    far = (fetch(down[:pair], "x", -1), fetch(up[pair:], "x", 1))
    x_blocks = (came, up) + far + (down,)
    out_own, out_sib, hidden, slope, act = forward(ids, far, near, weights)

    whole, out_sib = lax.optimization_barrier((whole, out_sib))
    own, sib, maps = pick(ids, whole, n_exp)
    sib, out_sib = lax.optimization_barrier((sib, fetch(out_sib, "c", 1)))

    far = sum_tokens(ids, maps, out_own, out_sib, True)
    sib, far = lax.optimization_barrier((fetch(sib, "c", 1), far))
    got_y = (fetch(far[0], "y", -1), fetch(far[1], "y", 1))
    got_z = (fetch(far[2], "z", -1), fetch(far[3], "z", 1))
    g_blocks = (own, sib)
    mid = jax.ShapeDtypeStruct(hidden.shape, BF)
    grad_a, grad_b, back = backward(ids, g_blocks, slope, act, weights, mid, came.shape)
    back = lax.psum_scatter(back.reshape(-1, width), "x", scatter_dimension=0, tiled=True)

    out_sib, grad_a = lax.optimization_barrier((out_sib, grad_a))
    near = sum_tokens(ids, maps, out_own, out_sib, False)
    near, got_y, got_z = lax.optimization_barrier((near, got_y, got_z))
    ends_y, ends_z = collect_far(near[:3], got_y), collect_far(near[3:], got_z)
    hidden, ends_y, ends_z = lax.optimization_barrier((hidden, ends_y, ends_z))
    grads = weight_grads(ids, x_blocks, g_blocks, (hidden, grad_a, grad_b), w_gate)
    part1, part2 = collect_near(ends_y, "y"), collect_near(ends_z, "z")
    grads, part1, part2 = lax.optimization_barrier((grads, part1, part2))
    part1, part2 = collect_small(part1, "z"), collect_small(part2, "y")

    back, part1, part2 = lax.optimization_barrier((back, part1, part2))
    back = exchange(regroup(back, n_exp, False).reshape(slots, width))
    mixed = collect_small((part1[0], part1[1], part2[0], part2[1]), "x")
    grad_tokens = tn(own_map, back).astype(BF)
    return (mixed, grad_tokens) + tuple(grads)


def solution(mesh):
    split = Mesh(mesh.devices.reshape(4, 2, 4, 4), ("y", "c", "z", "x"))
    acts = P(GROUP, "x")
    rows = P(GROUP, None)
    wts = P(GROUP, "x", None)
    return jax.shard_map(
        body,
        mesh=split,
        in_specs=(acts, rows, rows, acts, wts, wts, wts),
        out_specs=(acts, acts, wts, wts, wts),
        check_vma=False,
    )
```

```python
import functools

import jax
import jax.numpy as jnp
from jax import lax
from jax.experimental import pallas as pl
from jax.experimental.pallas import tpu as pltpu
from jax.sharding import Mesh
from jax.sharding import PartitionSpec as P

BF = jnp.bfloat16
F32 = jnp.float32
CAP = 12
GROUP = ("y", "c", "z")
VMEM_LIMIT = 36 * 1024 * 1024


def fetch(a, axis, r):
    n = lax.axis_size(axis)
    return lax.ppermute(a, axis, [((i + r) % n, i) for i in range(n)])


def add(*terms):
    total = terms[0].astype(F32)
    for term in terms[1:]:
        total = total + term.astype(F32)
    return total.astype(BF)


def nt(a, b):
    return lax.dot_general(a, b, (((1,), (1,)), ((), ())), preferred_element_type=F32)


def tn(a, b):
    return lax.dot_general(a, b, (((0,), (0,)), ((), ())), preferred_element_type=F32)


def nn(a, b):
    return jnp.dot(a, b, preferred_element_type=F32)


def slot_map(ids_ref, meta, n_exp):
    tok = meta[0].shape[1]
    y, z, c = ids_ref[0], ids_ref[1], ids_ref[2]
    top = meta[0].shape[0] // 2
    both = 2 * n_exp
    line = lax.broadcasted_iota(jnp.int32, (both, tok), 0)
    core = jnp.where(line < n_exp, c, 1 - c)
    expert = (y * 2 + core) * 4 + z
    expert = (expert * n_exp + lax.rem(line, n_exp)).astype(F32)
    earlier = (
        lax.broadcasted_iota(jnp.int32, (tok, tok), 0) < lax.broadcasted_iota(jnp.int32, (tok, tok), 1)
    ).astype(BF)
    widen = (
        lax.broadcasted_iota(jnp.int32, (both * 4, both), 0) // 4
        == lax.broadcasted_iota(jnp.int32, (both * 4, both), 1)
    ).astype(BF)
    owner = lax.rem(lax.broadcasted_iota(jnp.int32, (both * 4, tok), 0), 4)
    slots = both * 4 * CAP
    repeat = (
        lax.broadcasted_iota(jnp.int32, (slots, both * 4), 0) // CAP
        == lax.broadcasted_iota(jnp.int32, (slots, both * 4), 1)
    ).astype(BF)
    slot = lax.rem(lax.broadcasted_iota(jnp.int32, (slots, 1), 0), CAP).astype(F32)
    places, gates = [], []
    for zz in range(4):
        data = meta[zz].astype(F32)
        named = jnp.zeros((both, tok), F32)
        gate = jnp.zeros((both, tok), F32)
        for k in range(top):
            same = data[k : k + 1] == expert
            named = jnp.where(same, 1.0, named)
            gate = jnp.where(same, data[top + k : top + k + 1], gate)
        rank = jnp.where(named > 0, nn(named.astype(BF), earlier), -1.0)
        here = owner == zz
        places.append(jnp.where(here, nn(widen, rank.astype(BF)), -1.0).astype(BF))
        gates.append(nn(widen, gate.astype(BF)).astype(BF))
    place = nn(repeat, jnp.concatenate(places, axis=1))
    gate = nn(repeat, jnp.concatenate(gates, axis=1))
    return jnp.where(place == slot, gate, 0.0).astype(BF)


def pick_kernel(ids_ref, whole_ref, own_ref, sib_ref, maps_ref):
    n_exp, span = own_ref.shape[:2]
    tok, width = 128, whole_ref.shape[2]
    n = own_ref.shape[2] // width
    slots = slot_map(ids_ref, [whole_ref[z, n * tok :, :tok] for z in range(4)], n_exp)
    maps_ref[0] = slots
    for r in range(n):
        block = jnp.concatenate([whole_ref[z, r * tok : (r + 1) * tok] for z in range(4)], axis=0)
        picked = nn(slots, block).astype(BF)
        cols = slice(r * width, (r + 1) * width)
        for e in range(n_exp):
            own_ref[e, :, cols] = picked[e * span : (e + 1) * span]
            lo = (n_exp + e) * span
            sib_ref[e, :, cols] = picked[lo : lo + span]


def pick(ids, whole, n_exp):
    width = whole.shape[2]
    span = 4 * CAP
    rows = jax.ShapeDtypeStruct((n_exp, 4 * span, 4 * width), BF)
    maps = jax.ShapeDtypeStruct((4, 2 * n_exp * span, 4 * 128), BF)
    rows_spec = pl.BlockSpec((n_exp, span, 4 * width), lambda i: (0, i, 0))
    return pl.pallas_call(
        pick_kernel,
        grid=(4,),
        out_shape=(rows, rows, maps),
        in_specs=[
            pl.BlockSpec(memory_space=pltpu.SMEM),
            pl.BlockSpec((4,) + whole.shape[1:], lambda i: (i, 0, 0)),
        ],
        out_specs=(rows_spec, rows_spec, pl.BlockSpec((1,) + maps.shape[1:], lambda i: (i, 0, 0))),
        compiler_params=pltpu.CompilerParams(vmem_limit_bytes=VMEM_LIMIT),
        cost_estimate=pl.CostEstimate(flops=4 << 30, bytes_accessed=18 << 20, transcendentals=0),
    )(ids, whole)


def gates_of(ids_ref, map_ref, which):
    tok = 128
    there = [pl.multiple_of(lax.rem(ids_ref[1] + zr, 4) * tok, tok) for zr in which]
    return jnp.concatenate([map_ref[0, :, pl.ds(t, tok)] for t in there], axis=1)


def rows_of(own_ref, sib_ref):
    return jnp.concatenate(
        [ref[e] for ref in (own_ref, sib_ref) for e in range(own_ref.shape[0])], axis=0
    )


def sum_far_kernel(
    ids_ref, map_ref, own_ref, sib_ref, map2_ref, own2_ref, sib2_ref, y_lo, y_hi, z_lo, z_hi
):
    yr = pl.program_id(0)
    tok, width = y_lo.shape[2:]
    gates = gates_of(ids_ref, map_ref, (2,))
    total = tn(gates, rows_of(own_ref, sib_ref)).astype(BF)
    for part, ref in enumerate((z_lo, z_hi)):

        @pl.when(yr // 2 == part)
        def _(ref=ref):
            ref[0, 0], ref[0, 1] = total[:, :width], total[:, width:]

    @pl.when(yr == 0)
    def _():
        rows = rows_of(own2_ref, sib2_ref)
        for part, ref in enumerate((y_lo, y_hi)):
            gates = gates_of(ids_ref, map2_ref, (2 * part, 2 * part + 1))
            total = tn(gates, rows).astype(BF)
            for i in range(2):
                for f in range(2):
                    ref[i, f] = total[i * tok : (i + 1) * tok, f * width : (f + 1) * width]


def sum_near_kernel(ids_ref, map_ref, own_ref, sib_ref, y0, y1, y3, z0, z1, z3):
    yr = pl.program_id(0)
    tok, width = y0.shape[2:]
    rows = rows_of(own_ref, sib_ref)
    near = tn(gates_of(ids_ref, map_ref, (0, 1, 3)), rows[:, 2 * width :]).astype(BF)
    for i, ref in enumerate((z0, z1, z3)):
        for f in range(2):
            ref[0, f] = near[i * tok : (i + 1) * tok, f * width : (f + 1) * width]

    @pl.when(yr != 2)
    def _():
        total = tn(gates_of(ids_ref, map_ref, range(4)), rows[:, : 2 * width]).astype(BF)
        for i, ref in ((0, y0), (1, y1), (3, y3)):

            @pl.when(yr == i)
            def _(ref=ref):
                for zr in range(4):
                    for f in range(2):
                        ref[zr, f] = total[zr * tok : (zr + 1) * tok, f * width : (f + 1) * width]


def sum_tokens(ids, maps, own, sib, far):
    n_exp, rows, cols = own.shape
    whole = jax.ShapeDtypeStruct((4, 2, 128, cols // 4), BF)
    half = jax.ShapeDtypeStruct((2,) + whole.shape[1:], BF)
    at = lambda i, ids: lax.rem(ids[0] + i, 4)
    block = (1,) + whole.shape[1:]
    keep = lambda a: pl.BlockSpec(a.shape, lambda i, ids: (0,) * 4)
    each_y = pl.BlockSpec(block, lambda i, ids: (i, 0, 0, 0))
    first = pl.BlockSpec(block, lambda i, ids: (jnp.minimum(i, 1), 0, 0, 0))
    last = pl.BlockSpec(block, lambda i, ids: (jnp.maximum(i - 2, 0), 0, 0, 0))
    one_map = (1,) + maps.shape[1:]
    map_y = pl.BlockSpec(one_map, lambda i, ids: (at(i, ids), 0, 0))
    map_2 = pl.BlockSpec(one_map, lambda i, ids: (at(2, ids), 0, 0))
    rows_y = pl.BlockSpec((n_exp, rows // 4, cols), lambda i, ids: (0, at(i, ids), 0))
    some = (n_exp, rows // 4, cols // 2)
    rows_z = pl.BlockSpec(some, lambda i, ids: (0, at(i, ids), 1))
    rows_2 = pl.BlockSpec(some, lambda i, ids: (0, at(2, ids), 0))

    def call(kernel, in_specs, args, outs, out_specs, flops):
        return pl.pallas_call(
            kernel,
            grid_spec=pltpu.PrefetchScalarGridSpec(
                num_scalar_prefetch=1, grid=(4,), in_specs=in_specs, out_specs=out_specs
            ),
            out_shape=outs,
            compiler_params=pltpu.CompilerParams(vmem_limit_bytes=VMEM_LIMIT),
            cost_estimate=pl.CostEstimate(flops=flops, bytes_accessed=flops >> 8, transcendentals=0),
        )(ids, *args)

    if far:
        return call(
            sum_far_kernel,
            [map_y, rows_z, rows_z, map_2, rows_2, rows_2],
            (maps, own, sib) * 2,
            (half,) * 4,
            (keep(half), keep(half), first, last),
            1 << 30,
        )
    return call(
        sum_near_kernel,
        [map_y, rows_y, rows_y],
        (maps, own, sib),
        (whole,) * 6,
        (keep(whole),) * 3 + (each_y,) * 3,
        3 << 30,
    )


def moved_columns(me, n, width):
    return [pl.ds(pl.multiple_of(lax.rem(me + r, n) * width, width), width) for r in range(n)]


def both_cores(c, ref):
    return jnp.concatenate([ref[0, c], ref[0, 1 - c]], axis=0)


def far_rows(c, lo, hi):
    return jnp.where(pl.program_id(0) < 2, both_cores(c, lo), both_cores(c, hi))


def x_rows_of(c, refs):
    x0, x1, lo, hi, x3 = refs
    return [both_cores(c, x0), both_cores(c, x1), far_rows(c, lo, hi), both_cores(c, x3)]


def near_kernel(ids_ref, x0, x1, x3, wg, wu, a_ref, b_ref):
    c = ids_ref[2]
    n, width = 4, x0.shape[3]
    moved = moved_columns(ids_ref[3], n, width)
    blocks = [(0, both_cores(c, x0)), (1, both_cores(c, x1)), (3, both_cores(c, x3))]
    a_ref[0] = sum(nt(rows, wg[0, :, moved[r]]) for r, rows in blocks)
    b_ref[0] = sum(nt(rows, wu[0, :, moved[r]]) for r, rows in blocks)


def forward_kernel(ids_ref, lo, hi, a_ref, b_ref, wg2, wu2, wd, oo, os, hid_ref, slope_ref, act_ref):
    half, cols = oo.shape[1:]
    n, width = 4, cols // 4
    moved = moved_columns(ids_ref[3], n, width)
    far = far_rows(ids_ref[2], lo, hi)
    a = a_ref[0] + nt(far, wg2[0])
    b = b_ref[0] + nt(far, wu2[0])
    s = jax.nn.sigmoid(a)
    act = a * s
    hidden = (act * b).astype(BF)
    hid_ref[0] = hidden
    slope_ref[0] = b * s * (1.0 + a * (1.0 - s))
    act_ref[0] = act
    for r in range(n):
        out = nn(hidden, wd[0, :, moved[r]]).astype(BF)
        oo[0, :, r * width : (r + 1) * width] = out[:half]
        os[0, :, r * width : (r + 1) * width] = out[half:]


def back_kernel(ids_ref, own, sib, slope_ref, act_ref, wg, wu, wd, da_ref, db_ref, back_ref):
    c = ids_ref[2]
    n = back_ref.shape[0]
    half, width = back_ref.shape[3:]
    moved = moved_columns(ids_ref[3], n, width)
    fixed = [slice(r * width, (r + 1) * width) for r in range(n)]
    g_rows = [jnp.concatenate([own[0, :, f], sib[0, :, f]], axis=0) for f in fixed]
    gh = sum(nt(g_rows[r], wd[0, :, moved[r]]) for r in range(n))
    da = (gh * slope_ref[0]).astype(BF)
    db = (gh * act_ref[0]).astype(BF)
    da_ref[0] = da
    db_ref[0] = db
    for r in range(n):
        back = (nn(da, wg[0, :, fixed[r]]) + nn(db, wu[0, :, fixed[r]])).astype(BF)
        back_ref[r, 0, c] = back[:half]
        back_ref[r, 0, 1 - c] = back[half:]


def weights_kernel(ids_ref, *refs):
    x_refs, refs = refs[:5], refs[5:]
    own, sib, hid_ref, da_ref, db_ref, dwg, dwu, dwd = refs
    cols = own.shape[2]
    n, width = 4, cols // 4
    fixed = [slice(r * width, (r + 1) * width) for r in range(n)]
    moved = moved_columns(ids_ref[3], n, width)
    x_rows = x_rows_of(ids_ref[2], x_refs)
    hidden, da, db = hid_ref[0], da_ref[0], db_ref[0]
    for r in range(n):
        g_rows = jnp.concatenate([own[0, :, fixed[r]], sib[0, :, fixed[r]]], axis=0)
        dwg[0, :, moved[r]] = tn(da, x_rows[r]).astype(BF)
        dwu[0, :, moved[r]] = tn(db, x_rows[r]).astype(BF)
        dwd[0, :, moved[r]] = tn(hidden, g_rows).astype(BF)


def each(a):
    return pl.BlockSpec((1,) + a.shape[1:], lambda i, *_: (i,) + (0,) * (len(a.shape) - 1))


def each_far(lo, hi):
    return [
        pl.BlockSpec((1,) + lo.shape[1:], lambda i, *_: (jnp.minimum(i, 1), 0, 0, 0)),
        pl.BlockSpec((1,) + hi.shape[1:], lambda i, *_: (jnp.maximum(i - 2, 0), 0, 0, 0)),
    ]


def each_x(blocks):
    specs = [each(a) for a in blocks]
    return specs[:2] + each_far(blocks[2], blocks[3]) + specs[4:]


def per_expert(kernel, ids, in_specs, args, outs, out_specs, products, mebibytes):
    return pl.pallas_call(
        kernel,
        grid_spec=pltpu.PrefetchScalarGridSpec(
            num_scalar_prefetch=1, grid=(4,), in_specs=in_specs, out_specs=out_specs
        ),
        out_shape=outs,
        compiler_params=pltpu.CompilerParams(vmem_limit_bytes=VMEM_LIMIT),
        cost_estimate=pl.CostEstimate(
            flops=products * (1536 * 192 * 2048 * 3), bytes_accessed=mebibytes << 20, transcendentals=0
        ),
    )(ids, *args)


def near_products(ids, x, weights):
    n_exp, _, rows, _ = x[0].shape
    wide = jax.ShapeDtypeStruct((n_exp, 2 * rows, weights[0].shape[1]), F32)
    args = tuple(x) + tuple(weights)
    specs = [each(a) for a in args]
    return per_expert(near_kernel, ids, specs, args, (wide, wide), (each(wide),) * 2, 2, 14)


def forward(ids, far, near, weights):
    n_exp, _, rows, width = far[0].shape
    n_exp *= 2
    wide = near[0]
    mid = jax.ShapeDtypeStruct(wide.shape, BF)
    out = jax.ShapeDtypeStruct((n_exp, rows, 4 * width), BF)
    outs = (out, out, mid, wide, wide)
    wg, wu, wd = weights
    one = pl.BlockSpec(
        (1, wg.shape[1], width), lambda i, ids: (i, 0, lax.rem(ids[3] + 2, 4))
    )
    specs = each_far(*far) + [each(wide), each(wide), one, one, each(wd)]
    args = tuple(far) + tuple(near) + (wg, wu, wd)
    outs = tuple(jax.ShapeDtypeStruct(o.shape, o.dtype) for o in outs)
    return per_expert(forward_kernel, ids, specs, args, outs, tuple(each(a) for a in outs), 2, 18)


def backward(ids, g, slope, act, weights, mid, shape):
    outs = (mid, mid, jax.ShapeDtypeStruct((4,) + shape, BF))
    args = tuple(g) + (slope, act) + tuple(weights)
    spec = pl.BlockSpec((4, 1) + shape[1:], lambda i, *_: (0, i, 0, 0, 0))
    out_specs = (each(mid), each(mid), spec)
    return per_expert(back_kernel, ids, [each(a) for a in args], args, outs, out_specs, 3, 26)


def weight_grads(ids, x, g, mids, like):
    outs = (jax.ShapeDtypeStruct(like.shape, BF),) * 3
    args = tuple(x) + tuple(g) + tuple(mids)
    specs = each_x(x) + [each(a) for a in tuple(g) + tuple(mids)]
    return per_expert(weights_kernel, ids, specs, args, outs, tuple(each(a) for a in outs), 3, 24)


def regroup_matrix(span):
    n = 4 * span
    line = lax.broadcasted_iota(jnp.int32, (n, 1), 0)
    col = lax.broadcasted_iota(jnp.int32, (n, n), 1)
    swapped = (lax.rem(line // CAP, 4) * 4 + line // span) * CAP + lax.rem(line, CAP)
    return (swapped == col).astype(BF)


def by_expert_kernel(rows_ref, out_ref):
    span = out_ref.shape[2] // 4
    matrix = regroup_matrix(span)
    for i in range(rows_ref.shape[0]):
        rows = nn(matrix, rows_ref[i]).astype(BF)
        y, c = i // 2, i % 2
        for e in range(out_ref.shape[0]):
            out_ref[e, c, y * span : (y + 1) * span] = rows[e * span : (e + 1) * span]


def by_group_kernel(rows_ref, out_ref):
    span = rows_ref.shape[2] // 4
    matrix = regroup_matrix(span)
    for i in range(out_ref.shape[0]):
        y, c = i // 2, i % 2
        rows = [rows_ref[e, c, y * span : (y + 1) * span] for e in range(rows_ref.shape[0])]
        out_ref[i] = tn(matrix, jnp.concatenate(rows, axis=0)).astype(BF)


def regroup(rows, n_exp, to_experts):
    width = rows.shape[-1]
    flat, deep = (8, 4 * n_exp * CAP, width), (n_exp, 2, 16 * CAP, width)
    vmem = pl.BlockSpec(memory_space=pltpu.VMEM)
    return pl.pallas_call(
        by_expert_kernel if to_experts else by_group_kernel,
        out_shape=jax.ShapeDtypeStruct(deep if to_experts else flat, BF),
        in_specs=[vmem],
        out_specs=vmem,
        compiler_params=pltpu.CompilerParams(vmem_limit_bytes=VMEM_LIMIT),
        cost_estimate=pl.CostEstimate(flops=1 << 29, bytes_accessed=3 << 20, transcendentals=0),
    )(rows.reshape(flat if to_experts else deep))


def collect_far(parts, got):
    own, up, down = parts
    got_lo, got_hi = got
    half = got_lo.shape[0]
    up = jnp.concatenate([add(up[:half], got_lo), up[half:]])
    down = jnp.concatenate([down[:half], add(down[half:], got_hi)])
    return own, up, down


def collect_near(parts, axis):
    own, up, down = parts
    return add(own, fetch(up, axis, -1), fetch(down, axis, 1))


def collect_small(parts, axis):
    return add(parts[0], *[fetch(parts[r], axis, -r) for r in (1, 2, 3)])


def ranks(named):
    tok = named.shape[-1]
    earlier = jnp.arange(tok)[:, None] < jnp.arange(tok)[None, :]
    count = jnp.dot(named.astype(BF), earlier.astype(BF), preferred_element_type=F32)
    return jnp.where(named > 0, count, -1.0)


def body(tokens, routes, gates, cotangent, w_gate, w_up, w_down):
    y, c, z, x = (lax.axis_index(a) for a in ("y", "c", "z", "x"))
    ids = jnp.stack([y, z, c, x]).astype(jnp.int32)
    n_exp = w_gate.shape[0]
    total_exp = n_exp * 32
    tok, width = tokens.shape
    weights = (w_gate, w_up, w_down)

    cot = [cotangent] + [fetch(cotangent, "x", r) for r in (1, 2, 3)]
    routes_t = routes.T
    experts_all = jnp.arange(total_exp, dtype=jnp.int32)
    named = jnp.sum((routes_t[:, None, :] == experts_all[None, :, None]).astype(F32), axis=0)
    place = ranks(named).astype(BF)
    slots = total_exp * CAP
    slot = jnp.arange(slots, dtype=jnp.int32)
    repeat = (slot[:, None] // CAP == experts_all[None, :]).astype(BF)
    place_rep = jnp.dot(repeat, place, preferred_element_type=F32)
    own_map = (place_rep == (slot % CAP).astype(F32)[:, None]).astype(BF)

    def exchange(a):
        return lax.all_to_all(a, GROUP, split_axis=0, concat_axis=0, tiled=True)

    came = exchange(jnp.dot(own_map, tokens, preferred_element_type=F32).astype(BF))

    meta = jnp.concatenate([routes_t.astype(BF), gates.T], axis=0)
    meta = jnp.pad(meta, ((0, 0), (0, width - tok)))
    whole = jnp.concatenate(cot + [meta])
    came, whole = lax.optimization_barrier((came, whole))
    whole = lax.all_gather(whole, ("y", "z"))

    came = regroup(came, n_exp, True)
    up, down = fetch(came, "x", 1), fetch(came, "x", -1)
    pair = n_exp // 2
    near = near_products(ids, (came, up, down), weights[:2])
    far = (fetch(down[:pair], "x", -1), fetch(up[pair:], "x", 1))
    x_blocks = (came, up) + far + (down,)
    out_own, out_sib, hidden, slope, act = forward(ids, far, near, weights)

    whole, out_sib = lax.optimization_barrier((whole, out_sib))
    own, sib, maps = pick(ids, whole, n_exp)
    sib, out_sib = lax.optimization_barrier((sib, fetch(out_sib, "c", 1)))

    far = sum_tokens(ids, maps, out_own, out_sib, True)
    sib, far = lax.optimization_barrier((fetch(sib, "c", 1), far))
    got_y = (fetch(far[0], "y", -1), fetch(far[1], "y", 1))
    got_z = (fetch(far[2], "z", -1), fetch(far[3], "z", 1))
    g_blocks = (own, sib)
    mid = jax.ShapeDtypeStruct(hidden.shape, BF)
    grad_a, grad_b, back = backward(ids, g_blocks, slope, act, weights, mid, came.shape)
    back = lax.psum_scatter(back.reshape(-1, width), "x", scatter_dimension=0, tiled=True)

    out_sib, grad_a = lax.optimization_barrier((out_sib, grad_a))
    near = sum_tokens(ids, maps, out_own, out_sib, False)
    near, got_y, got_z = lax.optimization_barrier((near, got_y, got_z))
    ends_y, ends_z = collect_far(near[:3], got_y), collect_far(near[3:], got_z)
    hidden, ends_y, ends_z = lax.optimization_barrier((hidden, ends_y, ends_z))
    grads = weight_grads(ids, x_blocks, g_blocks, (hidden, grad_a, grad_b), w_gate)
    part1, part2 = collect_near(ends_y, "y"), collect_near(ends_z, "z")
    grads, part1, part2 = lax.optimization_barrier((grads, part1, part2))
    part1, part2 = collect_small(part1, "z"), collect_small(part2, "y")

    back, part1, part2 = lax.optimization_barrier((back, part1, part2))
    back = exchange(regroup(back, n_exp, False).reshape(slots, width))
    mixed = collect_small((part1[0], part1[1], part2[0], part2[1]), "x")
    grad_tokens = tn(own_map, back).astype(BF)
    return (mixed, grad_tokens) + tuple(grads)


def solution(mesh):
    split = Mesh(mesh.devices.reshape(4, 2, 4, 4), ("y", "c", "z", "x"))
    acts = P(GROUP, "x")
    rows = P(GROUP, None)
    wts = P(GROUP, "x", None)
    return jax.shard_map(
        body,
        mesh=split,
        in_specs=(acts, rows, rows, acts, wts, wts, wts),
        out_specs=(acts, acts, wts, wts, wts),
        check_vma=False,
    )
```
